32 devices in a mesh: cfg: 2 (over core), seq: 4 (over z), blk: 4 (over y, x).
Axes of the slice: x: 2, y: 2, z: 4, core: 2. Of those that a mesh axis runs over, the one named last changes fastest.
Arguments:
- queries: bfloat16 [2, 1536, 1536], P('cfg', 'seq', 'blk'), may hold values from -20 to 20
- keys: bfloat16 [2, 1536, 1536], P('cfg', 'seq', 'blk'), may hold values from -20 to 20
- values: bfloat16 [2, 1536, 1536], P('cfg', 'seq', 'blk'), may hold values from -6 to 6
- residual: bfloat16 [2, 1536, 1536], P('cfg', 'seq'), may hold values from -6 to 6
- w_out: bfloat16 [1536, 1536], P('blk'), may hold values from -0.15625 to 0.15625
- w_up: bfloat16 [1536, 6144], P(None, 'blk'), may hold values from -0.15625 to 0.15625
- w_down: bfloat16 [6144, 1536], P('blk'), may hold values from -0.078125 to 0.078125
- modulation: float32 [3, 4, 1536], replicated, may hold values from -3 to 3
- guide_scale: float32 [3], replicated, may hold values from 1.5 to 4
- slot_clip: int32 [1536], P('seq'), may hold values from 0 to 3, as said below
- owner: int32 [1536, 1], P('seq'), may hold values from 0 to 3; in each aligned block of 192 rows (0 to 191, 192 to 383, ...) at most 96 rows name the same one
Outputs:
- returned: bfloat16 [2, 1536, 1536], P('cfg', 'seq', 'blk')
The draws below stay inside these ranges and needn't reach their ends.
Inputs may be any that keep to these rules, and one draw needn't show every extreme that they name: `slot_clip`: each device's block of 384 slots holds its live slots first and its padding slots, marked 3, last; live slots, counted block after block, are dealt to the clips in turn (the t-th live slot belongs to clip t mod 3), so each clip has 448 live slots. In each aligned half-block of 192 slots no owner is named more than 96 times.
All inputs are finite; a program needn't handle non-finite values.
Results may differ from the reference program's by a relative error of at most 0.017.
Values may be sent and summed in bfloat16 or wider, within the bound.
No kernel may reach another device: no remote copies, remote signals or barrier semaphores. Data moves between devices by JAX's collectives and lax.ppermute only.
A program may use at most 128 MiB of HBM per device.

```python
import math
import jax
import jax.numpy as jnp
import numpy as np
from jax import lax

D = 1536
HEADS = 12
HEAD_DIM = 128
FFW = 6144
CLIPS = 3
SLOTS = 384
PAD_DEV = 48
HALF = 192
ROWS = 1536
CAP = 96
OUT_ROWS = 1536
N_SEQ = 4


def draw_queries(key, part):
    result = jnp.clip(1.6 * jax.random.normal(jax.random.fold_in(key, 21), (2, ROWS, D), jnp.float32), -9.6, 9.6)
    return result.astype(jnp.bfloat16)


def draw_keys(key, part):
    result = jnp.clip(1.6 * jax.random.normal(jax.random.fold_in(key, 22), (2, ROWS, D), jnp.float32), -9.6, 9.6)
    return result.astype(jnp.bfloat16)


def draw_slot_clip(key, part):
    blocks = ROWS // SLOTS
    swing = jax.random.randint(jax.random.fold_in(key, 1), (blocks // 2,), -PAD_DEV, PAD_DEV + 1)
    order = jax.random.permutation(jax.random.fold_in(key, 2), blocks)
    padding = PAD_DEV + jnp.concatenate([swing, -swing])[order]
    filled = SLOTS - padding
    starts = jnp.cumsum(filled) - filled
    position = jnp.arange(SLOTS)
    token = starts[:, None] + position[None, :]
    clip_id = jnp.where(position[None, :] < filled[:, None], token % CLIPS, CLIPS)
    return clip_id.reshape(ROWS).astype(jnp.int32)


def level_of(key, extent, cuts, least, top_value):
    factor_of = 1.0
    for dim, blocks in cuts:
        draws = jax.random.uniform(jax.random.fold_in(jax.random.fold_in(key, 6), dim), (blocks,), jnp.float32, least / len(cuts), top_value / len(cuts))
        factor_of = factor_of * jnp.repeat(jnp.exp(draws), extent[dim] // blocks).reshape((-1,) + (1,) * (len(extent) - 1 - dim))
    return factor_of


def deal_out(stream_key, own, number, rows, amount, top, bound, slope):
    order = jax.random.permutation(stream_key, amount)
    packed, usual = portions_of(amount, rows * top, bound, slope, True), portions_of(amount, rows * top, bound, slope, False)
    places = jnp.arange(amount)

    def named(lengths, offset_by):
        used = int((lengths > 0).sum())
        fixed = max(1, used // 4)
        shifted = fixed + (places - fixed + offset_by * (used - fixed)) % max(1, amount - fixed)
        return jnp.zeros((amount,), jnp.int32).at[order[jnp.where(places < fixed, places, shifted)]].set(jnp.asarray(lengths, jnp.int32))

    lengths = jnp.where(number % 4 == 0, named(packed, number // 4), named(usual, number - number // 4 - 1))
    mixed = jax.random.permutation(jax.random.fold_in(own, 3), amount)
    donor, receiver = mixed[0:amount // 2 * 2:2], mixed[1:amount // 2 * 2:2]
    margin = jnp.minimum(lengths[donor] - 1, bound - lengths[receiver]) // 2
    margin = jnp.where((donor == order[0]) | (receiver == order[0]) | (lengths[receiver] == 0), 0, jnp.maximum(margin, 0))
    shifted = jax.random.randint(jax.random.fold_in(own, 4), (amount // 2,), 0, 1 << 20) % (margin + 1)
    lengths = lengths.at[donor].add(-shifted).at[receiver].add(shifted)
    labels = jnp.searchsorted(jnp.cumsum(lengths), jnp.arange(rows * top), side="right").astype(jnp.int32)
    table = labels.reshape(top, rows).T
    table = table[jax.random.permutation(jax.random.fold_in(own, 1), rows)]
    offset_by = jax.random.randint(jax.random.fold_in(own, 2), (rows, 1), 0, top)
    return jnp.take_along_axis(table, (jnp.arange(top)[None, :] + offset_by) % top, axis=1)


def portions_of(count, total, reach, lean, full):
    portions = [(1 << 20) // math.isqrt(grade ** lean) + 1 for grade in range(1, count + 1)]
    largest = reach if full else min(reach, max(-(-total // count), total * portions[0] // sum(portions)))
    least = 1 if total - largest >= count - 1 else 0
    counts, surplus = [largest] + [least] * (count - 1), total - largest - least * (count - 1)
    while surplus > 0:
        candidates = [i for i in range(1, count) if counts[i] < largest] or [i for i in range(1, count) if counts[i] < reach]
        pool, left = sum([portions[i] for i in candidates]), surplus
        for i in candidates:
            extra = min(reach - counts[i], max(1, left * portions[i] // pool), surplus)
            counts[i] = counts[i] + extra
            surplus = surplus - extra
    return np.array(counts)


def noise(stream_key, extent, scale, reach, shards=(), held_as=jnp.bfloat16):
    values = scale * jax.random.normal(stream_key, extent, jnp.float32)
    if shards:
        values = values * level_of(stream_key, extent, shards, -0.22, 0.18)
    return jnp.clip(values, -reach, reach).astype(held_as)


def setup_inputs(seed: int = 0) -> dict:
    key_list = jax.random.split(jax.random.key(seed), 12)
    queries = draw_queries(jax.random.fold_in(key_list[11], 71), 0)
    keys = draw_keys(jax.random.fold_in(key_list[11], 71), 0)
    values = noise(key_list[2], (2, ROWS, D), 1.0, 6.0, ((0, 2), (1, 4), (2, 4)))
    residual = noise(key_list[3], (2, ROWS, D), 1.0, 6.0, ((0, 2), (1, 4)))
    w_out = noise(key_list[4], (D, D), D ** -0.5, 0.15625, ((0, 4),))
    w_up = noise(key_list[5], (D, FFW), D ** -0.5, 0.15625, ((1, 4),))
    w_down = noise(key_list[6], (FFW, D), FFW ** -0.5, 0.078125, ((0, 4),))
    modulation = noise(key_list[7], (CLIPS, 4, D), 0.5, 3.0, (), jnp.float32)
    guide_scale = jnp.clip(jax.random.uniform(key_list[8], (CLIPS,), jnp.float32, 1.5, 4.0), 1.5, 4.0)
    slot_clip = draw_slot_clip(jax.random.fold_in(key_list[11], 71), 0)
    owner_keys = jax.random.split(jax.random.fold_in(key_list[10], 1), ROWS // HALF)
    owner_turns = jax.random.permutation(jax.random.fold_in(key_list[10], 3), ROWS // HALF)
    owner = jax.vmap(lambda own, number: deal_out(jax.random.fold_in(key_list[10], 2), own, number, HALF, N_SEQ, 1, CAP, 1))(owner_keys, owner_turns).reshape((ROWS, 1))
    return {"queries": queries, "keys": keys, "values": values, "residual": residual, "w_out": w_out, "w_up": w_up, "w_down": w_down, "modulation": modulation, "guide_scale": guide_scale, "slot_clip": slot_clip, "owner": owner}


NEG_FILL = -1e+30

def reference(queries, keys, values, residual, w_out, w_up, w_down, modulation, guide_scale, slot_clip, owner):
    live = slot_clip < CLIPS
    factor = 1.0 / math.sqrt(HEAD_DIM)

    def split_heads(tensor):
        return tensor.reshape(2, ROWS, HEADS, HEAD_DIM).transpose(0, 2, 1, 3).reshape(2 * HEADS, ROWS, HEAD_DIM)

    def attend_group(group):
        query_rows, key_rows, value_rows = group

        def one_block(block):
            start = (block * SLOTS).astype(jnp.int32)
            query_block = lax.dynamic_slice_in_dim(query_rows, start, SLOTS, 0)
            clip_block = lax.dynamic_slice_in_dim(slot_clip, start, SLOTS, 0)
            scores = jnp.dot(query_block, key_rows.T, preferred_element_type=jnp.float32) * factor
            kept = (slot_clip[None, :] == clip_block[:, None]) & (clip_block[:, None] < CLIPS)
            scores = jnp.where(kept, scores, NEG_FILL)
            peak = lax.optimization_barrier(jnp.max(scores, axis=1, keepdims=True))
            weights = jnp.exp(scores - peak)
            totals = lax.optimization_barrier(jnp.sum(weights, axis=1, keepdims=True))
            summed = jnp.dot(weights.astype(jnp.bfloat16), value_rows, preferred_element_type=jnp.float32)
            return summed / totals
        blocks = lax.map(one_block, jnp.arange(ROWS // SLOTS, dtype=jnp.int32))
        return blocks.reshape(ROWS, HEAD_DIM)
    attended = lax.map(attend_group, (split_heads(queries), split_heads(keys), split_heads(values)))
    attended = attended.reshape(2, HEADS, ROWS, HEAD_DIM).transpose(0, 2, 1, 3).reshape(2, ROWS, D)
    attended = jnp.where(live[None, :, None], attended, 0.0).astype(jnp.bfloat16)
    projected = jnp.dot(attended.reshape(2 * ROWS, D), w_out, preferred_element_type=jnp.float32).reshape(2, ROWS, D)
    table = jnp.concatenate([modulation, jnp.zeros((1, 4, D), jnp.float32)], axis=0)
    row_mod = table[slot_clip]
    gate_attn = row_mod[None, :, 0]
    shift = row_mod[None, :, 1]
    stretch = row_mod[None, :, 2]
    gate_mlp = row_mod[None, :, 3]
    mixed = residual.astype(jnp.float32) + gate_attn * projected
    centre = mixed - lax.optimization_barrier(jnp.mean(mixed, axis=-1, keepdims=True))
    spread = lax.optimization_barrier(jnp.mean(centre * centre, axis=-1, keepdims=True))
    normed = (centre * lax.rsqrt(spread + 1e-06) * (1.0 + stretch) + shift).astype(jnp.bfloat16)
    hidden = jax.nn.gelu(jnp.dot(normed.reshape(2 * ROWS, D), w_up, preferred_element_type=jnp.float32), approximate=True).astype(jnp.bfloat16)
    feed = jnp.dot(hidden, w_down, preferred_element_type=jnp.float32).reshape(2, ROWS, D)
    block_out = (mixed + gate_mlp * feed).astype(jnp.bfloat16)
    cond = block_out[0].astype(jnp.float32)
    uncond = block_out[1].astype(jnp.float32)
    strength = jnp.concatenate([guide_scale, jnp.zeros((1,), jnp.float32)])[slot_clip]
    guided = jnp.where(live[:, None], uncond + strength[:, None] * (cond - uncond), 0.0).astype(jnp.bfloat16)
    owned = owner[:, 0].reshape(N_SEQ, 2, HALF)
    onehot = (owned[..., None] == jnp.arange(N_SEQ, dtype=jnp.int32)).astype(jnp.int32)
    rank = lax.optimization_barrier(jnp.sum((jnp.cumsum(onehot, axis=2) - onehot) * onehot, axis=-1))
    source = jnp.arange(N_SEQ, dtype=jnp.int32)[:, None, None]
    halfid = jnp.arange(2, dtype=jnp.int32)[None, :, None]
    target = (((halfid * N_SEQ + owned) * N_SEQ + source) * CAP + rank).astype(jnp.int32)
    returned = jnp.zeros((2 * OUT_ROWS, D), jnp.bfloat16).at[target.reshape(-1)].set(guided.reshape(ROWS, D))
    return returned.reshape(2, OUT_ROWS, D)
```

```python
import functools
import math

import jax
import jax.numpy as jnp
from jax import lax
from jax.experimental import pallas as pl
from jax.experimental.pallas import tpu as pltpu
from jax.sharding import PartitionSpec as P

D = 1536
HEAD_DIM = 128
CLIPS = 3
NEG_FILL = -1e30
FAR = 2.0**100
VMEM = pl.BlockSpec(memory_space=pltpu.VMEM)
ANY = pl.BlockSpec(memory_space=pl.ANY)
F32 = jnp.float32
BF16 = jnp.bfloat16


def shape_of(extent, dtype=BF16):
    return jax.ShapeDtypeStruct(extent, dtype)


def params(mib):
    return pltpu.CompilerParams(vmem_limit_bytes=mib * 2**20)


def head_at(side, place):
    return jnp.where(side == 0, place, 3 - place)


def works(side, place):
    return place < 3 if side == 0 else place >= 1


def hop(value, step, back=False):
    pairs = []
    for side in range(2):
        for place in range(4):
            target = (place + step) % 4
            if works(side, target):
                pair = (side * 4 + place, side * 4 + target)
                pairs.append(pair[::-1] if back else pair)
    return lax.ppermute(value, ("cfg", "seq"), pairs)


def pack_kernel(q_ref, k_ref, v_ref, clip_ref, *outs):
    side, place = lax.axis_index("cfg"), lax.axis_index("seq")
    slots = q_ref.shape[0]
    for step, out in enumerate(outs):
        head = jnp.clip(head_at(side, lax.rem(place + step, 4)), 0, 2)
        columns = pl.ds(pl.multiple_of(head * HEAD_DIM, HEAD_DIM), HEAD_DIM)
        for part, source in enumerate((q_ref, k_ref, v_ref)):
            out[part * slots : (part + 1) * slots, :] = source[:, columns]
        out[3 * slots :, :] = clip_ref[...]


def attend_kernel(*refs):
    blocks, outs, (q_aug, k_aug, v_aug, clips) = refs[:4], refs[4:8], refs[8:]
    slots = outs[0].shape[0]
    lane = lax.broadcasted_iota(jnp.int32, (128, 128), 1)
    row = lax.broadcasted_iota(jnp.int32, (128, 128), 0)
    eye = (lane == row).astype(BF16)
    for index, block in enumerate(blocks):
        base = index * slots
        here = slice(base, base + slots)
        q_aug[here, :128] = block[:slots, :]
        k_aug[here, :128] = block[slots : 2 * slots, :]
        v_aug[here, :128] = block[2 * slots : 3 * slots, :]
        turned = lax.dot_general(
            eye, block[3 * slots :, :], (((1,), (1,)), ((), ())), preferred_element_type=F32
        )
        for group in range(slots // 128):
            part = slice(base + group * 128, base + (group + 1) * 128)
            clip = jnp.broadcast_to(turned[:, group : group + 1], (128, 128)).astype(jnp.int32)
            clips[part, :] = clip
            same = lane == clip
            kept = same & (clip < CLIPS)
            k_aug[part, 128:] = same.astype(BF16)
            q_aug[part, 128:] = jnp.where(kept | (lane > CLIPS), 0.0, -FAR).astype(BF16)
            v_aug[part, 128:] = (lane == 0).astype(BF16)
    scale = math.log2(math.e) / math.sqrt(HEAD_DIM)
    for index, out in enumerate(outs):
        here = slice(index * slots, (index + 1) * slots)
        scores = lax.dot_general(
            q_aug[here, :], k_aug[...], (((1,), (1,)), ((), ())), preferred_element_type=F32
        )
        peak = jnp.max(scores, axis=1, keepdims=True)
        probs = jnp.exp2((scores - peak) * scale).astype(BF16)
        summed = jnp.dot(probs, v_aug[...], preferred_element_type=F32)
        result = summed[:, :128] / summed[:, 128:129]
        out[...] = jnp.where(clips[here, :] < CLIPS, result, 0.0).astype(BF16)


def regroup_kernel(own, back1, back2, back3, first, second):
    side, place = lax.axis_index("cfg"), lax.axis_index("seq")
    half = first.shape[0]
    for head in range(3):
        home = jnp.where(side == 0, head, 3 - head)
        step = lax.rem(home - place + 4, 4)
        columns = slice(head * HEAD_DIM, (head + 1) * HEAD_DIM)
        for index, source in enumerate((own, back1, back2, back3)):

            @pl.when(step == index)
            def _():
                for out, which in ((first, 1 - side), (second, side)):
                    rows = pl.ds(pl.multiple_of(which * half, half), half)
                    out[:, columns] = source[rows, :]


def attention_by_head(query, key, value, slot_clip):
    slots = query.shape[0]
    clip_rows = jnp.pad(slot_clip.reshape(slots // 128, 128), ((0, 16 - slots // 128), (0, 0)))
    packed = pl.pallas_call(
        pack_kernel,
        out_shape=[shape_of((3 * slots + 16, 128))] * 4,
        in_specs=[VMEM] * 4,
        out_specs=[VMEM] * 4,
        compiler_params=params(16),
        name="pack",
    )(query, key, value, clip_rows.astype(BF16))
    blocks = [packed[0]] + [hop(packed[step], step) for step in (1, 2, 3)]
    results = pl.pallas_call(
        attend_kernel,
        out_shape=[shape_of((slots, 128))] * 4,
        in_specs=[VMEM] * 4,
        out_specs=[VMEM] * 4,
        scratch_shapes=[pltpu.VMEM((4 * slots, 256), BF16)] * 3
        + [pltpu.VMEM((4 * slots, 128), jnp.int32)],
        compiler_params=params(32),
        name="attend",
    )(*blocks)
    backs = [hop(results[step], step, back=True) for step in (1, 2, 3)]
    half = slots // 2
    return pl.pallas_call(
        regroup_kernel,
        out_shape=[shape_of((half, 3 * HEAD_DIM))] * 2,
        in_specs=[VMEM] * 4,
        out_specs=[VMEM] * 2,
        compiler_params=params(16),
        name="regroup",
    )(results[0], *backs)


def attention_by_rows(query, key, value, slot_clip):
    slots, width = query.shape
    heads = width // HEAD_DIM
    live = slot_clip < CLIPS
    factor = 1.0 / math.sqrt(HEAD_DIM)
    query_heads = query.reshape(slots, heads, HEAD_DIM)

    def absorb(carry, piece):
        key_piece, value_piece, clip_piece = piece
        best, total, accum = carry
        kept = (clip_piece[None, :] == slot_clip[:, None]) & live[:, None]
        scores = jnp.einsum("qhd,khd->hqk", query_heads, key_piece, preferred_element_type=F32)
        scores = jnp.where(kept[None], scores * factor, NEG_FILL)
        new_best = jnp.maximum(best, jnp.max(scores, axis=-1))
        fade = jnp.exp(best - new_best)
        probs = jnp.exp(scores - new_best[..., None])
        total = total * fade + jnp.sum(probs, axis=-1)
        added = jnp.einsum(
            "hqk,khd->qhd", probs.astype(BF16), value_piece, preferred_element_type=F32
        )
        accum = accum * jnp.transpose(fade)[:, :, None] + added
        return (new_best, total, accum), None

    start = (
        jnp.full((heads, slots), NEG_FILL, F32),
        jnp.zeros((heads, slots), F32),
        jnp.zeros((slots, heads, HEAD_DIM), F32),
    )
    pieces = (
        lax.all_gather(key, "seq").reshape(-1, slots, heads, HEAD_DIM),
        lax.all_gather(value, "seq").reshape(-1, slots, heads, HEAD_DIM),
        lax.all_gather(slot_clip, "seq"),
    )
    (best, total, accum), _ = lax.scan(absorb, start, pieces)
    attended = (accum / jnp.transpose(total)[:, :, None]).reshape(slots, width)
    attended = jnp.where(live[:, None], attended, 0.0).astype(BF16)
    half = slots // 2
    side = lax.axis_index("cfg")
    return [
        lax.dynamic_slice_in_dim(attended, which * half, half, 0) for which in (1 - side, side)
    ]


def feed_kernel(turn, *refs):
    (att, (w_own, *w_got), (up_hbm, down_hbm, res_hbm, mod, clip_ref)) = (
        refs[:4],
        refs[4:11],
        refs[11:16],
    )
    out = refs[16]
    rows_in, w_out, up, down, res, mixed, total, normed, hidden, sems = refs[17:]
    side, blk = lax.axis_index("cfg"), lax.axis_index("blk")
    half = out.shape[0]
    which = 1 - side if turn == 0 else side
    rows = pl.ds(pl.multiple_of(which * half, half), half)
    width = att[0].shape[1]
    part = width // 2
    first = []
    for step in range(4):
        first.append((att[step], rows_in.at[:, step * width : (step + 1) * width]))
    first.append((w_own, w_out.at[0:width, :]))
    for step in range(1, 4):
        for piece, where in ((w_got[step - 1], side), (w_got[step + 2], 1 - side)):
            offset = pl.multiple_of(step * width + where * part, part)
            first.append((piece, w_out.at[pl.ds(offset, part), :]))
    first.append((res_hbm.at[rows, :], res))
    plan = first + [(up_hbm, up), (down_hbm, down)]
    copies = [
        pltpu.make_async_copy(source, target, sems.at[index])
        for index, (source, target) in enumerate(plan)
    ]
    for copy in copies:
        copy.start()
    clip = clip_ref[rows, :][:, :1]
    tile = 512

    def chosen(kind, columns):
        picked = jnp.zeros((half, tile), F32)
        for index in range(CLIPS):
            line = mod[index * 4 + kind : index * 4 + kind + 1, columns]
            picked = jnp.where(clip == index, line, picked)
        return picked

    for copy in copies[:-2]:
        copy.wait()
    for start in range(0, D, tile):
        columns = slice(start, start + tile)
        projected = jnp.dot(rows_in[...], w_out[:, columns], preferred_element_type=F32)
        mixed[:, columns] = res[:, columns].astype(F32) + chosen(0, columns) * projected
    held = mixed[...]
    centre = held - jnp.mean(held, axis=1, keepdims=True)
    spread = lax.rsqrt(jnp.mean(centre * centre, axis=1, keepdims=True) + 1e-06)
    for start in range(0, D, tile):
        columns = slice(start, start + tile)
        value = centre[:, columns] * spread * (1.0 + chosen(2, columns)) + chosen(1, columns)
        normed[:, columns] = value.astype(BF16)
    copies[-2].wait()
    for start in range(0, D, tile):
        columns = slice(start, start + tile)
        raised = jnp.dot(normed[...], up[:, columns], preferred_element_type=F32)
        hidden[:, columns] = jax.nn.gelu(raised, approximate=True).astype(BF16)
    copies[-1].wait()
    for start in range(0, D, tile):
        columns = slice(start, start + tile)
        lowered = jnp.dot(hidden[...], down[:, columns], preferred_element_type=F32)
        total[:, columns] = chosen(3, columns) * lowered
    own = pl.ds(pl.multiple_of(blk * width, width), width)
    total[:, own] = total[:, own] + mixed[:, own]
    out[...] = total[...].astype(out.dtype)


def feed(turn, att, w_parts, w_up, w_down, residual, mod, clip_wide):
    half, width = att[0].shape
    return pl.pallas_call(
        functools.partial(feed_kernel, turn),
        out_shape=shape_of((half, D), BF16 if turn == 0 else F32),
        in_specs=[ANY] * 14 + [VMEM] * 2,
        out_specs=VMEM,
        scratch_shapes=[
            pltpu.VMEM((half, D), BF16),
            pltpu.VMEM((D, D), BF16),
            pltpu.VMEM((D, D), BF16),
            pltpu.VMEM((D, D), BF16),
            pltpu.VMEM((half, D), BF16),
            pltpu.VMEM((half, D), F32),
            pltpu.VMEM((half, D), F32),
            pltpu.VMEM((half, D), BF16),
            pltpu.VMEM((half, D), BF16),
            pltpu.SemaphoreType.DMA((14,)),
        ],
        compiler_params=params(40),
        name="feed",
    )(*att, *w_parts, w_up, w_down, residual, mod, clip_wide)


def guide_kernel(mine_ref, other_ref, strength_ref, own, *sent):
    side, blk = lax.axis_index("cfg"), lax.axis_index("blk")
    width = own.shape[1]
    strength = strength_ref[:, :1]
    lean = jnp.where(side == 0, strength, 1.0 - strength)
    for step, out in enumerate((own, *sent)):
        target = jnp.bitwise_xor(blk, step)
        columns = pl.ds(pl.multiple_of(target * width, width), width)
        other = other_ref[:, columns].astype(F32)
        guided = other + lean * (mine_ref[:, columns] - other)
        out[...] = guided.astype(out.dtype)


def place_kernel(own, got1, got2, got3, placing, *outs):
    guided = own[...] + got1[...].astype(F32) + got2[...].astype(F32) + got3[...].astype(F32)
    placed = jnp.dot(placing[...], guided.astype(BF16), preferred_element_type=F32).astype(BF16)
    if len(outs) == 1:
        outs[0][...] = placed
    else:
        count = outs[0].shape[0]
        for index, out in enumerate(outs):
            out[...] = placed[index * count : (index + 1) * count, :]


def arrange_kernel(own, got1, got2, got3, out):
    place = lax.axis_index("seq")
    count = own.shape[0]
    for step, source in enumerate((own, got1, got2, got3)):
        origin = lax.rem(place + 4 - step, 4)
        out[pl.ds(pl.multiple_of(origin * count, count), count), :] = source[...]


def exchanged(value, axis, mask):
    pairs = [(index, index ^ mask) for index in range(lax.axis_size(axis))]
    return lax.ppermute(value, axis, pairs)


def shards(
    queries, keys, values, residual, w_out, w_up, w_down, modulation, guide_scale, slot_clip, owner
):
    slots, width = queries.shape[1:]
    half = slots // 2
    seq_count = lax.axis_size("seq")
    capacity = max(2, slots // seq_count)
    side, place = lax.axis_index("cfg"), lax.axis_index("seq")

    if seq_count == 4:
        attended = attention_by_head(queries[0], keys[0], values[0], slot_clip)
    else:
        attended = attention_by_rows(queries[0], keys[0], values[0], slot_clip)

    w_half = lax.dynamic_slice_in_dim(w_out, side * (width // 2), width // 2, 0)
    w_got = [exchanged(w_half, "blk", mask) for mask in (1, 2, 3)]
    w_parts = [w_out] + w_got + [exchanged(piece, "cfg", 1) for piece in w_got]

    clip_wide = jnp.broadcast_to(slot_clip[:, None], (slots, 128))
    mod = modulation.reshape(CLIPS * 4, D)
    clip_half = lax.dynamic_slice_in_dim(slot_clip, side * half, half, 0)
    strength = jnp.zeros((half,), F32)
    for index in range(CLIPS):
        strength = jnp.where(clip_half == index, guide_scale[index], strength)
    strength = jnp.broadcast_to(strength[:, None], (half, 128))
    owner_half = lax.dynamic_slice_in_dim(owner[:, 0], side * half, half, 0)
    order = jnp.arange(half, dtype=jnp.int32)
    before = (owner_half[None, :] == owner_half[:, None]) & (order[None, :] < order[:, None])
    rank = jnp.sum(before.astype(jnp.int32), axis=1)
    if seq_count == 4:
        lane = lax.rem(owner_half - place + seq_count, seq_count)
    else:
        lane = owner_half
    target = jnp.where(clip_half < CLIPS, lane * capacity + rank, -1)
    placing = (
        jnp.arange(seq_count * capacity, dtype=jnp.int32)[:, None] == target[None, :]
    ).astype(BF16)

    parts = []
    for turn in range(2):
        piece = attended[turn]
        gathered = [piece] + [exchanged(piece, "blk", mask) for mask in (1, 2, 3)]
        parts.append(feed(turn, gathered, w_parts, w_up, w_down, residual[0], mod, clip_wide))
    other = exchanged(parts[0], "cfg", 1)
    own, *sent = pl.pallas_call(
        guide_kernel,
        out_shape=[shape_of((half, width), F32)] + [shape_of((half, width))] * 3,
        in_specs=[VMEM] * 3,
        out_specs=[VMEM] * 4,
        compiler_params=params(16),
        name="guide",
    )(parts[1], other, strength)
    got = [exchanged(piece, "blk", mask) for mask, piece in zip((1, 2, 3), sent)]
    by_step = seq_count == 4
    placed = pl.pallas_call(
        place_kernel,
        out_shape=[shape_of((capacity, width))] * 4
        if by_step
        else [shape_of((seq_count * capacity, width))],
        in_specs=[VMEM] * 5,
        out_specs=[VMEM] * (4 if by_step else 1),
        compiler_params=params(16),
        name="place",
    )(own, *got, placing)
    if not by_step:
        arrived = lax.all_to_all(
            placed[0].reshape(seq_count, capacity, width), "seq", split_axis=0, concat_axis=0,
            tiled=True,
        )
        return arrived.reshape(1, seq_count * capacity, width)
    home = [
        lax.ppermute(placed[step], "seq", [(i, (i + step) % 4) for i in range(4)])
        for step in (1, 2, 3)
    ]
    arranged = pl.pallas_call(
        arrange_kernel,
        out_shape=shape_of((4 * capacity, width)),
        in_specs=[VMEM] * 4,
        out_specs=VMEM,
        compiler_params=params(16),
        name="arrange",
    )(placed[0], *home)
    return arranged[None]


def solution(mesh):
    placed = (
        P("cfg", "seq", "blk"),
        P("cfg", "seq", "blk"),
        P("cfg", "seq", "blk"),
        P("cfg", "seq", None),
        P("blk", None),
        P(None, "blk"),
        P("blk", None),
        P(),
        P(),
        P("seq"),
        P("seq", None),
    )
    return jax.shard_map(
        shards, mesh=mesh, in_specs=placed, out_specs=P("cfg", "seq", "blk"), check_vma=False
    )
```

```python
import functools
import math

import jax
import jax.numpy as jnp
from jax import lax
from jax.experimental import pallas as pl
from jax.experimental.pallas import tpu as pltpu
from jax.sharding import PartitionSpec as P

D = 1536
HEAD_DIM = 128
CLIPS = 3
NEG_FILL = -1e30
FAR = 2.0**100
VMEM = pl.BlockSpec(memory_space=pltpu.VMEM)
ANY = pl.BlockSpec(memory_space=pl.ANY)
F32 = jnp.float32
BF16 = jnp.bfloat16


def shape_of(extent, dtype=BF16):
    return jax.ShapeDtypeStruct(extent, dtype)


def params(mib):
    return pltpu.CompilerParams(vmem_limit_bytes=mib * 2**20)


def cost(flops, moved):
    return pl.CostEstimate(flops=flops, bytes_accessed=moved, transcendentals=0)


def head_at(side, place):
    return jnp.where(side == 0, place, 3 - place)


def works(side, place):
    return place < 3 if side == 0 else place >= 1


def hop(value, step, back=False):
    pairs = []
    for side in range(2):
        for place in range(4):
            target = (place + step) % 4
            if works(side, target):
                pair = (side * 4 + place, side * 4 + target)
                pairs.append(pair[::-1] if back else pair)
    return lax.ppermute(value, ("cfg", "seq"), pairs)


def pack_kernel(q_ref, k_ref, v_ref, clip_ref, *refs):
    outs, sems = refs[:4], refs[4]
    side, place = lax.axis_index("cfg"), lax.axis_index("seq")
    slots = q_ref.shape[0]
    copies = []
    for step, out in enumerate(outs):
        head = jnp.clip(head_at(side, lax.rem(place + step, 4)), 0, 2)
        columns = pl.ds(pl.multiple_of(head * HEAD_DIM, HEAD_DIM), HEAD_DIM)
        for part, source in enumerate((q_ref, k_ref, v_ref)):
            target = out.at[part * slots : (part + 1) * slots, :]
            copy = pltpu.make_async_copy(source.at[:, columns], target, sems.at[len(copies)])
            copy.start()
            copies.append(copy)
    rows = clip_ref[...].astype(F32).astype(BF16)
    for out in outs:
        out[3 * slots :, :] = jnp.zeros((16, 128), BF16)
        out[3 * slots : 3 * slots + rows.shape[0], :] = rows
    for copy in copies:
        copy.wait()


def attend_kernel(*refs):
    blocks, outs, (q_aug, k_aug, v_aug, clips) = refs[:4], refs[9:13], refs[13:]
    slots = outs[0].shape[0]
    lane = lax.broadcasted_iota(jnp.int32, (128, 128), 1)
    row = lax.broadcasted_iota(jnp.int32, (128, 128), 0)
    eye = (lane == row).astype(BF16)
    for index, block in enumerate(blocks):
        base = index * slots
        here = slice(base, base + slots)
        q_aug[here, :128] = block[:slots, :]
        k_aug[here, :128] = block[slots : 2 * slots, :]
        v_aug[here, :128] = block[2 * slots : 3 * slots, :]
        turned = lax.dot_general(
            eye, block[3 * slots :, :], (((1,), (1,)), ((), ())), preferred_element_type=F32
        )
        for group in range(slots // 128):
            part = slice(base + group * 128, base + (group + 1) * 128)
            clip = jnp.broadcast_to(turned[:, group : group + 1], (128, 128)).astype(jnp.int32)
            clips[part, :] = clip
            same = lane == clip
            kept = same & (clip < CLIPS)
            k_aug[part, 128:] = same.astype(BF16)
            q_aug[part, 128:] = jnp.where(kept | (lane > CLIPS), 0.0, -FAR).astype(BF16)
            v_aug[part, 128:] = (lane == 0).astype(BF16)
    scale = math.log2(math.e) / math.sqrt(HEAD_DIM)
    for index, out in enumerate(outs):
        here = slice(index * slots, (index + 1) * slots)
        scores = lax.dot_general(
            q_aug[here, :], k_aug[...], (((1,), (1,)), ((), ())), preferred_element_type=F32
        )
        peak = jnp.max(scores, axis=1, keepdims=True)
        probs = jnp.exp2((scores - peak) * scale).astype(BF16)
        summed = jnp.dot(probs, v_aug[...], preferred_element_type=F32)
        result = summed[:, :128] / summed[:, 128:129]
        out[...] = jnp.where(clips[here, :] < CLIPS, result, 0.0).astype(BF16)


def regroup_kernel(own, back1, back2, back3, after, first, second):
    side, place = lax.axis_index("cfg"), lax.axis_index("seq")
    half = first.shape[0]
    for head in range(3):
        home = jnp.where(side == 0, head, 3 - head)
        step = lax.rem(home - place + 4, 4)
        columns = slice(head * HEAD_DIM, (head + 1) * HEAD_DIM)
        for index, source in enumerate((own, back1, back2, back3)):

            @pl.when(step == index)
            def _():
                for out, which in ((first, 1 - side), (second, side)):
                    rows = pl.ds(pl.multiple_of(which * half, half), half)
                    out[:, columns] = source[rows, :]


def kept(value):
    return pltpu.with_memory_space_constraint(value, pltpu.VMEM)


def afar(value):
    return pltpu.with_memory_space_constraint(value, pltpu.HBM)


def load_kernel(up, down, after, up_out, down_out, sems):
    copies = [
        pltpu.make_async_copy(source, target, sems.at[index])
        for index, (source, target) in enumerate(((up, up_out), (down, down_out)))
    ]
    for copy in copies:
        copy.start()
    for copy in copies:
        copy.wait()


def load(up, down, after):
    return pl.pallas_call(
        load_kernel,
        out_shape=[pltpu.VMEM(up.shape, BF16), pltpu.VMEM(down.shape, BF16)],
        in_specs=[ANY] * 3,
        out_specs=[VMEM] * 2,
        scratch_shapes=[pltpu.SemaphoreType.DMA((2,))],
        compiler_params=params(16),
        name="load",
    )(afar(up), afar(down), after)


def across(value, masks):
    pairs = [
        (side * 4 + blk, side * 4 + (blk ^ masks[side])) for side in range(2) for blk in range(4)
    ]
    return lax.ppermute(value, ("cfg", "blk"), pairs)


def cut_kernel(got, out, sem):
    part = out.shape[0]
    offset = pl.multiple_of((1 - lax.axis_index("cfg")) * part, part)
    copy = pltpu.make_async_copy(got.at[pl.ds(offset, part), :], out, sem)
    copy.start()
    copy.wait()


def join_kernel(own, near, near_swap, far, far_swap, after, out, sems):
    side = lax.axis_index("cfg")
    width, part = own.shape[0], far.shape[0]
    plan = (
        (own, 0, width),
        (near, (1 + side) * width, width),
        (near_swap, (2 - side) * width, width),
        (far, 3 * width + (1 - side) * part, part),
        (far_swap, 3 * width + side * part, part),
    )
    copies = []
    for index, (source, offset, rows) in enumerate(plan):
        target = out.at[pl.ds(pl.multiple_of(offset, part), rows), :]
        copy = pltpu.make_async_copy(source, target, sems.at[index])
        copy.start()
        copies.append(copy)
    for copy in copies:
        copy.wait()


def gate_kernel(value, after, out):
    pass


def gate(value, after):
    return pl.pallas_call(
        gate_kernel,
        out_shape=shape_of(value.shape, value.dtype),
        in_specs=[ANY] * 2,
        out_specs=ANY,
        input_output_aliases={0: 0},
        compiler_params=params(1),
        name="gate",
    )(value, after)


def fetch_near(w_out):
    near = across(w_out, (1, 2))
    half = pl.pallas_call(
        cut_kernel,
        out_shape=shape_of((w_out.shape[0] // 2, D)),
        in_specs=[ANY],
        out_specs=ANY,
        scratch_shapes=[pltpu.SemaphoreType.DMA],
        compiler_params=params(16),
        name="cut",
    )(near)
    return near, half


def fetch_rest(w_out, near, half, after):
    far = across(half, (2, 1))
    far = gate(far, after)
    pieces = (afar(w_out), near, exchanged(near, "cfg", 1), far, exchanged(far, "cfg", 1))
    return pl.pallas_call(
        join_kernel,
        out_shape=pltpu.VMEM((D, D), BF16),
        in_specs=[ANY] * 6,
        out_specs=VMEM,
        scratch_shapes=[pltpu.SemaphoreType.DMA((5,))],
        compiler_params=params(16),
        name="join",
    )(*pieces, after)


def attention_by_head(query, key, value, slot_clip, early, weights, rest):
    slots = query.shape[0]
    packed = pl.pallas_call(
        pack_kernel,
        out_shape=[shape_of((3 * slots + 16, 128))] * 4,
        in_specs=[ANY] * 3 + [VMEM],
        out_specs=[VMEM] * 4,
        scratch_shapes=[pltpu.SemaphoreType.DMA((12,))],
        compiler_params=params(16),
        name="pack",
    )(afar(query), afar(key), afar(value), slot_clip.reshape(slots // 128, 128))
    blocks = [packed[0]] + [hop(packed[step], step) for step in (1, 2, 3)]
    early = (*early, *(kept(weight) for weight in load(*weights, packed[0])))
    results = pl.pallas_call(
        attend_kernel,
        out_shape=[shape_of((slots, 128))] * 4,
        in_specs=[VMEM] * 4 + [ANY] * (len(early) - 2) + [VMEM] * 2,
        out_specs=[VMEM] * 4,
        scratch_shapes=[pltpu.VMEM((4 * slots, 256), BF16)] * 3
        + [pltpu.VMEM((4 * slots, 128), jnp.int32)],
        compiler_params=params(28),
        cost_estimate=cost(2**32, 2**21),
        name="attend",
    )(*blocks, *early)
    backs = [hop(results[step], step, back=True) for step in (1, 2, 3)]
    half = slots // 2
    whole = rest(results[0])
    return whole, early[-2:], pl.pallas_call(
        regroup_kernel,
        out_shape=[shape_of((half, 3 * HEAD_DIM))] * 2,
        in_specs=[VMEM] * 4 + [ANY],
        out_specs=[VMEM] * 2,
        compiler_params=params(16),
        name="regroup",
    )(results[0], *backs, whole)


def attention_by_rows(query, key, value, slot_clip):
    slots, width = query.shape
    heads = width // HEAD_DIM
    live = slot_clip < CLIPS
    factor = 1.0 / math.sqrt(HEAD_DIM)
    query_heads = query.reshape(slots, heads, HEAD_DIM)

    def absorb(carry, piece):
        key_piece, value_piece, clip_piece = piece
        best, total, accum = carry
        kept = (clip_piece[None, :] == slot_clip[:, None]) & live[:, None]
        scores = jnp.einsum("qhd,khd->hqk", query_heads, key_piece, preferred_element_type=F32)
        scores = jnp.where(kept[None], scores * factor, NEG_FILL)
        new_best = jnp.maximum(best, jnp.max(scores, axis=-1))
        fade = jnp.exp(best - new_best)
        probs = jnp.exp(scores - new_best[..., None])
        total = total * fade + jnp.sum(probs, axis=-1)
        added = jnp.einsum(
            "hqk,khd->qhd", probs.astype(BF16), value_piece, preferred_element_type=F32
        )
        accum = accum * jnp.transpose(fade)[:, :, None] + added
        return (new_best, total, accum), None

    start = (
        jnp.full((heads, slots), NEG_FILL, F32),
        jnp.zeros((heads, slots), F32),
        jnp.zeros((slots, heads, HEAD_DIM), F32),
    )
    pieces = (
        lax.all_gather(key, "seq").reshape(-1, slots, heads, HEAD_DIM),
        lax.all_gather(value, "seq").reshape(-1, slots, heads, HEAD_DIM),
        lax.all_gather(slot_clip, "seq"),
    )
    (best, total, accum), _ = lax.scan(absorb, start, pieces)
    attended = (accum / jnp.transpose(total)[:, :, None]).reshape(slots, width)
    attended = jnp.where(live[:, None], attended, 0.0).astype(BF16)
    half = slots // 2
    side = lax.axis_index("cfg")
    return [
        lax.dynamic_slice_in_dim(attended, which * half, half, 0) for which in (1 - side, side)
    ]


def feed_kernel(turn, *refs):
    (att, (w_out, up, down, res_hbm, mod, clip_ref), out) = refs[:4], refs[4:10], refs[10]
    rows_in, res, mixed, total, normed, hidden, sems = refs[11:]
    side, blk = lax.axis_index("cfg"), lax.axis_index("blk")
    half = out.shape[0]
    which = 1 - side if turn == 0 else side
    rows = pl.ds(pl.multiple_of(which * half, half), half)
    width = att[0].shape[1]
    plan = [
        (att[step], rows_in.at[:, step * width : (step + 1) * width]) for step in range(4)
    ] + [(res_hbm.at[rows, :], res)]
    copies = [
        pltpu.make_async_copy(source, target, sems.at[index])
        for index, (source, target) in enumerate(plan)
    ]
    for copy in copies:
        copy.start()
    clip = clip_ref[rows, :][:, :1]
    tile = 512

    def chosen(kind, columns):
        picked = jnp.zeros((half, tile), F32)
        for index in range(CLIPS):
            line = mod[index, kind : kind + 1, columns]
            picked = jnp.where(clip == index, line, picked)
        return picked

    for copy in copies:
        copy.wait()
    for start in range(0, D, tile):
        columns = slice(start, start + tile)
        projected = jnp.dot(rows_in[...], w_out[:, columns], preferred_element_type=F32)
        mixed[:, columns] = res[:, columns].astype(F32) + chosen(0, columns) * projected
    held = mixed[...]
    centre = held - jnp.mean(held, axis=1, keepdims=True)
    spread = lax.rsqrt(jnp.mean(centre * centre, axis=1, keepdims=True) + 1e-06)
    for start in range(0, D, tile):
        columns = slice(start, start + tile)
        value = centre[:, columns] * spread * (1.0 + chosen(2, columns)) + chosen(1, columns)
        normed[:, columns] = value.astype(BF16)
    for start in range(0, D, tile):
        columns = slice(start, start + tile)
        raised = jnp.dot(normed[...], up[:, columns], preferred_element_type=F32)
        hidden[:, columns] = jax.nn.gelu(raised, approximate=True).astype(BF16)
    for start in range(0, D, tile):
        columns = slice(start, start + tile)
        lowered = jnp.dot(hidden[...], down[:, columns], preferred_element_type=F32)
        total[:, columns] = chosen(3, columns) * lowered
    own = pl.ds(pl.multiple_of(blk * width, width), width)
    total[:, own] = total[:, own] + mixed[:, own]
    out[...] = total[...].astype(out.dtype)


def feed(turn, att, w_out, w_up, w_down, residual, mod, clip_wide):
    half, width = att[0].shape
    return pl.pallas_call(
        functools.partial(feed_kernel, turn),
        out_shape=shape_of((half, D), BF16 if turn == 0 else F32),
        in_specs=[ANY] * 4 + [VMEM] * 3 + [ANY] + [VMEM] * 2,
        out_specs=VMEM,
        scratch_shapes=[
            pltpu.VMEM((half, D), BF16),
            pltpu.VMEM((half, D), BF16),
            pltpu.VMEM((half, D), F32),
            pltpu.VMEM((half, D), F32),
            pltpu.VMEM((half, D), BF16),
            pltpu.VMEM((half, D), BF16),
            pltpu.SemaphoreType.DMA((5,)),
        ],
        compiler_params=params(24),
        cost_estimate=cost(2**36, 2**24),
        name="feed",
    )(*att, kept(w_out), kept(w_up), kept(w_down), afar(residual), mod, clip_wide)


def guide_kernel(mine_ref, other_ref, clip_ref, scale_ref, own, *sent):
    side, blk = lax.axis_index("cfg"), lax.axis_index("blk")
    half, width = own.shape
    clip = clip_ref[pl.ds(pl.multiple_of(side * half, half), half), :][:, :1]
    strength = jnp.zeros((half, 1), F32)
    for index in range(CLIPS):
        strength = jnp.where(clip == index, scale_ref[index], strength)
    lean = jnp.where(side == 0, strength, 1.0 - strength)
    for step, out in enumerate((own, *sent)):
        target = jnp.bitwise_xor(blk, step)
        columns = pl.ds(pl.multiple_of(target * width, width), width)
        other = other_ref[:, columns].astype(F32)
        guided = other + lean * (mine_ref[:, columns] - other)
        out[...] = guided.astype(out.dtype)


def place_kernel(own, got1, got2, got3, placing, *outs):
    guided = own[...] + got1[...].astype(F32) + got2[...].astype(F32) + got3[...].astype(F32)
    placed = jnp.dot(placing[...], guided.astype(BF16), preferred_element_type=F32).astype(BF16)
    if len(outs) == 1:
        outs[0][...] = placed
    else:
        count = outs[0].shape[0]
        for index, out in enumerate(outs):
            out[...] = placed[index * count : (index + 1) * count, :]


def arrange_kernel(own, got1, got2, got3, out):
    place = lax.axis_index("seq")
    count = own.shape[0]
    for step, source in enumerate((own, got1, got2, got3)):
        origin = lax.rem(place + 4 - step, 4)
        out[pl.ds(pl.multiple_of(origin * count, count), count), :] = source[...]


def exchanged(value, axis, mask):
    pairs = [(index, index ^ mask) for index in range(lax.axis_size(axis))]
    return lax.ppermute(value, axis, pairs)


def shards(
    queries, keys, values, residual, w_out, w_up, w_down, modulation, guide_scale, slot_clip, owner
):
    slots, width = queries.shape[1:]
    half = slots // 2
    seq_count = lax.axis_size("seq")
    capacity = max(2, slots // seq_count)
    side, place = lax.axis_index("cfg"), lax.axis_index("seq")

    clip_wide = jnp.broadcast_to(slot_clip[:, None], (slots, 128))
    clip_half = lax.dynamic_slice_in_dim(slot_clip, side * half, half, 0)
    owner_half = lax.dynamic_slice_in_dim(owner[:, 0], side * half, half, 0)
    order = jnp.arange(half, dtype=jnp.int32)
    before = (owner_half[None, :] == owner_half[:, None]) & (order[None, :] < order[:, None])
    rank = jnp.sum(before.astype(jnp.int32), axis=1)
    if seq_count == 4:
        lane = lax.rem(owner_half - place + seq_count, seq_count)
    else:
        lane = owner_half
    target = jnp.where(clip_half < CLIPS, lane * capacity + rank, -1)
    placing = (
        jnp.arange(seq_count * capacity, dtype=jnp.int32)[:, None] == target[None, :]
    ).astype(BF16)

    near, w_half = fetch_near(w_out)
    if seq_count == 4:
        whole, (up, down), attended = attention_by_head(
            queries[0],
            keys[0],
            values[0],
            slot_clip,
            (clip_wide, placing, w_half),
            (w_up, w_down),
            functools.partial(fetch_rest, w_out, near, w_half),
        )
    else:
        attended = attention_by_rows(queries[0], keys[0], values[0], slot_clip)
        up, down = load(w_up, w_down, attended[0])
        whole = fetch_rest(w_out, near, w_half, attended[0])

    parts = []
    for turn in range(2):
        piece = attended[turn]
        gathered = [piece] + [exchanged(piece, "blk", mask) for mask in (1, 2, 3)]
        parts.append(feed(turn, gathered, whole, up, down, residual[0], modulation, clip_wide))
    other = exchanged(parts[0], "cfg", 1)
    own, *sent = pl.pallas_call(
        guide_kernel,
        out_shape=[shape_of((half, width), F32)] + [shape_of((half, width))] * 3,
        in_specs=[VMEM] * 3 + [pl.BlockSpec(memory_space=pltpu.SMEM)],
        out_specs=[VMEM] * 4,
        compiler_params=params(16),
        name="guide",
    )(parts[1], other, clip_wide, guide_scale)
    got = [exchanged(piece, "blk", mask) for mask, piece in zip((1, 2, 3), sent)]
    by_step = seq_count == 4
    placed = pl.pallas_call(
        place_kernel,
        out_shape=[shape_of((capacity, width))] * 4
        if by_step
        else [shape_of((seq_count * capacity, width))],
        in_specs=[VMEM] * 5,
        out_specs=[VMEM] * (4 if by_step else 1),
        compiler_params=params(16),
        name="place",
    )(own, *got, placing)
    if not by_step:
        arrived = lax.all_to_all(
            placed[0].reshape(seq_count, capacity, width), "seq", split_axis=0, concat_axis=0,
            tiled=True,
        )
        return arrived.reshape(1, seq_count * capacity, width)
    home = [
        lax.ppermute(placed[step], "seq", [(i, (i + step) % 4) for i in range(4)])
        for step in (1, 2, 3)
    ]
    arranged = pl.pallas_call(
        arrange_kernel,
        out_shape=shape_of((4 * capacity, width)),
        in_specs=[VMEM] * 4,
        out_specs=VMEM,
        compiler_params=params(16),
        name="arrange",
    )(placed[0], *home)
    return arranged[None]


def solution(mesh):
    placed = (
        P("cfg", "seq", "blk"),
        P("cfg", "seq", "blk"),
        P("cfg", "seq", "blk"),
        P("cfg", "seq", None),
        P("blk", None),
        P(None, "blk"),
        P("blk", None),
        P(),
        P(),
        P("seq"),
        P("seq", None),
    )
    return jax.shard_map(
        shards, mesh=mesh, in_specs=placed, out_specs=P("cfg", "seq", "blk"), check_vma=False
    )
```

```python
import functools
import math

import jax
import jax.numpy as jnp
from jax import lax
from jax.experimental import pallas as pl
from jax.experimental.pallas import tpu as pltpu
from jax.sharding import PartitionSpec as P

D = 1536
HEAD_DIM = 128
CLIPS = 3
NEG_FILL = -1e30
FAR = 2.0**100
VMEM = pl.BlockSpec(memory_space=pltpu.VMEM)
ANY = pl.BlockSpec(memory_space=pl.ANY)
F32 = jnp.float32
BF16 = jnp.bfloat16


def shape_of(extent, dtype=BF16):
    return jax.ShapeDtypeStruct(extent, dtype)


def params(mib):
    return pltpu.CompilerParams(vmem_limit_bytes=mib * 2**20)


def cost(flops, moved):
    return pl.CostEstimate(flops=flops, bytes_accessed=moved, transcendentals=0)


def head_at(side, place):
    return jnp.where(side == 0, place, 3 - place)


def works(side, place):
    return place < 3 if side == 0 else place >= 1


def hop(value, step, back=False):
    pairs = []
    for side in range(2):
        for place in range(4):
            target = (place + step) % 4
            if works(side, target):
                pair = (side * 4 + place, side * 4 + target)
                pairs.append(pair[::-1] if back else pair)
    return lax.ppermute(value, ("cfg", "seq"), pairs)


def pack_kernel(q_ref, k_ref, v_ref, clip_ref, *refs):
    outs, sems = refs[:4], refs[4]
    side, place = lax.axis_index("cfg"), lax.axis_index("seq")
    slots = q_ref.shape[0]
    copies = []
    for step, out in enumerate(outs):
        head = jnp.clip(head_at(side, lax.rem(place + step, 4)), 0, 2)
        columns = pl.ds(pl.multiple_of(head * HEAD_DIM, HEAD_DIM), HEAD_DIM)
        for part, source in enumerate((q_ref, k_ref, v_ref)):
            target = out.at[part * slots : (part + 1) * slots, :]
            copy = pltpu.make_async_copy(source.at[:, columns], target, sems.at[len(copies)])
            copy.start()
            copies.append(copy)
    rows = clip_ref[...].astype(F32).astype(BF16)
    for out in outs:
        out[3 * slots :, :] = jnp.zeros((16, 128), BF16)
        out[3 * slots : 3 * slots + rows.shape[0], :] = rows
    for copy in copies:
        copy.wait()


def attend_kernel(*refs):
    blocks, outs, (q_aug, k_aug, v_aug, clips) = refs[:4], refs[9:13], refs[13:]
    slots = outs[0].shape[0]
    lane = lax.broadcasted_iota(jnp.int32, (128, 128), 1)
    row = lax.broadcasted_iota(jnp.int32, (128, 128), 0)
    eye = (lane == row).astype(BF16)
    for index, block in enumerate(blocks):
        base = index * slots
        here = slice(base, base + slots)
        q_aug[here, :128] = block[:slots, :]
        k_aug[here, :128] = block[slots : 2 * slots, :]
        v_aug[here, :128] = block[2 * slots : 3 * slots, :]
        turned = lax.dot_general(
            eye, block[3 * slots :, :], (((1,), (1,)), ((), ())), preferred_element_type=F32
        )
        for group in range(slots // 128):
            part = slice(base + group * 128, base + (group + 1) * 128)
            clip = jnp.broadcast_to(turned[:, group : group + 1], (128, 128)).astype(jnp.int32)
            clips[part, :] = clip
            same = lane == clip
            kept = same & (clip < CLIPS)
            k_aug[part, 128:] = same.astype(BF16)
            q_aug[part, 128:] = jnp.where(kept | (lane > CLIPS), 0.0, -FAR).astype(BF16)
            v_aug[part, 128:] = (lane == 0).astype(BF16)
    scale = math.log2(math.e) / math.sqrt(HEAD_DIM)
    for index, out in enumerate(outs):
        here = slice(index * slots, (index + 1) * slots)
        scores = lax.dot_general(
            q_aug[here, :], k_aug[...], (((1,), (1,)), ((), ())), preferred_element_type=F32
        )
        peak = jnp.max(scores, axis=1, keepdims=True)
        probs = jnp.exp2((scores - peak) * scale).astype(BF16)
        summed = jnp.dot(probs, v_aug[...], preferred_element_type=F32)
        result = summed[:, :128] / summed[:, 128:129]
        out[...] = jnp.where(clips[here, :] < CLIPS, result, 0.0).astype(BF16)


def regroup_kernel(own, back1, back2, back3, first, second):
    side, place = lax.axis_index("cfg"), lax.axis_index("seq")
    half = first.shape[0]
    for head in range(3):
        home = jnp.where(side == 0, head, 3 - head)
        step = lax.rem(home - place + 4, 4)
        columns = slice(head * HEAD_DIM, (head + 1) * HEAD_DIM)
        for index, source in enumerate((own, back1, back2, back3)):

            @pl.when(step == index)
            def _():
                for out, which in ((first, 1 - side), (second, side)):
                    rows = pl.ds(pl.multiple_of(which * half, half), half)
                    out[:, columns] = source[rows, :]


def kept(value):
    return pltpu.with_memory_space_constraint(value, pltpu.VMEM)


def afar(value):
    return pltpu.with_memory_space_constraint(value, pltpu.HBM)


def load_kernel(up, down, after, up_out, down_out, sems):
    copies = [
        pltpu.make_async_copy(source, target, sems.at[index])
        for index, (source, target) in enumerate(((up, up_out), (down, down_out)))
    ]
    for copy in copies:
        copy.start()
    for copy in copies:
        copy.wait()


def load(up, down, after):
    return pl.pallas_call(
        load_kernel,
        out_shape=[pltpu.VMEM(up.shape, BF16), pltpu.VMEM(down.shape, BF16)],
        in_specs=[ANY] * 3,
        out_specs=[VMEM] * 2,
        scratch_shapes=[pltpu.SemaphoreType.DMA((2,))],
        compiler_params=params(16),
        name="load",
    )(afar(up), afar(down), after)


def across(value, masks):
    pairs = [
        (side * 4 + blk, side * 4 + (blk ^ masks[side])) for side in range(2) for blk in range(4)
    ]
    return lax.ppermute(value, ("cfg", "blk"), pairs)


def cut_kernel(got, out, sem):
    part = out.shape[0]
    offset = pl.multiple_of((1 - lax.axis_index("cfg")) * part, part)
    copy = pltpu.make_async_copy(got.at[pl.ds(offset, part), :], out, sem)
    copy.start()
    copy.wait()


def join_kernel(own, near, near_swap, far, far_swap, after, out, sems):
    side = lax.axis_index("cfg")
    width, part = own.shape[0], far.shape[0]
    plan = (
        (own, 0, width),
        (near, (1 + side) * width, width),
        (near_swap, (2 - side) * width, width),
        (far, 3 * width + (1 - side) * part, part),
        (far_swap, 3 * width + side * part, part),
    )
    copies = []
    for index, (source, offset, rows) in enumerate(plan):
        target = out.at[pl.ds(pl.multiple_of(offset, part), rows), :]
        copy = pltpu.make_async_copy(source, target, sems.at[index])
        copy.start()
        copies.append(copy)
    for copy in copies:
        copy.wait()


def gate_kernel(value, after, out):
    pass


def gate(value, after):
    return pl.pallas_call(
        gate_kernel,
        out_shape=shape_of(value.shape, value.dtype),
        in_specs=[ANY] * 2,
        out_specs=ANY,
        input_output_aliases={0: 0},
        compiler_params=params(1),
        name="gate",
    )(value, after)


def fetch_near(w_out):
    near = across(w_out, (1, 2))
    half = pl.pallas_call(
        cut_kernel,
        out_shape=shape_of((w_out.shape[0] // 2, D)),
        in_specs=[ANY],
        out_specs=ANY,
        scratch_shapes=[pltpu.SemaphoreType.DMA],
        compiler_params=params(16),
        name="cut",
    )(near)
    return near, half


def fetch_rest(w_out, near, half, after):
    far = across(half, (2, 1))
    far = gate(far, after)
    pieces = (afar(w_out), near, exchanged(near, "cfg", 1), far, exchanged(far, "cfg", 1))
    return pl.pallas_call(
        join_kernel,
        out_shape=pltpu.VMEM((D, D), BF16),
        in_specs=[ANY] * 6,
        out_specs=VMEM,
        scratch_shapes=[pltpu.SemaphoreType.DMA((5,))],
        compiler_params=params(16),
        name="join",
    )(*pieces, after)


def attention_by_head(query, key, value, slot_clip, early, weights):
    slots = query.shape[0]
    packed = pl.pallas_call(
        pack_kernel,
        out_shape=[shape_of((3 * slots + 16, 128))] * 4,
        in_specs=[ANY] * 3 + [VMEM],
        out_specs=[VMEM] * 4,
        scratch_shapes=[pltpu.SemaphoreType.DMA((12,))],
        compiler_params=params(16),
        name="pack",
    )(afar(query), afar(key), afar(value), slot_clip.reshape(slots // 128, 128))
    blocks = [packed[0]] + [hop(packed[step], step) for step in (1, 2, 3)]
    early = (*early, *(kept(weight) for weight in load(*weights, packed[0])))
    results = pl.pallas_call(
        attend_kernel,
        out_shape=[shape_of((slots, 128))] * 4,
        in_specs=[VMEM] * 4 + [ANY] * (len(early) - 2) + [VMEM] * 2,
        out_specs=[VMEM] * 4,
        scratch_shapes=[pltpu.VMEM((4 * slots, 256), BF16)] * 3
        + [pltpu.VMEM((4 * slots, 128), jnp.int32)],
        compiler_params=params(28),
        cost_estimate=cost(2**32, 2**21),
        name="attend",
    )(*blocks, *early)
    backs = [hop(results[step], step, back=True) for step in (1, 2, 3)]
    half = slots // 2
    return early[-2:], pl.pallas_call(
        regroup_kernel,
        out_shape=[shape_of((half, 3 * HEAD_DIM))] * 2,
        in_specs=[VMEM] * 4,
        out_specs=[VMEM] * 2,
        compiler_params=params(16),
        name="regroup",
    )(results[0], *backs)


def attention_by_rows(query, key, value, slot_clip):
    slots, width = query.shape
    heads = width // HEAD_DIM
    live = slot_clip < CLIPS
    factor = 1.0 / math.sqrt(HEAD_DIM)
    query_heads = query.reshape(slots, heads, HEAD_DIM)

    def absorb(carry, piece):
        key_piece, value_piece, clip_piece = piece
        best, total, accum = carry
        kept = (clip_piece[None, :] == slot_clip[:, None]) & live[:, None]
        scores = jnp.einsum("qhd,khd->hqk", query_heads, key_piece, preferred_element_type=F32)
        scores = jnp.where(kept[None], scores * factor, NEG_FILL)
        new_best = jnp.maximum(best, jnp.max(scores, axis=-1))
        fade = jnp.exp(best - new_best)
        probs = jnp.exp(scores - new_best[..., None])
        total = total * fade + jnp.sum(probs, axis=-1)
        added = jnp.einsum(
            "hqk,khd->qhd", probs.astype(BF16), value_piece, preferred_element_type=F32
        )
        accum = accum * jnp.transpose(fade)[:, :, None] + added
        return (new_best, total, accum), None

    start = (
        jnp.full((heads, slots), NEG_FILL, F32),
        jnp.zeros((heads, slots), F32),
        jnp.zeros((slots, heads, HEAD_DIM), F32),
    )
    pieces = (
        lax.all_gather(key, "seq").reshape(-1, slots, heads, HEAD_DIM),
        lax.all_gather(value, "seq").reshape(-1, slots, heads, HEAD_DIM),
        lax.all_gather(slot_clip, "seq"),
    )
    (best, total, accum), _ = lax.scan(absorb, start, pieces)
    attended = (accum / jnp.transpose(total)[:, :, None]).reshape(slots, width)
    attended = jnp.where(live[:, None], attended, 0.0).astype(BF16)
    half = slots // 2
    side = lax.axis_index("cfg")
    return [
        lax.dynamic_slice_in_dim(attended, which * half, half, 0) for which in (1 - side, side)
    ]


def feed_kernel(turn, *refs):
    (att, (w_out, up, down, res_hbm, mod, clip_ref), out) = refs[:4], refs[4:10], refs[10]
    res, mixed, total, normed, hidden, sem = refs[11:]
    side, blk = lax.axis_index("cfg"), lax.axis_index("blk")
    half = out.shape[0]
    which = 1 - side if turn == 0 else side
    rows = pl.ds(pl.multiple_of(which * half, half), half)
    width = att[0].shape[1]
    copy = pltpu.make_async_copy(res_hbm.at[rows, :], res, sem)
    copy.start()
    rows_in = jnp.concatenate([piece[...] for piece in att], axis=1)
    clip = clip_ref[rows, :][:, :1]
    tile = 512

    def chosen(kind, columns):
        picked = jnp.zeros((half, tile), F32)
        for index in range(CLIPS):
            line = mod[index, kind : kind + 1, columns]
            picked = jnp.where(clip == index, line, picked)
        return picked

    for start in range(0, D, tile):
        columns = slice(start, start + tile)
        projected = jnp.dot(rows_in, w_out[:, columns], preferred_element_type=F32)
        mixed[:, columns] = chosen(0, columns) * projected
    copy.wait()
    held = mixed[...] + res[...].astype(F32)
    mixed[...] = held
    centre = held - jnp.mean(held, axis=1, keepdims=True)
    spread = lax.rsqrt(jnp.mean(centre * centre, axis=1, keepdims=True) + 1e-06)
    for start in range(0, D, tile):
        columns = slice(start, start + tile)
        value = centre[:, columns] * spread * (1.0 + chosen(2, columns)) + chosen(1, columns)
        normed[:, columns] = value.astype(BF16)
    for start in range(0, D, tile):
        columns = slice(start, start + tile)
        raised = jnp.dot(normed[...], up[:, columns], preferred_element_type=F32)
        hidden[:, columns] = jax.nn.gelu(raised, approximate=True).astype(BF16)
    for start in range(0, D, tile):
        columns = slice(start, start + tile)
        lowered = jnp.dot(hidden[...], down[:, columns], preferred_element_type=F32)
        total[:, columns] = chosen(3, columns) * lowered
    own = pl.ds(pl.multiple_of(blk * width, width), width)
    total[:, own] = total[:, own] + mixed[:, own]
    out[...] = total[...].astype(out.dtype)


def feed(turn, att, w_out, w_up, w_down, residual, mod, clip_wide):
    half, width = att[0].shape
    return pl.pallas_call(
        functools.partial(feed_kernel, turn),
        out_shape=shape_of((half, D), BF16 if turn == 0 else F32),
        in_specs=[VMEM] * 7 + [ANY] + [VMEM] * 2,
        out_specs=VMEM,
        scratch_shapes=[
            pltpu.VMEM((half, D), BF16),
            pltpu.VMEM((half, D), F32),
            pltpu.VMEM((half, D), F32),
            pltpu.VMEM((half, D), BF16),
            pltpu.VMEM((half, D), BF16),
            pltpu.SemaphoreType.DMA,
        ],
        compiler_params=params(24),
        cost_estimate=cost(2**36, 2**24),
        name="feed",
    )(*att, kept(w_out), kept(w_up), kept(w_down), afar(residual), mod, clip_wide)


def guide_kernel(mine_ref, other_ref, clip_ref, scale_ref, own, *sent):
    side, blk = lax.axis_index("cfg"), lax.axis_index("blk")
    half, width = own.shape
    clip = clip_ref[pl.ds(pl.multiple_of(side * half, half), half), :][:, :1]
    strength = jnp.zeros((half, 1), F32)
    for index in range(CLIPS):
        strength = jnp.where(clip == index, scale_ref[index], strength)
    lean = jnp.where(side == 0, strength, 1.0 - strength)
    for step, out in enumerate((own, *sent)):
        target = jnp.bitwise_xor(blk, step)
        columns = pl.ds(pl.multiple_of(target * width, width), width)
        other = other_ref[:, columns].astype(F32)
        guided = other + lean * (mine_ref[:, columns] - other)
        out[...] = guided.astype(out.dtype)


def place_kernel(own, got1, got2, got3, placing, *outs):
    guided = own[...] + got1[...].astype(F32) + got2[...].astype(F32) + got3[...].astype(F32)
    placed = jnp.dot(placing[...], guided.astype(BF16), preferred_element_type=F32).astype(BF16)
    if len(outs) == 1:
        outs[0][...] = placed
    else:
        count = outs[0].shape[0]
        for index, out in enumerate(outs):
            out[...] = placed[index * count : (index + 1) * count, :]


def arrange_kernel(own, got1, got2, got3, out):
    place = lax.axis_index("seq")
    count = own.shape[0]
    for step, source in enumerate((own, got1, got2, got3)):
        origin = lax.rem(place + 4 - step, 4)
        out[pl.ds(pl.multiple_of(origin * count, count), count), :] = source[...]


def exchanged(value, axis, mask):
    pairs = [(index, index ^ mask) for index in range(lax.axis_size(axis))]
    return lax.ppermute(value, axis, pairs)


def shards(
    queries, keys, values, residual, w_out, w_up, w_down, modulation, guide_scale, slot_clip, owner
):
    slots, width = queries.shape[1:]
    half = slots // 2
    seq_count = lax.axis_size("seq")
    capacity = max(2, slots // seq_count)
    side, place = lax.axis_index("cfg"), lax.axis_index("seq")

    clip_wide = jnp.broadcast_to(slot_clip[:, None], (slots, 128))
    clip_half = lax.dynamic_slice_in_dim(slot_clip, side * half, half, 0)
    owner_half = lax.dynamic_slice_in_dim(owner[:, 0], side * half, half, 0)
    order = jnp.arange(half, dtype=jnp.int32)
    before = (owner_half[None, :] == owner_half[:, None]) & (order[None, :] < order[:, None])
    rank = jnp.sum(before.astype(jnp.int32), axis=1)
    if seq_count == 4:
        lane = lax.rem(owner_half - place + seq_count, seq_count)
    else:
        lane = owner_half
    target = jnp.where(clip_half < CLIPS, lane * capacity + rank, -1)
    placing = (
        jnp.arange(seq_count * capacity, dtype=jnp.int32)[:, None] == target[None, :]
    ).astype(BF16)

    near, w_half = fetch_near(w_out)
    if seq_count == 4:
        (up, down), attended = attention_by_head(
            queries[0],
            keys[0],
            values[0],
            slot_clip,
            (clip_wide, placing, w_half),
            (w_up, w_down),
        )
    else:
        attended = attention_by_rows(queries[0], keys[0], values[0], slot_clip)
        up, down = load(w_up, w_down, attended[0])

    whole = fetch_rest(w_out, near, w_half, attended[0])
    parts = []
    for turn in range(2):
        piece = attended[turn]
        gathered = [piece] + [exchanged(piece, "blk", mask) for mask in (1, 2, 3)]
        parts.append(feed(turn, gathered, whole, up, down, residual[0], modulation, clip_wide))
    other = exchanged(parts[0], "cfg", 1)
    own, *sent = pl.pallas_call(
        guide_kernel,
        out_shape=[shape_of((half, width), F32)] + [shape_of((half, width))] * 3,
        in_specs=[VMEM] * 3 + [pl.BlockSpec(memory_space=pltpu.SMEM)],
        out_specs=[VMEM] * 4,
        compiler_params=params(16),
        name="guide",
    )(parts[1], other, clip_wide, guide_scale)
    got = [exchanged(piece, "blk", mask) for mask, piece in zip((1, 2, 3), sent)]
    by_step = seq_count == 4
    placed = pl.pallas_call(
        place_kernel,
        out_shape=[shape_of((capacity, width))] * 4
        if by_step
        else [shape_of((seq_count * capacity, width))],
        in_specs=[VMEM] * 5,
        out_specs=[VMEM] * (4 if by_step else 1),
        compiler_params=params(16),
        name="place",
    )(own, *got, placing)
    if not by_step:
        arrived = lax.all_to_all(
            placed[0].reshape(seq_count, capacity, width), "seq", split_axis=0, concat_axis=0,
            tiled=True,
        )
        return arrived.reshape(1, seq_count * capacity, width)
    home = [
        lax.ppermute(placed[step], "seq", [(i, (i + step) % 4) for i in range(4)])
        for step in (1, 2, 3)
    ]
    arranged = pl.pallas_call(
        arrange_kernel,
        out_shape=shape_of((4 * capacity, width)),
        in_specs=[VMEM] * 4,
        out_specs=VMEM,
        compiler_params=params(16),
        name="arrange",
    )(placed[0], *home)
    return arranged[None]


def solution(mesh):
    placed = (
        P("cfg", "seq", "blk"),
        P("cfg", "seq", "blk"),
        P("cfg", "seq", "blk"),
        P("cfg", "seq", None),
        P("blk", None),
        P(None, "blk"),
        P("blk", None),
        P(),
        P(),
        P("seq"),
        P("seq", None),
    )
    return jax.shard_map(
        shards, mesh=mesh, in_specs=placed, out_specs=P("cfg", "seq", "blk"), check_vma=False
    )
```

```python
import functools
import math

import jax
import jax.numpy as jnp
from jax import lax
from jax.experimental import pallas as pl
from jax.experimental.pallas import tpu as pltpu
from jax.sharding import PartitionSpec as P

D = 1536
HEAD_DIM = 128
CLIPS = 3
NEG_FILL = -1e30
FAR = 2.0**100
VMEM = pl.BlockSpec(memory_space=pltpu.VMEM)
ANY = pl.BlockSpec(memory_space=pl.ANY)
F32 = jnp.float32
BF16 = jnp.bfloat16


def shape_of(extent, dtype=BF16):
    return jax.ShapeDtypeStruct(extent, dtype)


def params(mib):
    return pltpu.CompilerParams(vmem_limit_bytes=mib * 2**20)


def cost(flops, moved):
    return pl.CostEstimate(flops=flops, bytes_accessed=moved, transcendentals=0)


STEPS = (0, 2, 3, 1)


def head_at(side, place):
    return jnp.where(side == 0, place, 3 - place)


def works(side, place):
    return place < 3 if side == 0 else place >= 1


def hop(value, step, back=False):
    pairs = []
    for side in range(2):
        for place in range(4):
            target = place ^ step
            if works(side, target):
                pair = (side * 4 + place, side * 4 + target)
                pairs.append(pair[::-1] if back else pair)
    return lax.ppermute(value, ("cfg", "seq"), pairs)


def pack_kernel(q_ref, k_ref, v_ref, clip_ref, *refs):
    outs, clips, sems = refs[:4], refs[4], refs[5]
    side, place = lax.axis_index("cfg"), lax.axis_index("seq")
    slots = q_ref.shape[0]
    clip_copy = pltpu.make_async_copy(clip_ref, clips, sems.at[12])
    clip_copy.start()
    copies = []
    for step, out in zip(STEPS, outs):
        head = jnp.clip(head_at(side, jnp.bitwise_xor(place, step)), 0, 2)
        columns = pl.ds(pl.multiple_of(head * HEAD_DIM, HEAD_DIM), HEAD_DIM)
        for part, source in enumerate((q_ref, k_ref, v_ref)):
            target = out.at[part * slots : (part + 1) * slots, :]
            copy = pltpu.make_async_copy(source.at[:, columns], target, sems.at[len(copies)])
            copy.start()
            copies.append(copy)
    clip_copy.wait()
    rows = clips[...].astype(F32).astype(BF16)
    for out in outs:
        out[3 * slots :, :] = jnp.zeros((16, 128), BF16)
        out[3 * slots : 3 * slots + rows.shape[0], :] = rows
    for copy in copies:
        copy.wait()


def attend_kernel(*refs):
    blocks, outs, (q_aug, k_aug, v_aug, clips) = refs[:4], refs[9:13], refs[13:]
    slots = outs[0].shape[0]
    lane = lax.broadcasted_iota(jnp.int32, (128, 128), 1)
    row = lax.broadcasted_iota(jnp.int32, (128, 128), 0)
    eye = (lane == row).astype(BF16)
    for index, block in enumerate(blocks):
        base = index * slots
        here = slice(base, base + slots)
        q_aug[here, :128] = block[:slots, :]
        k_aug[here, :128] = block[slots : 2 * slots, :]
        v_aug[here, :128] = block[2 * slots : 3 * slots, :]
        turned = lax.dot_general(
            eye, block[3 * slots :, :], (((1,), (1,)), ((), ())), preferred_element_type=F32
        )
        for group in range(slots // 128):
            part = slice(base + group * 128, base + (group + 1) * 128)
            clip = jnp.broadcast_to(turned[:, group : group + 1], (128, 128)).astype(jnp.int32)
            clips[part, :] = clip
            same = lane == clip
            kept = same & (clip < CLIPS)
            k_aug[part, 128:] = same.astype(BF16)
            q_aug[part, 128:] = jnp.where(kept | (lane > CLIPS), 0.0, -FAR).astype(BF16)
            v_aug[part, 128:] = (lane == 0).astype(BF16)
    scale = math.log2(math.e) / math.sqrt(HEAD_DIM)
    for index, out in enumerate(outs):
        here = slice(index * slots, (index + 1) * slots)
        scores = lax.dot_general(
            q_aug[here, :], k_aug[...], (((1,), (1,)), ((), ())), preferred_element_type=F32
        )
        peak = jnp.max(scores, axis=1, keepdims=True)
        probs = jnp.exp2((scores - peak) * scale).astype(BF16)
        summed = jnp.dot(probs, v_aug[...], preferred_element_type=F32)
        result = summed[:, :128] / summed[:, 128:129]
        out[...] = jnp.where(clips[here, :] < CLIPS, result, 0.0).astype(BF16)


def regroup_kernel(own, back1, back2, back3, first, second):
    side, place = lax.axis_index("cfg"), lax.axis_index("seq")
    half = first.shape[0]
    for head in range(3):
        home = jnp.where(side == 0, head, 3 - head)
        step = jnp.bitwise_xor(home, place)
        columns = slice(head * HEAD_DIM, (head + 1) * HEAD_DIM)
        for index, source in zip(STEPS, (own, back1, back2, back3)):

            @pl.when(step == index)
            def _():
                for out, which in ((first, 1 - side), (second, side)):
                    rows = pl.ds(pl.multiple_of(which * half, half), half)
                    out[:, columns] = source[rows, :]


def kept(value):
    return pltpu.with_memory_space_constraint(value, pltpu.VMEM)


def afar(value):
    return pltpu.with_memory_space_constraint(value, pltpu.HBM)


def load_kernel(up, down, after, up_out, down_out, sems):
    copies = [
        pltpu.make_async_copy(source, target, sems.at[index])
        for index, (source, target) in enumerate(((up, up_out), (down, down_out)))
    ]
    for copy in copies:
        copy.start()
    for copy in copies:
        copy.wait()


def load(up, down, after):
    return pl.pallas_call(
        load_kernel,
        out_shape=[pltpu.VMEM(up.shape, BF16), pltpu.VMEM(down.shape, BF16)],
        in_specs=[ANY] * 3,
        out_specs=[VMEM] * 2,
        scratch_shapes=[pltpu.SemaphoreType.DMA((2,))],
        compiler_params=params(16),
        name="load",
    )(afar(up), afar(down), after)


def across(value, masks):
    pairs = [
        (side * 4 + blk, side * 4 + (blk ^ masks[side])) for side in range(2) for blk in range(4)
    ]
    return lax.ppermute(value, ("cfg", "blk"), pairs)


def cut_kernel(got, out, sem):
    part = out.shape[0]
    offset = pl.multiple_of((1 - lax.axis_index("cfg")) * part, part)
    copy = pltpu.make_async_copy(got.at[pl.ds(offset, part), :], out, sem)
    copy.start()
    copy.wait()


def join_kernel(own, near, near_swap, far, far_swap, after, out, sems):
    side = lax.axis_index("cfg")
    width, part = own.shape[0], far.shape[0]
    plan = (
        (own, 0, width),
        (near, (1 + side) * width, width),
        (near_swap, (2 - side) * width, width),
        (far, 3 * width + (1 - side) * part, part),
        (far_swap, 3 * width + side * part, part),
    )
    copies = []
    for index, (source, offset, rows) in enumerate(plan):
        target = out.at[pl.ds(pl.multiple_of(offset, part), rows), :]
        copy = pltpu.make_async_copy(source, target, sems.at[index])
        copy.start()
        copies.append(copy)
    for copy in copies:
        copy.wait()


def gate_kernel(value, after, out):
    pass


def gate(value, after):
    return pl.pallas_call(
        gate_kernel,
        out_shape=shape_of(value.shape, value.dtype),
        in_specs=[ANY] * 2,
        out_specs=ANY,
        input_output_aliases={0: 0},
        compiler_params=params(1),
        name="gate",
    )(value, after)


def fetch_near(w_out):
    near = across(w_out, (1, 2))
    half = pl.pallas_call(
        cut_kernel,
        out_shape=shape_of((w_out.shape[0] // 2, D)),
        in_specs=[ANY],
        out_specs=ANY,
        scratch_shapes=[pltpu.SemaphoreType.DMA],
        compiler_params=params(16),
        name="cut",
    )(near)
    return near, half


def fetch_rest(w_out, near, half, after):
    far = across(half, (2, 1))
    far = gate(far, after)
    pieces = (afar(w_out), near, exchanged(near, "cfg", 1), far, exchanged(far, "cfg", 1))
    return pl.pallas_call(
        join_kernel,
        out_shape=pltpu.VMEM((D, D), BF16),
        in_specs=[ANY] * 6,
        out_specs=VMEM,
        scratch_shapes=[pltpu.SemaphoreType.DMA((5,))],
        compiler_params=params(16),
        name="join",
    )(*pieces, after)


def attention_by_head(query, key, value, slot_clip, early, weights):
    slots = query.shape[0]
    packed = pl.pallas_call(
        pack_kernel,
        out_shape=[shape_of((3 * slots + 16, 128))] * 4,
        in_specs=[ANY] * 4,
        out_specs=[VMEM] * 4,
        scratch_shapes=[
            pltpu.VMEM((slots // 128, 128), jnp.int32),
            pltpu.SemaphoreType.DMA((13,)),
        ],
        compiler_params=params(16),
        name="pack",
    )(afar(query), afar(key), afar(value), afar(slot_clip.reshape(slots // 128, 128)))
    blocks = [packed[0]] + [hop(packed[index], STEPS[index]) for index in (1, 2, 3)]
    early = (*early, *(kept(weight) for weight in load(*weights, packed[0])))
    results = pl.pallas_call(
        attend_kernel,
        out_shape=[shape_of((slots, 128))] * 4,
        in_specs=[VMEM] * 4 + [ANY] * (len(early) - 2) + [VMEM] * 2,
        out_specs=[VMEM] * 4,
        scratch_shapes=[pltpu.VMEM((4 * slots, 256), BF16)] * 3
        + [pltpu.VMEM((4 * slots, 128), jnp.int32)],
        compiler_params=params(28),
        cost_estimate=cost(2**32, 2**21),
        name="attend",
    )(*blocks, *early)
    backs = [hop(results[index], STEPS[index], back=True) for index in (1, 2, 3)]
    half = slots // 2
    return early[-2:], pl.pallas_call(
        regroup_kernel,
        out_shape=[shape_of((half, 3 * HEAD_DIM))] * 2,
        in_specs=[VMEM] * 4,
        out_specs=[VMEM] * 2,
        compiler_params=params(16),
        name="regroup",
    )(results[0], *backs)


def attention_by_rows(query, key, value, slot_clip):
    slots, width = query.shape
    heads = width // HEAD_DIM
    live = slot_clip < CLIPS
    factor = 1.0 / math.sqrt(HEAD_DIM)
    query_heads = query.reshape(slots, heads, HEAD_DIM)

    def absorb(carry, piece):
        key_piece, value_piece, clip_piece = piece
        best, total, accum = carry
        kept = (clip_piece[None, :] == slot_clip[:, None]) & live[:, None]
        scores = jnp.einsum("qhd,khd->hqk", query_heads, key_piece, preferred_element_type=F32)
        scores = jnp.where(kept[None], scores * factor, NEG_FILL)
        new_best = jnp.maximum(best, jnp.max(scores, axis=-1))
        fade = jnp.exp(best - new_best)
        probs = jnp.exp(scores - new_best[..., None])
        total = total * fade + jnp.sum(probs, axis=-1)
        added = jnp.einsum(
            "hqk,khd->qhd", probs.astype(BF16), value_piece, preferred_element_type=F32
        )
        accum = accum * jnp.transpose(fade)[:, :, None] + added
        return (new_best, total, accum), None

    start = (
        jnp.full((heads, slots), NEG_FILL, F32),
        jnp.zeros((heads, slots), F32),
        jnp.zeros((slots, heads, HEAD_DIM), F32),
    )
    pieces = (
        lax.all_gather(key, "seq").reshape(-1, slots, heads, HEAD_DIM),
        lax.all_gather(value, "seq").reshape(-1, slots, heads, HEAD_DIM),
        lax.all_gather(slot_clip, "seq"),
    )
    (best, total, accum), _ = lax.scan(absorb, start, pieces)
    attended = (accum / jnp.transpose(total)[:, :, None]).reshape(slots, width)
    attended = jnp.where(live[:, None], attended, 0.0).astype(BF16)
    half = slots // 2
    side = lax.axis_index("cfg")
    return [
        lax.dynamic_slice_in_dim(attended, which * half, half, 0) for which in (1 - side, side)
    ]


def chosen(mod, kind, clip, columns):
    picked = jnp.zeros((clip.shape[0], mod[0, :1, columns].shape[1]), F32)
    for index in range(CLIPS):
        picked = jnp.where(clip == index, mod[index, kind : kind + 1, columns], picked)
    return picked


def feed_kernel(turn, *refs):
    att, (w_out, up, down, res_hbm, mod, clip_ref), refs = refs[:4], refs[4:10], refs[10:]
    if turn == 0:
        out, mixed, hidden, res, normed, sem = refs
    else:
        hidden, mixed, res, normed, sem = refs
    side, blk = lax.axis_index("cfg"), lax.axis_index("blk")
    half = hidden.shape[0]
    which = 1 - side if turn == 0 else side
    rows = pl.ds(pl.multiple_of(which * half, half), half)
    width = att[0].shape[1]
    copy = pltpu.make_async_copy(res_hbm.at[rows, :], res, sem)
    copy.start()
    rows_in = jnp.concatenate([piece[...] for piece in att], axis=1)
    clip = clip_ref[rows, :][:, :1]
    tiles = [slice(start, start + 512) for start in range(0, D, 512)]
    for columns in tiles:
        projected = jnp.dot(rows_in, w_out[:, columns], preferred_element_type=F32)
        mixed[:, columns] = chosen(mod, 0, clip, columns) * projected
    copy.wait()
    held = mixed[...] + res[...].astype(F32)
    mixed[...] = held
    centre = held - jnp.mean(held, axis=1, keepdims=True)
    spread = lax.rsqrt(jnp.mean(centre * centre, axis=1, keepdims=True) + 1e-06)
    for columns in tiles:
        stretch, shift = chosen(mod, 2, clip, columns), chosen(mod, 1, clip, columns)
        normed[:, columns] = (centre[:, columns] * spread * (1.0 + stretch) + shift).astype(BF16)
    for columns in tiles:
        raised = jnp.dot(normed[...], up[:, columns], preferred_element_type=F32)
        hidden[:, columns] = jax.nn.gelu(raised, approximate=True).astype(BF16)
    if turn == 0:
        for columns in tiles:
            lowered = jnp.dot(hidden[...], down[:, columns], preferred_element_type=F32)
            out[:, columns] = (chosen(mod, 3, clip, columns) * lowered).astype(BF16)
        own = pl.ds(pl.multiple_of(blk * width, width), width)
        lowered = jnp.dot(hidden[...], down[:, own], preferred_element_type=F32)
        out[:, own] = (chosen(mod, 3, clip, own) * lowered + mixed[:, own]).astype(BF16)


def feed(turn, att, w_out, w_up, w_down, residual, mod, clip_wide):
    half, width = att[0].shape
    inner = [pltpu.VMEM((half, D), BF16), pltpu.VMEM((half, D), BF16), pltpu.SemaphoreType.DMA]
    if turn == 0:
        out_shape = shape_of((half, D))
        inner = [pltpu.VMEM((half, D), F32), pltpu.VMEM((half, D), BF16)] + inner
    else:
        out_shape = [shape_of((half, D)), shape_of((half, D), F32)]
    return pl.pallas_call(
        functools.partial(feed_kernel, turn),
        out_shape=out_shape,
        in_specs=[VMEM] * 7 + [ANY] + [VMEM] * 2,
        out_specs=VMEM if turn == 0 else [VMEM] * 2,
        scratch_shapes=inner,
        compiler_params=params(24),
        cost_estimate=cost(2**36, 2**24),
        name="feed",
    )(*att, kept(w_out), kept(w_up), kept(w_down), afar(residual), mod, clip_wide)


def guide_kernel(hidden, mixed, down, other_ref, clip_ref, mod, scale_ref, own, *sent):
    side, blk = lax.axis_index("cfg"), lax.axis_index("blk")
    half, width = own.shape
    clip = clip_ref[pl.ds(pl.multiple_of(side * half, half), half), :][:, :1]
    strength = jnp.zeros((half, 1), F32)
    for index in range(CLIPS):
        strength = jnp.where(clip == index, scale_ref[index], strength)
    lean = jnp.where(side == 0, strength, 1.0 - strength)
    for step, out in enumerate((own, *sent)):
        target = jnp.bitwise_xor(blk, step)
        columns = pl.ds(pl.multiple_of(target * width, width), width)
        lowered = jnp.dot(hidden[...], down[:, columns], preferred_element_type=F32)
        mine = chosen(mod, 3, clip, columns) * lowered
        if step == 0:
            mine = mine + mixed[:, columns]
        other = other_ref[:, columns].astype(F32)
        out[...] = (other + lean * (mine - other)).astype(out.dtype)


def place_kernel(own, got1, got2, got3, placing, *outs):
    guided = own[...] + got1[...].astype(F32) + got2[...].astype(F32) + got3[...].astype(F32)
    placed = jnp.dot(placing[...], guided.astype(BF16), preferred_element_type=F32).astype(BF16)
    if len(outs) == 1:
        outs[0][...] = placed
    else:
        count = outs[0].shape[0]
        for index, out in enumerate(outs):
            out[...] = placed[index * count : (index + 1) * count, :]


def arrange_kernel(*refs):
    out = refs[4]
    place = lax.axis_index("seq")
    count = refs[0].shape[0]
    for step, source in zip(STEPS, refs):
        origin = jnp.bitwise_xor(place, step)
        out[pl.ds(pl.multiple_of(origin * count, count), count), :] = source[...]


def exchanged(value, axis, mask):
    pairs = [(index, index ^ mask) for index in range(lax.axis_size(axis))]
    return lax.ppermute(value, axis, pairs)


def shards(
    queries, keys, values, residual, w_out, w_up, w_down, modulation, guide_scale, slot_clip, owner
):
    slots, width = queries.shape[1:]
    half = slots // 2
    seq_count = lax.axis_size("seq")
    capacity = max(2, slots // seq_count)
    side, place = lax.axis_index("cfg"), lax.axis_index("seq")

    clip_wide = jnp.broadcast_to(slot_clip[:, None], (slots, 128))
    clip_half = lax.dynamic_slice_in_dim(slot_clip, side * half, half, 0)
    owner_half = lax.dynamic_slice_in_dim(owner[:, 0], side * half, half, 0)
    order = jnp.arange(half, dtype=jnp.int32)
    before = (owner_half[None, :] == owner_half[:, None]) & (order[None, :] < order[:, None])
    rank = jnp.sum(before.astype(jnp.int32), axis=1)
    if seq_count == 4:
        lane = jnp.bitwise_xor(owner_half, place)
    else:
        lane = owner_half
    target = jnp.where(clip_half < CLIPS, lane * capacity + rank, -1)
    placing = (
        jnp.arange(seq_count * capacity, dtype=jnp.int32)[:, None] == target[None, :]
    ).astype(BF16)

    near, w_half = fetch_near(w_out)
    if seq_count == 4:
        (up, down), attended = attention_by_head(
            queries[0],
            keys[0],
            values[0],
            slot_clip,
            (clip_wide, placing, w_half),
            (w_up, w_down),
        )
    else:
        attended = attention_by_rows(queries[0], keys[0], values[0], slot_clip)
        up, down = load(w_up, w_down, attended[0])

    whole = fetch_rest(w_out, near, w_half, attended[0])
    parts = []
    for turn in range(2):
        piece = attended[turn]
        gathered = [piece] + [exchanged(piece, "blk", mask) for mask in (1, 2, 3)]
        parts.append(feed(turn, gathered, whole, up, down, residual[0], modulation, clip_wide))
    other = exchanged(parts[0], "cfg", 1)
    own, *sent = pl.pallas_call(
        guide_kernel,
        out_shape=[shape_of((half, width), F32)] + [shape_of((half, width))] * 3,
        in_specs=[VMEM] * 6 + [pl.BlockSpec(memory_space=pltpu.SMEM)],
        out_specs=[VMEM] * 4,
        compiler_params=params(16),
        name="guide",
    )(*parts[1], kept(down), other, clip_wide, modulation, guide_scale)
    got = [exchanged(piece, "blk", mask) for mask, piece in zip((1, 2, 3), sent)]
    by_step = seq_count == 4
    placed = pl.pallas_call(
        place_kernel,
        out_shape=[shape_of((capacity, width))] * 4
        if by_step
        else [shape_of((seq_count * capacity, width))],
        in_specs=[VMEM] * 5,
        out_specs=[VMEM] * (4 if by_step else 1),
        compiler_params=params(16),
        name="place",
    )(own, *got, placing)
    if not by_step:
        arrived = lax.all_to_all(
            placed[0].reshape(seq_count, capacity, width), "seq", split_axis=0, concat_axis=0,
            tiled=True,
        )
        return arrived.reshape(1, seq_count * capacity, width)
    home = [
        exchanged(placed[step], "seq", step) for step in STEPS[1:]
    ]
    arranged = pl.pallas_call(
        arrange_kernel,
        out_shape=shape_of((4 * capacity, width)),
        in_specs=[VMEM] * 4,
        out_specs=VMEM,
        compiler_params=params(16),
        name="arrange",
    )(placed[0], *home)
    return arranged[None]


def solution(mesh):
    placed = (
        P("cfg", "seq", "blk"),
        P("cfg", "seq", "blk"),
        P("cfg", "seq", "blk"),
        P("cfg", "seq", None),
        P("blk", None),
        P(None, "blk"),
        P("blk", None),
        P(),
        P(),
        P("seq"),
        P("seq", None),
    )
    return jax.shard_map(
        shards, mesh=mesh, in_specs=placed, out_specs=P("cfg", "seq", "blk"), check_vma=False
    )
```

```python
import functools
import math

import jax
import jax.numpy as jnp
from jax import lax
from jax.experimental import pallas as pl
from jax.experimental.pallas import tpu as pltpu
from jax.sharding import PartitionSpec as P

D = 1536
HEAD_DIM = 128
CLIPS = 3
NEG_FILL = -1e30
FAR = 2.0**100
VMEM = pl.BlockSpec(memory_space=pltpu.VMEM)
ANY = pl.BlockSpec(memory_space=pl.ANY)
F32 = jnp.float32
BF16 = jnp.bfloat16


def shape_of(extent, dtype=BF16):
    return jax.ShapeDtypeStruct(extent, dtype)


def params(mib):
    return pltpu.CompilerParams(vmem_limit_bytes=mib * 2**20)


def cost(flops, moved):
    return pl.CostEstimate(flops=flops, bytes_accessed=moved, transcendentals=0)


STEPS = (0, 2, 3, 1)


def head_at(side, place):
    return jnp.where(side == 0, place, 3 - place)


def works(side, place):
    return place < 3 if side == 0 else place >= 1


def hop(value, step, back=False):
    pairs = []
    for side in range(2):
        for place in range(4):
            target = place ^ step
            if works(side, target):
                pair = (side * 4 + place, side * 4 + target)
                pairs.append(pair[::-1] if back else pair)
    return lax.ppermute(value, ("cfg", "seq"), pairs)


def pack_kernel(q_ref, k_ref, v_ref, clip_ref, *refs):
    outs, clips, sems = refs[:4], refs[4], refs[5]
    side, place = lax.axis_index("cfg"), lax.axis_index("seq")
    slots = q_ref.shape[0]
    clip_copy = pltpu.make_async_copy(clip_ref, clips, sems.at[12])
    clip_copy.start()
    copies = []
    for step, out in zip(STEPS, outs):
        head = jnp.clip(head_at(side, jnp.bitwise_xor(place, step)), 0, 2)
        columns = pl.ds(pl.multiple_of(head * HEAD_DIM, HEAD_DIM), HEAD_DIM)
        for part, source in enumerate((q_ref, k_ref, v_ref)):
            target = out.at[part * slots : (part + 1) * slots, :]
            copy = pltpu.make_async_copy(source.at[:, columns], target, sems.at[len(copies)])
            copy.start()
            copies.append(copy)
    clip_copy.wait()
    rows = clips[...].astype(F32).astype(BF16)
    for out in outs:
        out[3 * slots :, :] = jnp.zeros((16, 128), BF16)
        out[3 * slots : 3 * slots + rows.shape[0], :] = rows
    for copy in copies:
        copy.wait()


def attend_kernel(*refs):
    blocks, outs, (q_aug, k_aug, v_aug, clips) = refs[:4], refs[-8:-4], refs[-4:]
    slots = outs[0].shape[0]
    lane = lax.broadcasted_iota(jnp.int32, (128, 128), 1)
    row = lax.broadcasted_iota(jnp.int32, (128, 128), 0)
    eye = (lane == row).astype(BF16)
    for index, block in enumerate(blocks):
        base = index * slots
        here = slice(base, base + slots)
        q_aug[here, :128] = block[:slots, :]
        k_aug[here, :128] = block[slots : 2 * slots, :]
        v_aug[here, :128] = block[2 * slots : 3 * slots, :]
        turned = lax.dot_general(
            eye, block[3 * slots :, :], (((1,), (1,)), ((), ())), preferred_element_type=F32
        )
        for group in range(slots // 128):
            part = slice(base + group * 128, base + (group + 1) * 128)
            clip = jnp.broadcast_to(turned[:, group : group + 1], (128, 128)).astype(jnp.int32)
            clips[part, :] = clip
            same = lane == clip
            kept = same & (clip < CLIPS)
            k_aug[part, 128:] = same.astype(BF16)
            q_aug[part, 128:] = jnp.where(kept | (lane > CLIPS), 0.0, -FAR).astype(BF16)
            v_aug[part, 128:] = (lane == 0).astype(BF16)
    scale = math.log2(math.e) / math.sqrt(HEAD_DIM)
    rows = 384

    def score(first):
        return lax.dot_general(
            q_aug[first : first + rows, :],
            k_aug[...],
            (((1,), (1,)), ((), ())),
            preferred_element_type=F32,
        )

    firsts = range(0, 4 * slots, rows)
    ahead = score(0)
    for first in firsts:
        scores = ahead
        if first + rows < 4 * slots:
            ahead = score(first + rows)
        peak = jnp.max(scores, axis=1, keepdims=True)
        probs = jnp.exp2((scores - peak) * scale).astype(BF16)
        summed = jnp.dot(probs, v_aug[...], preferred_element_type=F32)
        result = summed[:, :128] / summed[:, 128:129]
        result = jnp.where(clips[first : first + rows, :] < CLIPS, result, 0.0).astype(BF16)
        outs[first // slots][first % slots : first % slots + rows, :] = result


def regroup_kernel(own, back1, back2, back3, first, second):
    side, place = lax.axis_index("cfg"), lax.axis_index("seq")
    half = first.shape[0]
    for head in range(3):
        home = jnp.where(side == 0, head, 3 - head)
        step = jnp.bitwise_xor(home, place)
        columns = slice(head * HEAD_DIM, (head + 1) * HEAD_DIM)
        for index, source in zip(STEPS, (own, back1, back2, back3)):

            @pl.when(step == index)
            def _():
                for out, which in ((first, 1 - side), (second, side)):
                    rows = pl.ds(pl.multiple_of(which * half, half), half)
                    out[:, columns] = source[rows, :]


def kept(value):
    return pltpu.with_memory_space_constraint(value, pltpu.VMEM)


def afar(value):
    return pltpu.with_memory_space_constraint(value, pltpu.HBM)


def load_kernel(*refs):
    outs, sems = refs[4:7], refs[7]
    copies = [
        pltpu.make_async_copy(refs[index], out, sems.at[index]) for index, out in enumerate(outs)
    ]
    for copy in copies:
        copy.start()
    for copy in copies:
        copy.wait()


def load(arrays, after):
    return pl.pallas_call(
        load_kernel,
        out_shape=[pltpu.VMEM(array.shape, BF16) for array in arrays],
        in_specs=[ANY] * 4,
        out_specs=[VMEM] * 3,
        scratch_shapes=[pltpu.SemaphoreType.DMA((3,))],
        compiler_params=params(16),
        name="load",
    )(*(afar(array) for array in arrays), after)


def across(value, masks):
    pairs = [
        (side * 4 + blk, side * 4 + (blk ^ masks[side])) for side in range(2) for blk in range(4)
    ]
    return lax.ppermute(value, ("cfg", "blk"), pairs)


def cut_kernel(got, out, sem):
    part = out.shape[0]
    offset = pl.multiple_of((1 - lax.axis_index("cfg")) * part, part)
    copy = pltpu.make_async_copy(got.at[pl.ds(offset, part), :], out, sem)
    copy.start()
    copy.wait()


def join_kernel(own, near, near_swap, far, far_swap, after, out, sems):
    side = lax.axis_index("cfg")
    width, part = own.shape[0], far.shape[0]
    plan = (
        (own, 0, width),
        (near, (1 + side) * width, width),
        (near_swap, (2 - side) * width, width),
        (far, 3 * width + (1 - side) * part, part),
        (far_swap, 3 * width + side * part, part),
    )
    copies = []
    for index, (source, offset, rows) in enumerate(plan):
        target = out.at[pl.ds(pl.multiple_of(offset, part), rows), :]
        copy = pltpu.make_async_copy(source, target, sems.at[index])
        copy.start()
        copies.append(copy)
    for copy in copies:
        copy.wait()


def gate_kernel(value, after, out):
    pass


def gate(value, after):
    return pl.pallas_call(
        gate_kernel,
        out_shape=shape_of(value.shape, value.dtype),
        in_specs=[ANY] * 2,
        out_specs=ANY,
        input_output_aliases={0: 0},
        compiler_params=params(1),
        name="gate",
    )(value, after)


def fetch_near(w_out):
    near = across(w_out, (1, 2))
    half = pl.pallas_call(
        cut_kernel,
        out_shape=shape_of((w_out.shape[0] // 2, D)),
        in_specs=[ANY],
        out_specs=ANY,
        scratch_shapes=[pltpu.SemaphoreType.DMA],
        compiler_params=params(16),
        name="cut",
    )(near)
    return near, half


def fetch_rest(w_out, near, half, after):
    far = across(half, (2, 1))
    far = gate(far, after)
    pieces = (afar(w_out), near, exchanged(near, "cfg", 1), far, exchanged(far, "cfg", 1))
    return pl.pallas_call(
        join_kernel,
        out_shape=pltpu.VMEM((D, D), BF16),
        in_specs=[ANY] * 6,
        out_specs=VMEM,
        scratch_shapes=[pltpu.SemaphoreType.DMA((5,))],
        compiler_params=params(16),
        name="join",
    )(*pieces, after)


def attention_by_head(query, key, value, slot_clip, early, weights):
    slots = query.shape[0]
    packed = pl.pallas_call(
        pack_kernel,
        out_shape=[shape_of((3 * slots + 16, 128))] * 4,
        in_specs=[ANY] * 4,
        out_specs=[VMEM] * 4,
        scratch_shapes=[
            pltpu.VMEM((slots // 128, 128), jnp.int32),
            pltpu.SemaphoreType.DMA((13,)),
        ],
        compiler_params=params(16),
        name="pack",
    )(afar(query), afar(key), afar(value), afar(slot_clip.reshape(slots // 128, 128)))
    blocks = [packed[0]] + [hop(packed[index], STEPS[index]) for index in (1, 2, 3)]
    early = (*early, *(kept(weight) for weight in load(weights, packed[0])))
    results = pl.pallas_call(
        attend_kernel,
        out_shape=[shape_of((slots, 128))] * 4,
        in_specs=[VMEM] * 4 + [ANY] * (len(early) - 3) + [VMEM] * 3,
        out_specs=[VMEM] * 4,
        scratch_shapes=[pltpu.VMEM((4 * slots, 256), BF16)] * 3
        + [pltpu.VMEM((4 * slots, 128), jnp.int32)],
        compiler_params=params(28),
        cost_estimate=cost(2**32, 2**21),
        name="attend",
    )(*blocks, *early)
    backs = [hop(results[index], STEPS[index], back=True) for index in (1, 2, 3)]
    half = slots // 2
    return early[-3:], pl.pallas_call(
        regroup_kernel,
        out_shape=[shape_of((half, 3 * HEAD_DIM))] * 2,
        in_specs=[VMEM] * 4,
        out_specs=[VMEM] * 2,
        compiler_params=params(16),
        name="regroup",
    )(results[0], *backs)


def attention_by_rows(query, key, value, slot_clip):
    slots, width = query.shape
    heads = width // HEAD_DIM
    live = slot_clip < CLIPS
    factor = 1.0 / math.sqrt(HEAD_DIM)
    query_heads = query.reshape(slots, heads, HEAD_DIM)

    def absorb(carry, piece):
        key_piece, value_piece, clip_piece = piece
        best, total, accum = carry
        kept = (clip_piece[None, :] == slot_clip[:, None]) & live[:, None]
        scores = jnp.einsum("qhd,khd->hqk", query_heads, key_piece, preferred_element_type=F32)
        scores = jnp.where(kept[None], scores * factor, NEG_FILL)
        new_best = jnp.maximum(best, jnp.max(scores, axis=-1))
        fade = jnp.exp(best - new_best)
        probs = jnp.exp(scores - new_best[..., None])
        total = total * fade + jnp.sum(probs, axis=-1)
        added = jnp.einsum(
            "hqk,khd->qhd", probs.astype(BF16), value_piece, preferred_element_type=F32
        )
        accum = accum * jnp.transpose(fade)[:, :, None] + added
        return (new_best, total, accum), None

    start = (
        jnp.full((heads, slots), NEG_FILL, F32),
        jnp.zeros((heads, slots), F32),
        jnp.zeros((slots, heads, HEAD_DIM), F32),
    )
    pieces = (
        lax.all_gather(key, "seq").reshape(-1, slots, heads, HEAD_DIM),
        lax.all_gather(value, "seq").reshape(-1, slots, heads, HEAD_DIM),
        lax.all_gather(slot_clip, "seq"),
    )
    (best, total, accum), _ = lax.scan(absorb, start, pieces)
    attended = (accum / jnp.transpose(total)[:, :, None]).reshape(slots, width)
    attended = jnp.where(live[:, None], attended, 0.0).astype(BF16)
    half = slots // 2
    side = lax.axis_index("cfg")
    return [
        lax.dynamic_slice_in_dim(attended, which * half, half, 0) for which in (1 - side, side)
    ]


def chosen(mod, kind, clip, columns):
    picked = jnp.zeros((clip.shape[0], columns.stop - columns.start), F32)
    for index in range(CLIPS):
        picked = jnp.where(clip == index, mod[index, kind : kind + 1, columns], picked)
    return picked


def lowered_tiles(hidden, mixed, down, mod, clip):
    blk = lax.axis_index("blk")
    width = D // lax.axis_size("blk")
    for start in range(0, D, 2 * width):
        columns = slice(start, start + 2 * width)
        lowered = jnp.dot(hidden[...], down[:, columns], preferred_element_type=F32)
        lowered = chosen(mod, 3, clip, columns) * lowered
        for index in range(2):
            part = slice(start + index * width, start + (index + 1) * width)
            stream = jnp.where(blk == part.start // width, mixed[:, part], 0.0)
            yield part, lowered[:, index * width : (index + 1) * width] + stream


def feed_kernel(turn, *refs):
    att, (w_out, up, down, res, mod, clip_ref), refs = refs[:4], refs[4:10], refs[10:]
    if turn == 0:
        out, mixed, hidden, normed = refs
    else:
        hidden, mixed, normed = refs
    side = lax.axis_index("cfg")
    half = hidden.shape[0]
    which = 1 - side if turn == 0 else side
    rows = pl.ds(pl.multiple_of(which * half, half), half)
    rows_in = jnp.concatenate([piece[...] for piece in att], axis=1)
    clip = clip_ref[rows, :][:, :1]
    tiles = [slice(start, start + 512) for start in range(0, D, 512)]
    for columns in tiles:
        projected = jnp.dot(rows_in, w_out[:, columns], preferred_element_type=F32)
        mixed[:, columns] = (
            res[rows, columns].astype(F32) + chosen(mod, 0, clip, columns) * projected
        )
    held = mixed[...]
    centre = held - jnp.mean(held, axis=1, keepdims=True)
    spread = lax.rsqrt(jnp.mean(centre * centre, axis=1, keepdims=True) + 1e-06)
    for columns in tiles:
        stretch, shift = chosen(mod, 2, clip, columns), chosen(mod, 1, clip, columns)
        normed[:, columns] = (centre[:, columns] * spread * (1.0 + stretch) + shift).astype(BF16)
    for columns in tiles:
        raised = jnp.dot(normed[...], up[:, columns], preferred_element_type=F32)
        hidden[:, columns] = jax.nn.gelu(raised, approximate=True).astype(BF16)
    if turn == 0:
        for columns, terms in lowered_tiles(hidden, mixed, down, mod, clip):
            out[:, columns] = terms.astype(BF16)


def feed(turn, att, w_out, w_up, w_down, residual, mod, clip_wide):
    half, width = att[0].shape
    inner = [pltpu.VMEM((half, D), BF16)]
    if turn == 0:
        out_shape = shape_of((half, D))
        inner = [pltpu.VMEM((half, D), F32), pltpu.VMEM((half, D), BF16)] + inner
    else:
        out_shape = [shape_of((half, D)), shape_of((half, D), F32)]
    return pl.pallas_call(
        functools.partial(feed_kernel, turn),
        out_shape=out_shape,
        in_specs=[VMEM] * 10,
        out_specs=VMEM if turn == 0 else [VMEM] * 2,
        scratch_shapes=inner,
        compiler_params=params(24),
        cost_estimate=cost(2**36, 2**24),
        name="feed",
    )(*att, kept(w_out), kept(w_up), kept(w_down), kept(residual), mod, clip_wide)


def guide_kernel(hidden, mixed, down, other_ref, clip_ref, mod, scale_ref, *refs):
    outs, held = refs[:4], refs[4]
    side, blk = lax.axis_index("cfg"), lax.axis_index("blk")
    half, width = outs[0].shape
    clip = clip_ref[pl.ds(pl.multiple_of(side * half, half), half), :][:, :1]
    strength = jnp.zeros((half, 1), F32)
    for index in range(CLIPS):
        strength = jnp.where(clip == index, scale_ref[index], strength)
    lean = jnp.where(side == 0, strength, 1.0 - strength)
    for columns, mine in lowered_tiles(hidden, mixed, down, mod, clip):
        other = other_ref[:, columns].astype(F32)
        held[:, columns] = other + lean * (mine - other)
    for step, out in enumerate(outs):
        target = jnp.bitwise_xor(blk, step)
        columns = pl.ds(pl.multiple_of(target * width, width), width)
        out[...] = held[:, columns].astype(out.dtype)


def place_kernel(own, got1, got2, got3, placing, *outs):
    guided = own[...] + got1[...].astype(F32) + got2[...].astype(F32) + got3[...].astype(F32)
    placed = jnp.dot(placing[...], guided.astype(BF16), preferred_element_type=F32).astype(BF16)
    if len(outs) == 1:
        outs[0][...] = placed
    else:
        count = outs[0].shape[0]
        for index, out in enumerate(outs):
            out[...] = placed[index * count : (index + 1) * count, :]


def arrange_kernel(*refs):
    out = refs[4]
    place = lax.axis_index("seq")
    count = refs[0].shape[0]
    for step, source in zip(STEPS, refs):
        origin = jnp.bitwise_xor(place, step)
        out[pl.ds(pl.multiple_of(origin * count, count), count), :] = source[...]


def exchanged(value, axis, mask):
    pairs = [(index, index ^ mask) for index in range(lax.axis_size(axis))]
    return lax.ppermute(value, axis, pairs)


def shards(
    queries, keys, values, residual, w_out, w_up, w_down, modulation, guide_scale, slot_clip, owner
):
    slots, width = queries.shape[1:]
    half = slots // 2
    seq_count = lax.axis_size("seq")
    capacity = max(2, slots // seq_count)
    side, place = lax.axis_index("cfg"), lax.axis_index("seq")

    clip_wide = jnp.broadcast_to(slot_clip[:, None], (slots, 128))
    clip_half = lax.dynamic_slice_in_dim(slot_clip, side * half, half, 0)
    owner_half = lax.dynamic_slice_in_dim(owner[:, 0], side * half, half, 0)
    order = jnp.arange(half, dtype=jnp.int32)
    before = (owner_half[None, :] == owner_half[:, None]) & (order[None, :] < order[:, None])
    rank = jnp.sum(before.astype(jnp.int32), axis=1)
    if seq_count == 4:
        lane = jnp.bitwise_xor(owner_half, place)
    else:
        lane = owner_half
    target = jnp.where(clip_half < CLIPS, lane * capacity + rank, -1)
    placing = (
        jnp.arange(seq_count * capacity, dtype=jnp.int32)[:, None] == target[None, :]
    ).astype(BF16)

    near, w_half = fetch_near(w_out)
    if seq_count == 4:
        (up, down, stream), attended = attention_by_head(
            queries[0],
            keys[0],
            values[0],
            slot_clip,
            (clip_wide, placing, w_half),
            (w_up, w_down, residual[0]),
        )
    else:
        attended = attention_by_rows(queries[0], keys[0], values[0], slot_clip)
        up, down, stream = load((w_up, w_down, residual[0]), attended[0])

    whole = fetch_rest(w_out, near, w_half, attended[0])
    parts = []
    for turn in range(2):
        piece = attended[turn]
        gathered = [piece] + [exchanged(piece, "blk", mask) for mask in (1, 2, 3)]
        parts.append(feed(turn, gathered, whole, up, down, stream, modulation, clip_wide))
    other = exchanged(parts[0], "cfg", 1)
    own, *sent = pl.pallas_call(
        guide_kernel,
        out_shape=[shape_of((half, width), F32)] + [shape_of((half, width))] * 3,
        in_specs=[VMEM] * 6 + [pl.BlockSpec(memory_space=pltpu.SMEM)],
        out_specs=[VMEM] * 4,
        scratch_shapes=[pltpu.VMEM((half, D), F32)],
        compiler_params=params(16),
        name="guide",
    )(*parts[1], kept(down), other, clip_wide, modulation, guide_scale)
    got = [exchanged(piece, "blk", mask) for mask, piece in zip((1, 2, 3), sent)]
    by_step = seq_count == 4
    placed = pl.pallas_call(
        place_kernel,
        out_shape=[shape_of((capacity, width))] * 4
        if by_step
        else [shape_of((seq_count * capacity, width))],
        in_specs=[VMEM] * 5,
        out_specs=[VMEM] * (4 if by_step else 1),
        compiler_params=params(16),
        name="place",
    )(own, *got, placing)
    if not by_step:
        arrived = lax.all_to_all(
            placed[0].reshape(seq_count, capacity, width), "seq", split_axis=0, concat_axis=0,
            tiled=True,
        )
        return arrived.reshape(1, seq_count * capacity, width)
    home = [
        exchanged(placed[step], "seq", step) for step in STEPS[1:]
    ]
    arranged = pl.pallas_call(
        arrange_kernel,
        out_shape=shape_of((4 * capacity, width)),
        in_specs=[VMEM] * 4,
        out_specs=VMEM,
        compiler_params=params(16),
        name="arrange",
    )(placed[0], *home)
    return arranged[None]


def solution(mesh):
    placed = (
        P("cfg", "seq", "blk"),
        P("cfg", "seq", "blk"),
        P("cfg", "seq", "blk"),
        P("cfg", "seq", None),
        P("blk", None),
        P(None, "blk"),
        P("blk", None),
        P(),
        P(),
        P("seq"),
        P("seq", None),
    )
    return jax.shard_map(
        shards, mesh=mesh, in_specs=placed, out_specs=P("cfg", "seq", "blk"), check_vma=False
    )
```

```python
import functools
import math

import jax
import jax.numpy as jnp
from jax import lax
from jax.experimental import pallas as pl
from jax.experimental.pallas import tpu as pltpu
from jax.sharding import PartitionSpec as P

D = 1536
HEAD_DIM = 128
CLIPS = 3
NEG_FILL = -1e30
FAR = 2.0**100
VMEM = pl.BlockSpec(memory_space=pltpu.VMEM)
ANY = pl.BlockSpec(memory_space=pl.ANY)
F32 = jnp.float32
BF16 = jnp.bfloat16


def shape_of(extent, dtype=BF16):
    return jax.ShapeDtypeStruct(extent, dtype)


def params(mib):
    return pltpu.CompilerParams(vmem_limit_bytes=mib * 2**20)


def cost(flops, moved):
    return pl.CostEstimate(flops=flops, bytes_accessed=moved, transcendentals=0)


STEPS = (0, 2, 3, 1)


def head_at(side, place):
    return jnp.where(side == 0, place, 3 - place)


def works(side, place):
    return place < 3 if side == 0 else place >= 1


def hop(value, step, back=False):
    pairs = []
    for side in range(2):
        for place in range(4):
            target = place ^ step
            if works(side, target):
                pair = (side * 4 + place, side * 4 + target)
                pairs.append(pair[::-1] if back else pair)
    return lax.ppermute(value, ("cfg", "seq"), pairs)


def pack_kernel(q_ref, k_ref, v_ref, clip_ref, *refs):
    outs, clips, sems = refs[:4], refs[4], refs[5]
    side, place = lax.axis_index("cfg"), lax.axis_index("seq")
    slots = q_ref.shape[0]
    clip_copy = pltpu.make_async_copy(clip_ref, clips, sems.at[12])
    clip_copy.start()
    copies = []
    for step, out in zip(STEPS, outs):
        head = jnp.clip(head_at(side, jnp.bitwise_xor(place, step)), 0, 2)
        columns = pl.ds(pl.multiple_of(head * HEAD_DIM, HEAD_DIM), HEAD_DIM)
        for part, source in enumerate((q_ref, k_ref, v_ref)):
            target = out.at[part * slots : (part + 1) * slots, :]
            copy = pltpu.make_async_copy(source.at[:, columns], target, sems.at[len(copies)])
            copy.start()
            copies.append(copy)
    clip_copy.wait()
    rows = clips[...].astype(F32).astype(BF16)
    for out in outs:
        out[3 * slots :, :] = jnp.zeros((16, 128), BF16)
        out[3 * slots : 3 * slots + rows.shape[0], :] = rows
    for copy in copies:
        copy.wait()


def attend_kernel(*refs):
    blocks, outs, (q_aug, k_aug, v_aug, wide, found) = refs[:4], refs[-9:-5], refs[-5:]
    slots = outs[0].shape[0]
    count = slots // CLIPS
    group = 4 * count
    lane = lax.broadcasted_iota(jnp.int32, (count, 128), 1)
    row = lax.broadcasted_iota(jnp.int32, (count, 128), 0)
    q_tail = jnp.where(lane == 0, -FAR, 0.0).astype(BF16)
    v_tail = (lane == 0).astype(BF16)
    fills, bases = [], []
    for index, block in enumerate(blocks):
        numbers = block[3 * slots :, :].astype(F32)
        line = lax.broadcasted_iota(jnp.int32, numbers.shape, 0)
        spot = lax.broadcasted_iota(jnp.int32, numbers.shape, 1)
        live = (line < slots // 128) & (numbers < CLIPS - 0.5)
        filled = jnp.sum(live.astype(F32)).astype(jnp.int32)
        first = jnp.sum(jnp.where((line == 0) & (spot == 0), numbers, 0.0)).astype(jnp.int32)
        fills.append(filled)
        wide[index, :, :] = block[: 3 * slots, :].astype(F32)
        for turn in range(CLIPS):
            clip = lax.rem(first + turn, CLIPS)
            base = pl.multiple_of((clip * 4 + index) * count, count)
            bases.append(base)
            here = pl.ds(base, count)
            for part, target in enumerate((q_aug, k_aug, v_aug)):
                rows = pl.ds(part * slots + turn, count, stride=CLIPS)
                target[here, :128] = wide[index, rows, :].astype(BF16)
            padding = (lane == 0) & (CLIPS * row + turn >= filled)
            q_aug[here, 128:] = q_tail
            k_aug[here, 128:] = padding.astype(BF16)
            v_aug[here, 128:] = v_tail
    scale = math.log2(math.e) / math.sqrt(HEAD_DIM)

    def score(clip):
        here = slice(clip * group, (clip + 1) * group)
        return lax.dot_general(
            q_aug[here, :], k_aug[here, :], (((1,), (1,)), ((), ())), preferred_element_type=F32
        )

    ahead = score(0)
    for clip in range(CLIPS):
        scores = ahead
        if clip + 1 < CLIPS:
            ahead = score(clip + 1)
        here = slice(clip * group, (clip + 1) * group)
        peak = jnp.max(scores, axis=1, keepdims=True)
        probs = jnp.exp2((scores - peak) * scale).astype(BF16)
        summed = jnp.dot(probs, v_aug[here, :], preferred_element_type=F32)
        found[here, :] = summed[:, :128] / summed[:, 128:129]
    line = lax.broadcasted_iota(jnp.int32, (slots, 128), 0)
    for index, out in enumerate(outs):
        for turn in range(CLIPS):
            base = bases[index * CLIPS + turn]
            wide[index, pl.ds(turn, count, stride=CLIPS), :] = found[pl.ds(base, count), :]
        out[...] = jnp.where(line < fills[index], wide[index, :slots, :], 0.0).astype(BF16)


def regroup_kernel(own, back1, back2, back3, first, second):
    side, place = lax.axis_index("cfg"), lax.axis_index("seq")
    half = first.shape[0]
    for head in range(3):
        home = jnp.where(side == 0, head, 3 - head)
        step = jnp.bitwise_xor(home, place)
        columns = slice(head * HEAD_DIM, (head + 1) * HEAD_DIM)
        for index, source in zip(STEPS, (own, back1, back2, back3)):

            @pl.when(step == index)
            def _():
                for out, which in ((first, 1 - side), (second, side)):
                    rows = pl.ds(pl.multiple_of(which * half, half), half)
                    out[:, columns] = source[rows, :]


def kept(value):
    return pltpu.with_memory_space_constraint(value, pltpu.VMEM)


def afar(value):
    return pltpu.with_memory_space_constraint(value, pltpu.HBM)


def load_kernel(*refs):
    outs, sems = refs[4:7], refs[7]
    copies = [
        pltpu.make_async_copy(refs[index], out, sems.at[index]) for index, out in enumerate(outs)
    ]
    for copy in copies:
        copy.start()
    for copy in copies:
        copy.wait()


def load(arrays, after):
    return pl.pallas_call(
        load_kernel,
        out_shape=[pltpu.VMEM(array.shape, BF16) for array in arrays],
        in_specs=[ANY] * 4,
        out_specs=[VMEM] * 3,
        scratch_shapes=[pltpu.SemaphoreType.DMA((3,))],
        compiler_params=params(16),
        cost_estimate=cost(2**34, 2**24),
        name="load",
    )(*(afar(array) for array in arrays), after)


def across(value, masks):
    pairs = [
        (side * 4 + blk, side * 4 + (blk ^ masks[side])) for side in range(2) for blk in range(4)
    ]
    return lax.ppermute(value, ("cfg", "blk"), pairs)


def cut_kernel(got, out, sem):
    part = out.shape[0]
    offset = pl.multiple_of((1 - lax.axis_index("cfg")) * part, part)
    copy = pltpu.make_async_copy(got.at[pl.ds(offset, part), :], out, sem)
    copy.start()
    copy.wait()


def join_kernel(own, near, near_swap, far, far_swap, after, out, sems):
    side = lax.axis_index("cfg")
    width, part = own.shape[0], far.shape[0]
    plan = (
        (own, 0, width),
        (near, (1 + side) * width, width),
        (near_swap, (2 - side) * width, width),
        (far, 3 * width + (1 - side) * part, part),
        (far_swap, 3 * width + side * part, part),
    )
    copies = []
    for index, (source, offset, rows) in enumerate(plan):
        target = out.at[pl.ds(pl.multiple_of(offset, part), rows), :]
        copy = pltpu.make_async_copy(source, target, sems.at[index])
        copy.start()
        copies.append(copy)
    for copy in copies:
        copy.wait()


def gate_kernel(value, after, out):
    pass


def gate(value, after):
    return pl.pallas_call(
        gate_kernel,
        out_shape=shape_of(value.shape, value.dtype),
        in_specs=[ANY] * 2,
        out_specs=ANY,
        input_output_aliases={0: 0},
        compiler_params=params(1),
        name="gate",
    )(value, after)


def fetch_near(w_out):
    near = across(w_out, (1, 2))
    half = pl.pallas_call(
        cut_kernel,
        out_shape=shape_of((w_out.shape[0] // 2, D)),
        in_specs=[ANY],
        out_specs=ANY,
        scratch_shapes=[pltpu.SemaphoreType.DMA],
        compiler_params=params(16),
        name="cut",
    )(near)
    return near, half


def fetch_rest(w_out, near, half, after):
    far = across(half, (2, 1))
    far = gate(far, after)
    pieces = (afar(w_out), near, exchanged(near, "cfg", 1), far, exchanged(far, "cfg", 1))
    return pl.pallas_call(
        join_kernel,
        out_shape=pltpu.VMEM((D, D), BF16),
        in_specs=[ANY] * 6,
        out_specs=VMEM,
        scratch_shapes=[pltpu.SemaphoreType.DMA((5,))],
        compiler_params=params(16),
        name="join",
    )(*pieces, after)


def attention_by_head(query, key, value, slot_clip, early, weights):
    slots = query.shape[0]
    packed = pl.pallas_call(
        pack_kernel,
        out_shape=[shape_of((3 * slots + 16, 128))] * 4,
        in_specs=[ANY] * 4,
        out_specs=[VMEM] * 4,
        scratch_shapes=[
            pltpu.VMEM((slots // 128, 128), jnp.int32),
            pltpu.SemaphoreType.DMA((13,)),
        ],
        compiler_params=params(16),
        name="pack",
    )(afar(query), afar(key), afar(value), afar(slot_clip.reshape(slots // 128, 128)))
    blocks = [packed[0]] + [hop(packed[index], STEPS[index]) for index in (1, 2, 3)]
    early = (*early, *(kept(weight) for weight in load(weights, packed[0])))
    results = pl.pallas_call(
        attend_kernel,
        out_shape=[shape_of((slots, 128))] * 4,
        in_specs=[VMEM] * 4 + [ANY] * (len(early) - 3) + [VMEM] * 3,
        out_specs=[VMEM] * 4,
        scratch_shapes=[pltpu.VMEM((4 * slots, 256), BF16)] * 3
        + [pltpu.VMEM((4, 3 * slots, 128), F32), pltpu.VMEM((4 * slots, 128), F32)],
        compiler_params=params(28),
        cost_estimate=cost(2**32, 2**21),
        name="attend",
    )(*blocks, *early)
    backs = [hop(results[index], STEPS[index], back=True) for index in (1, 2, 3)]
    half = slots // 2
    return early[-3:], pl.pallas_call(
        regroup_kernel,
        out_shape=[shape_of((half, 3 * HEAD_DIM))] * 2,
        in_specs=[VMEM] * 4,
        out_specs=[VMEM] * 2,
        compiler_params=params(16),
        name="regroup",
    )(results[0], *backs)


def attention_by_rows(query, key, value, slot_clip):
    slots, width = query.shape
    heads = width // HEAD_DIM
    live = slot_clip < CLIPS
    factor = 1.0 / math.sqrt(HEAD_DIM)
    query_heads = query.reshape(slots, heads, HEAD_DIM)

    def absorb(carry, piece):
        key_piece, value_piece, clip_piece = piece
        best, total, accum = carry
        kept = (clip_piece[None, :] == slot_clip[:, None]) & live[:, None]
        scores = jnp.einsum("qhd,khd->hqk", query_heads, key_piece, preferred_element_type=F32)
        scores = jnp.where(kept[None], scores * factor, NEG_FILL)
        new_best = jnp.maximum(best, jnp.max(scores, axis=-1))
        fade = jnp.exp(best - new_best)
        probs = jnp.exp(scores - new_best[..., None])
        total = total * fade + jnp.sum(probs, axis=-1)
        added = jnp.einsum(
            "hqk,khd->qhd", probs.astype(BF16), value_piece, preferred_element_type=F32
        )
        accum = accum * jnp.transpose(fade)[:, :, None] + added
        return (new_best, total, accum), None

    start = (
        jnp.full((heads, slots), NEG_FILL, F32),
        jnp.zeros((heads, slots), F32),
        jnp.zeros((slots, heads, HEAD_DIM), F32),
    )
    pieces = (
        lax.all_gather(key, "seq").reshape(-1, slots, heads, HEAD_DIM),
        lax.all_gather(value, "seq").reshape(-1, slots, heads, HEAD_DIM),
        lax.all_gather(slot_clip, "seq"),
    )
    (best, total, accum), _ = lax.scan(absorb, start, pieces)
    attended = (accum / jnp.transpose(total)[:, :, None]).reshape(slots, width)
    attended = jnp.where(live[:, None], attended, 0.0).astype(BF16)
    half = slots // 2
    side = lax.axis_index("cfg")
    return [
        lax.dynamic_slice_in_dim(attended, which * half, half, 0) for which in (1 - side, side)
    ]


def chosen(mod, kind, clip, columns):
    picked = jnp.zeros((clip.shape[0], columns.stop - columns.start), F32)
    for index in range(CLIPS):
        picked = jnp.where(clip == index, mod[index, kind : kind + 1, columns], picked)
    return picked


def lowered_tiles(hidden, mixed, down, mod, clip):
    blk = lax.axis_index("blk")
    width = D // lax.axis_size("blk")
    for start in range(0, D, 2 * width):
        columns = slice(start, start + 2 * width)
        lowered = jnp.dot(hidden[...], down[:, columns], preferred_element_type=F32)
        lowered = chosen(mod, 3, clip, columns) * lowered
        for index in range(2):
            part = slice(start + index * width, start + (index + 1) * width)
            stream = jnp.where(blk == part.start // width, mixed[:, part], 0.0)
            yield part, lowered[:, index * width : (index + 1) * width] + stream


def feed_kernel(turn, *refs):
    att, (w_out, up, down, res, mod, clip_ref), refs = refs[:4], refs[4:10], refs[10:]
    if turn == 0:
        out, mixed, hidden, normed = refs
    else:
        hidden, mixed, normed = refs
    side = lax.axis_index("cfg")
    half = hidden.shape[0]
    which = 1 - side if turn == 0 else side
    rows = pl.ds(pl.multiple_of(which * half, half), half)
    rows_in = jnp.concatenate([piece[...] for piece in att], axis=1)
    clip = clip_ref[rows, :][:, :1]
    tiles = [slice(start, start + 512) for start in range(0, D, 512)]
    for columns in tiles:
        projected = jnp.dot(rows_in, w_out[:, columns], preferred_element_type=F32)
        mixed[:, columns] = (
            res[rows, columns].astype(F32) + chosen(mod, 0, clip, columns) * projected
        )
    held = mixed[...]
    centre = held - jnp.mean(held, axis=1, keepdims=True)
    spread = lax.rsqrt(jnp.mean(centre * centre, axis=1, keepdims=True) + 1e-06)
    for columns in tiles:
        stretch, shift = chosen(mod, 2, clip, columns), chosen(mod, 1, clip, columns)
        normed[:, columns] = (centre[:, columns] * spread * (1.0 + stretch) + shift).astype(BF16)
    for columns in tiles:
        raised = jnp.dot(normed[...], up[:, columns], preferred_element_type=F32)
        hidden[:, columns] = jax.nn.gelu(raised, approximate=True).astype(BF16)
    if turn == 0:
        for columns, terms in lowered_tiles(hidden, mixed, down, mod, clip):
            out[:, columns] = terms.astype(BF16)


def feed(turn, att, w_out, w_up, w_down, residual, mod, clip_wide):
    half, width = att[0].shape
    inner = [pltpu.VMEM((half, D), BF16)]
    if turn == 0:
        out_shape = shape_of((half, D))
        inner = [pltpu.VMEM((half, D), F32), pltpu.VMEM((half, D), BF16)] + inner
    else:
        out_shape = [shape_of((half, D)), shape_of((half, D), F32)]
    return pl.pallas_call(
        functools.partial(feed_kernel, turn),
        out_shape=out_shape,
        in_specs=[VMEM] * 10,
        out_specs=VMEM if turn == 0 else [VMEM] * 2,
        scratch_shapes=inner,
        compiler_params=params(24),
        cost_estimate=cost(2**36, 2**24),
        name="feed",
    )(*att, kept(w_out), kept(w_up), kept(w_down), kept(residual), mod, clip_wide)


def guide_kernel(hidden, mixed, down, other_ref, clip_ref, mod, scale_ref, *refs):
    outs, held = refs[:4], refs[4]
    side, blk = lax.axis_index("cfg"), lax.axis_index("blk")
    half, width = outs[0].shape
    clip = clip_ref[pl.ds(pl.multiple_of(side * half, half), half), :][:, :1]
    strength = jnp.zeros((half, 1), F32)
    for index in range(CLIPS):
        strength = jnp.where(clip == index, scale_ref[index], strength)
    lean = jnp.where(side == 0, strength, 1.0 - strength)
    for columns, mine in lowered_tiles(hidden, mixed, down, mod, clip):
        other = other_ref[:, columns].astype(F32)
        held[:, columns] = other + lean * (mine - other)
    for step, out in enumerate(outs):
        target = jnp.bitwise_xor(blk, step)
        columns = pl.ds(pl.multiple_of(target * width, width), width)
        out[...] = held[:, columns].astype(out.dtype)


def place_kernel(own, got1, got2, got3, placing, *outs):
    guided = own[...] + got1[...].astype(F32) + got2[...].astype(F32) + got3[...].astype(F32)
    placed = jnp.dot(placing[...], guided.astype(BF16), preferred_element_type=F32).astype(BF16)
    if len(outs) == 1:
        outs[0][...] = placed
    else:
        count = outs[0].shape[0]
        for index, out in enumerate(outs):
            out[...] = placed[index * count : (index + 1) * count, :]


def arrange_kernel(*refs):
    out = refs[4]
    place = lax.axis_index("seq")
    count = refs[0].shape[0]
    for step, source in zip(STEPS, refs):
        origin = jnp.bitwise_xor(place, step)
        out[pl.ds(pl.multiple_of(origin * count, count), count), :] = source[...]


def exchanged(value, axis, mask):
    pairs = [(index, index ^ mask) for index in range(lax.axis_size(axis))]
    return lax.ppermute(value, axis, pairs)


def shards(
    queries, keys, values, residual, w_out, w_up, w_down, modulation, guide_scale, slot_clip, owner
):
    slots, width = queries.shape[1:]
    half = slots // 2
    seq_count = lax.axis_size("seq")
    capacity = max(2, slots // seq_count)
    side, place = lax.axis_index("cfg"), lax.axis_index("seq")

    clip_wide = jnp.broadcast_to(slot_clip[:, None], (slots, 128))
    clip_half = lax.dynamic_slice_in_dim(slot_clip, side * half, half, 0)
    owner_half = lax.dynamic_slice_in_dim(owner[:, 0], side * half, half, 0)
    order = jnp.arange(half, dtype=jnp.int32)
    before = (owner_half[None, :] == owner_half[:, None]) & (order[None, :] < order[:, None])
    rank = jnp.sum(before.astype(jnp.int32), axis=1)
    if seq_count == 4:
        lane = jnp.bitwise_xor(owner_half, place)
    else:
        lane = owner_half
    target = jnp.where(clip_half < CLIPS, lane * capacity + rank, -1)
    placing = (
        jnp.arange(seq_count * capacity, dtype=jnp.int32)[:, None] == target[None, :]
    ).astype(BF16)

    near, w_half = fetch_near(w_out)
    if seq_count == 4:
        (up, down, stream), attended = attention_by_head(
            queries[0],
            keys[0],
            values[0],
            slot_clip,
            (clip_wide, placing, w_half),
            (w_up, w_down, residual[0]),
        )
    else:
        attended = attention_by_rows(queries[0], keys[0], values[0], slot_clip)
        up, down, stream = load((w_up, w_down, residual[0]), attended[0])

    whole = fetch_rest(w_out, near, w_half, attended[0])
    parts = []
    for turn in range(2):
        piece = attended[turn]
        gathered = [piece] + [exchanged(piece, "blk", mask) for mask in (1, 2, 3)]
        parts.append(feed(turn, gathered, whole, up, down, stream, modulation, clip_wide))
    other = exchanged(parts[0], "cfg", 1)
    own, *sent = pl.pallas_call(
        guide_kernel,
        out_shape=[shape_of((half, width), F32)] + [shape_of((half, width))] * 3,
        in_specs=[VMEM] * 6 + [pl.BlockSpec(memory_space=pltpu.SMEM)],
        out_specs=[VMEM] * 4,
        scratch_shapes=[pltpu.VMEM((half, D), F32)],
        compiler_params=params(16),
        name="guide",
    )(*parts[1], kept(down), other, clip_wide, modulation, guide_scale)
    got = [exchanged(piece, "blk", mask) for mask, piece in zip((1, 2, 3), sent)]
    by_step = seq_count == 4
    placed = pl.pallas_call(
        place_kernel,
        out_shape=[shape_of((capacity, width))] * 4
        if by_step
        else [shape_of((seq_count * capacity, width))],
        in_specs=[VMEM] * 5,
        out_specs=[VMEM] * (4 if by_step else 1),
        compiler_params=params(16),
        name="place",
    )(own, *got, placing)
    if not by_step:
        arrived = lax.all_to_all(
            placed[0].reshape(seq_count, capacity, width), "seq", split_axis=0, concat_axis=0,
            tiled=True,
        )
        return arrived.reshape(1, seq_count * capacity, width)
    home = [
        exchanged(placed[step], "seq", step) for step in STEPS[1:]
    ]
    arranged = pl.pallas_call(
        arrange_kernel,
        out_shape=shape_of((4 * capacity, width)),
        in_specs=[VMEM] * 4,
        out_specs=VMEM,
        compiler_params=params(16),
        name="arrange",
    )(placed[0], *home)
    return arranged[None]


def solution(mesh):
    placed = (
        P("cfg", "seq", "blk"),
        P("cfg", "seq", "blk"),
        P("cfg", "seq", "blk"),
        P("cfg", "seq", None),
        P("blk", None),
        P(None, "blk"),
        P("blk", None),
        P(),
        P(),
        P("seq"),
        P("seq", None),
    )
    return jax.shard_map(
        shards, mesh=mesh, in_specs=placed, out_specs=P("cfg", "seq", "blk"), check_vma=False
    )
```

```python
import functools
import math

import jax
import jax.numpy as jnp
from jax import lax
from jax.experimental import pallas as pl
from jax.experimental.pallas import tpu as pltpu
from jax.sharding import PartitionSpec as P

D = 1536
HEAD_DIM = 128
CLIPS = 3
NEG_FILL = -1e30
FAR = 2.0**100
VMEM = pl.BlockSpec(memory_space=pltpu.VMEM)
ANY = pl.BlockSpec(memory_space=pl.ANY)
F32 = jnp.float32
BF16 = jnp.bfloat16


def shape_of(extent, dtype=BF16):
    return jax.ShapeDtypeStruct(extent, dtype)


def params(mib):
    return pltpu.CompilerParams(vmem_limit_bytes=mib * 2**20)


def cost(flops, moved):
    return pl.CostEstimate(flops=flops, bytes_accessed=moved, transcendentals=0)


STEPS = (0, 2, 3, 1)


def head_at(side, place):
    return jnp.where(side == 0, place, 3 - place)


def works(side, place):
    return place < 3 if side == 0 else place >= 1


def hop(value, step, back=False):
    pairs = []
    for side in range(2):
        for place in range(4):
            target = place ^ step
            if works(side, target):
                pair = (side * 4 + place, side * 4 + target)
                pairs.append(pair[::-1] if back else pair)
    return lax.ppermute(value, ("cfg", "seq"), pairs)


def pack_kernel(q_ref, k_ref, v_ref, clip_ref, *refs):
    outs, clips, held, sems = refs[:4], refs[4], refs[5], refs[6]
    side, place = lax.axis_index("cfg"), lax.axis_index("seq")
    slots = q_ref.shape[0]
    copies = [pltpu.make_async_copy(clip_ref, clips, sems.at[3])]
    for part, source in enumerate((q_ref, k_ref, v_ref)):
        copies.append(pltpu.make_async_copy(source, held.at[part], sems.at[part]))
    for copy in copies:
        copy.start()
    copies[0].wait()
    numbers = clips[...].astype(F32)
    rest = jnp.zeros((16 - numbers.shape[0], 128), F32)
    rows = jnp.concatenate([numbers, rest], axis=0).astype(BF16)
    for out in outs:
        out[3 * slots :, :] = rows
    for part in range(3):
        copies[1 + part].wait()
        for step, out in zip(STEPS, outs):
            head = jnp.clip(head_at(side, jnp.bitwise_xor(place, step)), 0, 2)
            columns = pl.ds(pl.multiple_of(head * HEAD_DIM, HEAD_DIM), HEAD_DIM)
            out[part * slots : (part + 1) * slots, :] = held[part, :, columns]


def attend_kernel(*refs):
    blocks, outs, (q_aug, k_aug, v_aug, wide, found) = refs[:4], refs[-9:-5], refs[-5:]
    slots = outs[0].shape[0]
    count = slots // CLIPS
    group = 4 * count
    lane = lax.broadcasted_iota(jnp.int32, (count, 128), 1)
    row = lax.broadcasted_iota(jnp.int32, (count, 128), 0)
    q_tail = jnp.where(lane == 0, -FAR, 0.0).astype(BF16)
    v_tail = (lane == 0).astype(BF16)
    fills, bases = [], []
    for index, block in enumerate(blocks):
        numbers = block[3 * slots :, :].astype(F32)
        line = lax.broadcasted_iota(jnp.int32, numbers.shape, 0)
        spot = lax.broadcasted_iota(jnp.int32, numbers.shape, 1)
        live = (line < slots // 128) & (numbers < CLIPS - 0.5)
        filled = jnp.sum(live.astype(F32)).astype(jnp.int32)
        first = jnp.sum(jnp.where((line == 0) & (spot == 0), numbers, 0.0)).astype(jnp.int32)
        fills.append(filled)
        wide[index, :, :] = block[: 3 * slots, :].astype(F32)
        for turn in range(CLIPS):
            clip = lax.rem(first + turn, CLIPS)
            base = pl.multiple_of((clip * 4 + index) * count, count)
            bases.append(base)
            here = pl.ds(base, count)
            for part, target in enumerate((q_aug, k_aug, v_aug)):
                rows = pl.ds(part * slots + turn, count, stride=CLIPS)
                target[here, :128] = wide[index, rows, :].astype(BF16)
            padding = (lane == 0) & (CLIPS * row + turn >= filled)
            q_aug[here, 128:] = q_tail
            k_aug[here, 128:] = padding.astype(BF16)
            v_aug[here, 128:] = v_tail
    scale = math.log2(math.e) / math.sqrt(HEAD_DIM)

    def score(clip):
        here = slice(clip * group, (clip + 1) * group)
        return lax.dot_general(
            q_aug[here, :], k_aug[here, :], (((1,), (1,)), ((), ())), preferred_element_type=F32
        )

    ahead = score(0)
    for clip in range(CLIPS):
        scores = ahead
        if clip + 1 < CLIPS:
            ahead = score(clip + 1)
        here = slice(clip * group, (clip + 1) * group)
        peak = jnp.max(scores, axis=1, keepdims=True)
        probs = jnp.exp2((scores - peak) * scale).astype(BF16)
        summed = jnp.dot(probs, v_aug[here, :], preferred_element_type=F32)
        found[here, :] = summed[:, :128] / summed[:, 128:129]
    line = lax.broadcasted_iota(jnp.int32, (slots, 128), 0)
    for index, out in enumerate(outs):
        for turn in range(CLIPS):
            base = bases[index * CLIPS + turn]
            wide[index, pl.ds(turn, count, stride=CLIPS), :] = found[pl.ds(base, count), :]
        out[...] = jnp.where(line < fills[index], wide[index, :slots, :], 0.0).astype(BF16)


def regroup_kernel(own, back1, back2, back3, first, second):
    side, place = lax.axis_index("cfg"), lax.axis_index("seq")
    half = first.shape[0]
    for head in range(3):
        home = jnp.where(side == 0, head, 3 - head)
        step = jnp.bitwise_xor(home, place)
        columns = slice(head * HEAD_DIM, (head + 1) * HEAD_DIM)
        for index, source in zip(STEPS, (own, back1, back2, back3)):

            @pl.when(step == index)
            def _():
                for out, which in ((first, 1 - side), (second, side)):
                    rows = pl.ds(pl.multiple_of(which * half, half), half)
                    out[:, columns] = source[rows, :]


def kept(value):
    return pltpu.with_memory_space_constraint(value, pltpu.VMEM)


def afar(value):
    return pltpu.with_memory_space_constraint(value, pltpu.HBM)


def load_kernel(*refs):
    outs, sems = refs[4:7], refs[7]
    copies = [
        pltpu.make_async_copy(refs[index], out, sems.at[index]) for index, out in enumerate(outs)
    ]
    for copy in copies:
        copy.start()
    for copy in copies:
        copy.wait()


def load(arrays, after):
    return pl.pallas_call(
        load_kernel,
        out_shape=[pltpu.VMEM(array.shape, BF16) for array in arrays],
        in_specs=[ANY] * 4,
        out_specs=[VMEM] * 3,
        scratch_shapes=[pltpu.SemaphoreType.DMA((3,))],
        compiler_params=params(16),
        cost_estimate=cost(2**34, 2**24),
        name="load",
    )(*(afar(array) for array in arrays), after)


def across(value, masks):
    pairs = [
        (side * 4 + blk, side * 4 + (blk ^ masks[side])) for side in range(2) for blk in range(4)
    ]
    return lax.ppermute(value, ("cfg", "blk"), pairs)


def cut_kernel(got, out, sem):
    part = out.shape[0]
    offset = pl.multiple_of((1 - lax.axis_index("cfg")) * part, part)
    copy = pltpu.make_async_copy(got.at[pl.ds(offset, part), :], out, sem)
    copy.start()
    copy.wait()


def join_kernel(own, near, near_swap, far, far_swap, after, out, sems):
    side = lax.axis_index("cfg")
    width, part = own.shape[0], far.shape[0]
    plan = (
        (own, 0, width),
        (near, (1 + side) * width, width),
        (near_swap, (2 - side) * width, width),
        (far, 3 * width + (1 - side) * part, part),
        (far_swap, 3 * width + side * part, part),
    )
    copies = []
    for index, (source, offset, rows) in enumerate(plan):
        target = out.at[pl.ds(pl.multiple_of(offset, part), rows), :]
        copy = pltpu.make_async_copy(source, target, sems.at[index])
        copy.start()
        copies.append(copy)
    for copy in copies:
        copy.wait()


def gate_kernel(value, after, out):
    pass


def gate(value, after):
    return pl.pallas_call(
        gate_kernel,
        out_shape=shape_of(value.shape, value.dtype),
        in_specs=[ANY] * 2,
        out_specs=ANY,
        input_output_aliases={0: 0},
        compiler_params=params(1),
        name="gate",
    )(value, after)


def fetch_near(w_out):
    near = across(w_out, (1, 2))
    half = pl.pallas_call(
        cut_kernel,
        out_shape=shape_of((w_out.shape[0] // 2, D)),
        in_specs=[ANY],
        out_specs=ANY,
        scratch_shapes=[pltpu.SemaphoreType.DMA],
        compiler_params=params(16),
        name="cut",
    )(near)
    return near, half


def fetch_rest(w_out, near, half, after):
    far = across(half, (2, 1))
    far = gate(far, after)
    pieces = (afar(w_out), near, exchanged(near, "cfg", 1), far, exchanged(far, "cfg", 1))
    return pl.pallas_call(
        join_kernel,
        out_shape=pltpu.VMEM((D, D), BF16),
        in_specs=[ANY] * 6,
        out_specs=VMEM,
        scratch_shapes=[pltpu.SemaphoreType.DMA((5,))],
        compiler_params=params(16),
        name="join",
    )(*pieces, after)


def attention_by_head(query, key, value, slot_clip, early, weights):
    slots = query.shape[0]
    packed = pl.pallas_call(
        pack_kernel,
        out_shape=[shape_of((3 * slots + 16, 128))] * 4,
        in_specs=[ANY] * 4,
        out_specs=[VMEM] * 4,
        scratch_shapes=[
            pltpu.VMEM((slots // 128, 128), jnp.int32),
            pltpu.VMEM((3, slots, 3 * HEAD_DIM), BF16),
            pltpu.SemaphoreType.DMA((4,)),
        ],
        compiler_params=params(16),
        name="pack",
    )(afar(query), afar(key), afar(value), afar(slot_clip.reshape(slots // 128, 128)))
    blocks = [packed[0]] + [hop(packed[index], STEPS[index]) for index in (1, 2, 3)]
    early = (*early, *(kept(weight) for weight in load(weights, packed[0])))
    results = pl.pallas_call(
        attend_kernel,
        out_shape=[shape_of((slots, 128))] * 4,
        in_specs=[VMEM] * 4 + [ANY] * (len(early) - 3) + [VMEM] * 3,
        out_specs=[VMEM] * 4,
        scratch_shapes=[pltpu.VMEM((4 * slots, 256), BF16)] * 3
        + [pltpu.VMEM((4, 3 * slots, 128), F32), pltpu.VMEM((4 * slots, 128), F32)],
        compiler_params=params(28),
        cost_estimate=cost(2**32, 2**21),
        name="attend",
    )(*blocks, *early)
    backs = [hop(results[index], STEPS[index], back=True) for index in (1, 2, 3)]
    half = slots // 2
    return early[-3:], pl.pallas_call(
        regroup_kernel,
        out_shape=[shape_of((half, 3 * HEAD_DIM))] * 2,
        in_specs=[VMEM] * 4,
        out_specs=[VMEM] * 2,
        compiler_params=params(16),
        name="regroup",
    )(results[0], *backs)


def attention_by_rows(query, key, value, slot_clip):
    slots, width = query.shape
    heads = width // HEAD_DIM
    live = slot_clip < CLIPS
    factor = 1.0 / math.sqrt(HEAD_DIM)
    query_heads = query.reshape(slots, heads, HEAD_DIM)

    def absorb(carry, piece):
        key_piece, value_piece, clip_piece = piece
        best, total, accum = carry
        kept = (clip_piece[None, :] == slot_clip[:, None]) & live[:, None]
        scores = jnp.einsum("qhd,khd->hqk", query_heads, key_piece, preferred_element_type=F32)
        scores = jnp.where(kept[None], scores * factor, NEG_FILL)
        new_best = jnp.maximum(best, jnp.max(scores, axis=-1))
        fade = jnp.exp(best - new_best)
        probs = jnp.exp(scores - new_best[..., None])
        total = total * fade + jnp.sum(probs, axis=-1)
        added = jnp.einsum(
            "hqk,khd->qhd", probs.astype(BF16), value_piece, preferred_element_type=F32
        )
        accum = accum * jnp.transpose(fade)[:, :, None] + added
        return (new_best, total, accum), None

    start = (
        jnp.full((heads, slots), NEG_FILL, F32),
        jnp.zeros((heads, slots), F32),
        jnp.zeros((slots, heads, HEAD_DIM), F32),
    )
    pieces = (
        lax.all_gather(key, "seq").reshape(-1, slots, heads, HEAD_DIM),
        lax.all_gather(value, "seq").reshape(-1, slots, heads, HEAD_DIM),
        lax.all_gather(slot_clip, "seq"),
    )
    (best, total, accum), _ = lax.scan(absorb, start, pieces)
    attended = (accum / jnp.transpose(total)[:, :, None]).reshape(slots, width)
    attended = jnp.where(live[:, None], attended, 0.0).astype(BF16)
    half = slots // 2
    side = lax.axis_index("cfg")
    return [
        lax.dynamic_slice_in_dim(attended, which * half, half, 0) for which in (1 - side, side)
    ]


def chosen(mod, kind, clip, columns):
    picked = jnp.zeros((clip.shape[0], columns.stop - columns.start), F32)
    for index in range(CLIPS):
        picked = jnp.where(clip == index, mod[index, kind : kind + 1, columns], picked)
    return picked


def lowered_tiles(hidden, mixed, down, mod, clip):
    blk = lax.axis_index("blk")
    width = D // lax.axis_size("blk")
    for start in range(0, D, 2 * width):
        columns = slice(start, start + 2 * width)
        lowered = jnp.dot(hidden[...], down[:, columns], preferred_element_type=F32)
        lowered = chosen(mod, 3, clip, columns) * lowered
        for index in range(2):
            part = slice(start + index * width, start + (index + 1) * width)
            stream = jnp.where(blk == part.start // width, mixed[:, part], 0.0)
            yield part, lowered[:, index * width : (index + 1) * width] + stream


def project_kernel(*refs):
    att, w_out, out = refs[:3], refs[3], refs[4]
    rows_in = jnp.concatenate([piece[...] for piece in att], axis=1)
    depth = rows_in.shape[1]
    for start in range(0, D, 512):
        columns = slice(start, start + 512)
        out[:, columns] = jnp.dot(
            rows_in, w_out[:depth, columns], preferred_element_type=F32
        )


def project(att, w_out):
    return pl.pallas_call(
        project_kernel,
        out_shape=shape_of((att[0].shape[0], D), F32),
        in_specs=[VMEM] * 4,
        out_specs=VMEM,
        compiler_params=params(16),
        cost_estimate=cost(2**32, 2**22),
        name="project",
    )(*att, kept(w_out))


def feed_kernel(turn, count, *refs):
    att, (w_out, up, down, res, mod, clip_ref), refs = (
        refs[:count],
        refs[count : count + 6],
        refs[count + 6 :],
    )
    if turn == 0:
        out, mixed, hidden, normed = refs
    else:
        partial, hidden, mixed, normed = refs
    side = lax.axis_index("cfg")
    half = hidden.shape[0]
    which = 1 - side if turn == 0 else side
    rows = pl.ds(pl.multiple_of(which * half, half), half)
    rows_in = jnp.concatenate([piece[...] for piece in att], axis=1)
    depth = rows_in.shape[1]
    clip = clip_ref[rows, :][:, :1]
    tiles = [slice(start, start + 512) for start in range(0, D, 512)]
    for columns in tiles:
        projected = jnp.dot(rows_in, w_out[D - depth :, columns], preferred_element_type=F32)
        if turn == 1:
            projected = projected + partial[:, columns]
        mixed[:, columns] = (
            res[rows, columns].astype(F32) + chosen(mod, 0, clip, columns) * projected
        )
    held = mixed[...]
    centre = held - jnp.mean(held, axis=1, keepdims=True)
    spread = lax.rsqrt(jnp.mean(centre * centre, axis=1, keepdims=True) + 1e-06)
    for columns in tiles:
        stretch, shift = chosen(mod, 2, clip, columns), chosen(mod, 1, clip, columns)
        normed[:, columns] = (centre[:, columns] * spread * (1.0 + stretch) + shift).astype(BF16)
    for columns in tiles:
        raised = jnp.dot(normed[...], up[:, columns], preferred_element_type=F32)
        hidden[:, columns] = jax.nn.gelu(raised, approximate=True).astype(BF16)
    if turn == 0:
        for columns, terms in lowered_tiles(hidden, mixed, down, mod, clip):
            out[:, columns] = terms.astype(BF16)


def feed(turn, att, w_out, w_up, w_down, residual, mod, clip_wide):
    half = att[0].shape[0]
    inner = [pltpu.VMEM((half, D), BF16)]
    more = []
    if turn == 0:
        out_shape = shape_of((half, D))
        inner = [pltpu.VMEM((half, D), F32), pltpu.VMEM((half, D), BF16)] + inner
    else:
        out_shape = [shape_of((half, D)), shape_of((half, D), F32)]
        more = [project(att[:3], w_out)]
        att = att[3:]
    return pl.pallas_call(
        functools.partial(feed_kernel, turn, len(att)),
        out_shape=out_shape,
        in_specs=[VMEM] * (len(att) + 6 + len(more)),
        out_specs=VMEM if turn == 0 else [VMEM] * 2,
        scratch_shapes=inner,
        compiler_params=params(24),
        cost_estimate=cost(2**36, 2**24),
        name="feed",
    )(*att, kept(w_out), kept(w_up), kept(w_down), kept(residual), mod, clip_wide, *more)


def guide_kernel(hidden, mixed, down, other_ref, clip_ref, mod, scale_ref, *refs):
    outs, held = refs[:4], refs[4]
    side, blk = lax.axis_index("cfg"), lax.axis_index("blk")
    half, width = outs[0].shape
    clip = clip_ref[pl.ds(pl.multiple_of(side * half, half), half), :][:, :1]
    strength = jnp.zeros((half, 1), F32)
    for index in range(CLIPS):
        strength = jnp.where(clip == index, scale_ref[index], strength)
    lean = jnp.where(side == 0, strength, 1.0 - strength)
    for columns, mine in lowered_tiles(hidden, mixed, down, mod, clip):
        other = other_ref[:, columns].astype(F32)
        held[:, columns] = other + lean * (mine - other)
    for step, out in enumerate(outs):
        target = jnp.bitwise_xor(blk, step)
        columns = pl.ds(pl.multiple_of(target * width, width), width)
        out[...] = held[:, columns].astype(out.dtype)


def place_kernel(own, got1, got2, got3, placing, *outs):
    guided = own[...] + got1[...].astype(F32) + got2[...].astype(F32) + got3[...].astype(F32)
    placed = jnp.dot(placing[...], guided.astype(BF16), preferred_element_type=F32).astype(BF16)
    if len(outs) == 1:
        outs[0][...] = placed
    else:
        count = outs[0].shape[0]
        for index, out in enumerate(outs):
            out[...] = placed[index * count : (index + 1) * count, :]


def arrange_kernel(*refs):
    out = refs[4]
    place = lax.axis_index("seq")
    count = refs[0].shape[0]
    for step, source in zip(STEPS, refs):
        origin = jnp.bitwise_xor(place, step)
        out[pl.ds(pl.multiple_of(origin * count, count), count), :] = source[...]


def exchanged(value, axis, mask):
    pairs = [(index, index ^ mask) for index in range(lax.axis_size(axis))]
    return lax.ppermute(value, axis, pairs)


def shards(
    queries, keys, values, residual, w_out, w_up, w_down, modulation, guide_scale, slot_clip, owner
):
    slots, width = queries.shape[1:]
    half = slots // 2
    seq_count = lax.axis_size("seq")
    capacity = max(2, slots // seq_count)
    side, place = lax.axis_index("cfg"), lax.axis_index("seq")

    clip_wide = jnp.broadcast_to(slot_clip[:, None], (slots, 128))
    clip_half = lax.dynamic_slice_in_dim(slot_clip, side * half, half, 0)
    owner_half = lax.dynamic_slice_in_dim(owner[:, 0], side * half, half, 0)
    order = jnp.arange(half, dtype=jnp.int32)
    before = (owner_half[None, :] == owner_half[:, None]) & (order[None, :] < order[:, None])
    rank = jnp.sum(before.astype(jnp.int32), axis=1)
    if seq_count == 4:
        lane = jnp.bitwise_xor(owner_half, place)
    else:
        lane = owner_half
    target = jnp.where(clip_half < CLIPS, lane * capacity + rank, -1)
    placing = (
        jnp.arange(seq_count * capacity, dtype=jnp.int32)[:, None] == target[None, :]
    ).astype(BF16)

    near, w_half = fetch_near(w_out)
    if seq_count == 4:
        (up, down, stream), attended = attention_by_head(
            queries[0],
            keys[0],
            values[0],
            slot_clip,
            (clip_wide, placing, w_half),
            (w_up, w_down, residual[0]),
        )
    else:
        attended = attention_by_rows(queries[0], keys[0], values[0], slot_clip)
        up, down, stream = load((w_up, w_down, residual[0]), attended[0])

    whole = fetch_rest(w_out, near, w_half, attended[0])
    parts = []
    for turn in range(2):
        piece = attended[turn]
        gathered = [piece] + [exchanged(piece, "blk", mask) for mask in (1, 2, 3)]
        parts.append(feed(turn, gathered, whole, up, down, stream, modulation, clip_wide))
    other = exchanged(parts[0], "cfg", 1)
    own, *sent = pl.pallas_call(
        guide_kernel,
        out_shape=[shape_of((half, width), F32)] + [shape_of((half, width))] * 3,
        in_specs=[VMEM] * 6 + [pl.BlockSpec(memory_space=pltpu.SMEM)],
        out_specs=[VMEM] * 4,
        scratch_shapes=[pltpu.VMEM((half, D), F32)],
        compiler_params=params(16),
        name="guide",
    )(*parts[1], kept(down), other, clip_wide, modulation, guide_scale)
    got = [exchanged(piece, "blk", mask) for mask, piece in zip((1, 2, 3), sent)]
    by_step = seq_count == 4
    placed = pl.pallas_call(
        place_kernel,
        out_shape=[shape_of((capacity, width))] * 4
        if by_step
        else [shape_of((seq_count * capacity, width))],
        in_specs=[VMEM] * 5,
        out_specs=[VMEM] * (4 if by_step else 1),
        compiler_params=params(16),
        name="place",
    )(own, *got, placing)
    if not by_step:
        arrived = lax.all_to_all(
            placed[0].reshape(seq_count, capacity, width), "seq", split_axis=0, concat_axis=0,
            tiled=True,
        )
        return arrived.reshape(1, seq_count * capacity, width)
    home = [
        exchanged(placed[step], "seq", step) for step in STEPS[1:]
    ]
    arranged = pl.pallas_call(
        arrange_kernel,
        out_shape=shape_of((4 * capacity, width)),
        in_specs=[VMEM] * 4,
        out_specs=VMEM,
        compiler_params=params(16),
        name="arrange",
    )(placed[0], *home)
    return arranged[None]


def solution(mesh):
    placed = (
        P("cfg", "seq", "blk"),
        P("cfg", "seq", "blk"),
        P("cfg", "seq", "blk"),
        P("cfg", "seq", None),
        P("blk", None),
        P(None, "blk"),
        P("blk", None),
        P(),
        P(),
        P("seq"),
        P("seq", None),
    )
    return jax.shard_map(
        shards, mesh=mesh, in_specs=placed, out_specs=P("cfg", "seq", "blk"), check_vma=False
    )
```

```python
import functools
import math

import jax
import jax.numpy as jnp
from jax import lax
from jax.experimental import pallas as pl
from jax.experimental.pallas import tpu as pltpu
from jax.sharding import PartitionSpec as P

D = 1536
HEAD_DIM = 128
CLIPS = 3
NEG_FILL = -1e30
FAR = 2.0**100
VMEM = pl.BlockSpec(memory_space=pltpu.VMEM)
ANY = pl.BlockSpec(memory_space=pl.ANY)
F32 = jnp.float32
BF16 = jnp.bfloat16


def shape_of(extent, dtype=BF16):
    return jax.ShapeDtypeStruct(extent, dtype)


def params(mib):
    return pltpu.CompilerParams(vmem_limit_bytes=mib * 2**20)


def cost(flops, moved):
    return pl.CostEstimate(flops=flops, bytes_accessed=moved, transcendentals=0)


STEPS = (0, 2, 3, 1)


def head_at(side, place):
    return jnp.where(side == 0, place, 3 - place)


def works(side, place):
    return place < 3 if side == 0 else place >= 1


def hop(value, step, back=False):
    pairs = []
    for side in range(2):
        for place in range(4):
            target = place ^ step
            if works(side, target):
                pair = (side * 4 + place, side * 4 + target)
                pairs.append(pair[::-1] if back else pair)
    return lax.ppermute(value, ("cfg", "seq"), pairs)


def pack_kernel(q_ref, k_ref, v_ref, clip_ref, *refs):
    outs, clips, held, sems = refs[:4], refs[4], refs[5], refs[6]
    side, place = lax.axis_index("cfg"), lax.axis_index("seq")
    slots = q_ref.shape[0]
    copies = [pltpu.make_async_copy(clip_ref, clips, sems.at[3])]
    for part, source in enumerate((q_ref, k_ref, v_ref)):
        copies.append(pltpu.make_async_copy(source, held.at[part], sems.at[part]))
    for copy in copies:
        copy.start()
    copies[0].wait()
    numbers = clips[...].astype(F32)
    rest = jnp.zeros((16 - numbers.shape[0], 128), F32)
    rows = jnp.concatenate([numbers, rest], axis=0).astype(BF16)
    for out in outs:
        out[3 * slots :, :] = rows
    for part in range(3):
        copies[1 + part].wait()
        for step, out in zip(STEPS, outs):
            head = jnp.clip(head_at(side, jnp.bitwise_xor(place, step)), 0, 2)
            columns = pl.ds(pl.multiple_of(head * HEAD_DIM, HEAD_DIM), HEAD_DIM)
            out[part * slots : (part + 1) * slots, :] = held[part, :, columns]


def attend_kernel(*refs):
    blocks, outs, (q_aug, k_aug, v_aug, wide, found) = refs[:4], refs[-9:-5], refs[-5:]
    slots = outs[0].shape[0]
    count = slots // CLIPS
    group = 4 * count
    lane = lax.broadcasted_iota(jnp.int32, (count, 128), 1)
    row = lax.broadcasted_iota(jnp.int32, (count, 128), 0)
    q_tail = jnp.where(lane == 0, -FAR, 0.0).astype(BF16)
    v_tail = (lane == 0).astype(BF16)
    fills, bases = [], []
    for index, block in enumerate(blocks):
        numbers = block[3 * slots :, :].astype(F32)
        line = lax.broadcasted_iota(jnp.int32, numbers.shape, 0)
        spot = lax.broadcasted_iota(jnp.int32, numbers.shape, 1)
        live = (line < slots // 128) & (numbers < CLIPS - 0.5)
        filled = jnp.sum(live.astype(F32)).astype(jnp.int32)
        first = jnp.sum(jnp.where((line == 0) & (spot == 0), numbers, 0.0)).astype(jnp.int32)
        fills.append(filled)
        wide[index, : 3 * slots, :] = block[: 3 * slots, :].astype(F32)
        for turn in range(CLIPS):
            clip = lax.rem(first + turn, CLIPS)
            base = pl.multiple_of((clip * 4 + index) * count, count)
            bases.append(base)
            here = pl.ds(base, count)
            for part, target in enumerate((q_aug, k_aug, v_aug)):
                rows = pl.ds(part * slots + turn, count, stride=CLIPS)
                target[here, :128] = wide[index, rows, :].astype(BF16)
            padding = (lane == 0) & (CLIPS * row + turn >= filled)
            q_aug[here, 128:] = q_tail
            k_aug[here, 128:] = padding.astype(BF16)
            v_aug[here, 128:] = v_tail
    scale = math.log2(math.e) / math.sqrt(HEAD_DIM)

    def score(clip):
        here = slice(clip * group, (clip + 1) * group)
        return lax.dot_general(
            q_aug[here, :], k_aug[here, :], (((1,), (1,)), ((), ())), preferred_element_type=F32
        )

    ahead = score(0)
    for clip in range(CLIPS):
        scores = ahead
        if clip + 1 < CLIPS:
            ahead = score(clip + 1)
        here = slice(clip * group, (clip + 1) * group)
        peak = jnp.max(scores, axis=1, keepdims=True)
        probs = jnp.exp2((scores - peak) * scale).astype(BF16)
        summed = jnp.dot(probs, v_aug[here, :], preferred_element_type=F32)
        found[here, :] = summed[:, :128] / summed[:, 128:129]
    line = lax.broadcasted_iota(jnp.int32, (slots, 128), 0)
    for index, out in enumerate(outs):
        for turn in range(CLIPS):
            base = bases[index * CLIPS + turn]
            wide[index, pl.ds(turn, count, stride=CLIPS), :] = found[pl.ds(base, count), :]
        out[...] = jnp.where(line < fills[index], wide[index, :slots, :], 0.0).astype(BF16)


def regroup_kernel(own, back1, back2, back3, first, second):
    side, place = lax.axis_index("cfg"), lax.axis_index("seq")
    half = first.shape[0]
    for head in range(3):
        home = jnp.where(side == 0, head, 3 - head)
        step = jnp.bitwise_xor(home, place)
        columns = slice(head * HEAD_DIM, (head + 1) * HEAD_DIM)
        for index, source in zip(STEPS, (own, back1, back2, back3)):

            @pl.when(step == index)
            def _():
                for out, which in ((first, 1 - side), (second, side)):
                    rows = pl.ds(pl.multiple_of(which * half, half), half)
                    out[:, columns] = source[rows, :]


def kept(value):
    return pltpu.with_memory_space_constraint(value, pltpu.VMEM)


def afar(value):
    return pltpu.with_memory_space_constraint(value, pltpu.HBM)


def load_kernel(*refs):
    outs, sems = refs[4:7], refs[7]
    copies = [
        pltpu.make_async_copy(refs[index], out, sems.at[index]) for index, out in enumerate(outs)
    ]
    for copy in copies:
        copy.start()
    for copy in copies:
        copy.wait()


def load(arrays, after):
    return pl.pallas_call(
        load_kernel,
        out_shape=[pltpu.VMEM(array.shape, BF16) for array in arrays],
        in_specs=[ANY] * 4,
        out_specs=[VMEM] * 3,
        scratch_shapes=[pltpu.SemaphoreType.DMA((3,))],
        compiler_params=params(16),
        cost_estimate=cost(2**34, 2**24),
        name="load",
    )(*(afar(array) for array in arrays), after)


def across(value, masks):
    pairs = [
        (side * 4 + blk, side * 4 + (blk ^ masks[side])) for side in range(2) for blk in range(4)
    ]
    return lax.ppermute(value, ("cfg", "blk"), pairs)


def cut_kernel(got, out, sem):
    part = out.shape[0]
    offset = pl.multiple_of((1 - lax.axis_index("cfg")) * part, part)
    copy = pltpu.make_async_copy(got.at[pl.ds(offset, part), :], out, sem)
    copy.start()
    copy.wait()


def join_kernel(own, near, near_swap, far, far_swap, after, out, sems):
    side = lax.axis_index("cfg")
    width, part = own.shape[0], far.shape[0]
    plan = (
        (own, 0, width),
        (near, (1 + side) * width, width),
        (near_swap, (2 - side) * width, width),
        (far, 3 * width + (1 - side) * part, part),
        (far_swap, 3 * width + side * part, part),
    )
    copies = []
    for index, (source, offset, rows) in enumerate(plan):
        target = out.at[pl.ds(pl.multiple_of(offset, part), rows), :]
        copy = pltpu.make_async_copy(source, target, sems.at[index])
        copy.start()
        copies.append(copy)
    for copy in copies:
        copy.wait()


def gate_kernel(value, after, out):
    pass


def gate(value, after):
    return pl.pallas_call(
        gate_kernel,
        out_shape=shape_of(value.shape, value.dtype),
        in_specs=[ANY] * 2,
        out_specs=ANY,
        input_output_aliases={0: 0},
        compiler_params=params(1),
        name="gate",
    )(value, after)


def fetch_near(w_out):
    near = across(w_out, (1, 2))
    half = pl.pallas_call(
        cut_kernel,
        out_shape=shape_of((w_out.shape[0] // 2, D)),
        in_specs=[ANY],
        out_specs=ANY,
        scratch_shapes=[pltpu.SemaphoreType.DMA],
        compiler_params=params(16),
        name="cut",
    )(near)
    return near, half


def fetch_rest(w_out, near, half, after):
    far = across(half, (2, 1))
    far = gate(far, after)
    pieces = (afar(w_out), near, exchanged(near, "cfg", 1), far, exchanged(far, "cfg", 1))
    return pl.pallas_call(
        join_kernel,
        out_shape=pltpu.VMEM((D, D), BF16),
        in_specs=[ANY] * 6,
        out_specs=VMEM,
        scratch_shapes=[pltpu.SemaphoreType.DMA((5,))],
        compiler_params=params(16),
        name="join",
    )(*pieces, after)


def attention_by_head(query, key, value, slot_clip, early, weights):
    slots = query.shape[0]
    packed = pl.pallas_call(
        pack_kernel,
        out_shape=[shape_of((3 * slots + 16, 128))] * 4,
        in_specs=[ANY] * 4,
        out_specs=[VMEM] * 4,
        scratch_shapes=[
            pltpu.VMEM((slots // 128, 128), jnp.int32),
            pltpu.VMEM((3, slots, 3 * HEAD_DIM), BF16),
            pltpu.SemaphoreType.DMA((4,)),
        ],
        compiler_params=params(16),
        name="pack",
    )(afar(query), afar(key), afar(value), afar(slot_clip.reshape(slots // 128, 128)))
    blocks = [packed[0]] + [hop(packed[index], STEPS[index]) for index in (1, 2, 3)]
    early = (*early, *(kept(weight) for weight in load(weights, packed[0])))
    results = pl.pallas_call(
        attend_kernel,
        out_shape=[shape_of((slots, 128))] * 4,
        in_specs=[VMEM] * 4 + [ANY] * (len(early) - 3) + [VMEM] * 3,
        out_specs=[VMEM] * 4,
        scratch_shapes=[pltpu.VMEM((4 * slots, 256), BF16)] * 3
        + [pltpu.VMEM((4, 3 * slots + 8, 128), F32), pltpu.VMEM((4 * slots, 128), F32)],
        compiler_params=params(28),
        cost_estimate=cost(2**32, 2**21),
        name="attend",
    )(*blocks, *early)
    backs = [hop(results[index], STEPS[index], back=True) for index in (1, 2, 3)]
    half = slots // 2
    return early[-3:], pl.pallas_call(
        regroup_kernel,
        out_shape=[shape_of((half, 3 * HEAD_DIM))] * 2,
        in_specs=[VMEM] * 4,
        out_specs=[VMEM] * 2,
        compiler_params=params(16),
        name="regroup",
    )(results[0], *backs)


def attention_by_rows(query, key, value, slot_clip):
    slots, width = query.shape
    heads = width // HEAD_DIM
    live = slot_clip < CLIPS
    factor = 1.0 / math.sqrt(HEAD_DIM)
    query_heads = query.reshape(slots, heads, HEAD_DIM)

    def absorb(carry, piece):
        key_piece, value_piece, clip_piece = piece
        best, total, accum = carry
        kept = (clip_piece[None, :] == slot_clip[:, None]) & live[:, None]
        scores = jnp.einsum("qhd,khd->hqk", query_heads, key_piece, preferred_element_type=F32)
        scores = jnp.where(kept[None], scores * factor, NEG_FILL)
        new_best = jnp.maximum(best, jnp.max(scores, axis=-1))
        fade = jnp.exp(best - new_best)
        probs = jnp.exp(scores - new_best[..., None])
        total = total * fade + jnp.sum(probs, axis=-1)
        added = jnp.einsum(
            "hqk,khd->qhd", probs.astype(BF16), value_piece, preferred_element_type=F32
        )
        accum = accum * jnp.transpose(fade)[:, :, None] + added
        return (new_best, total, accum), None

    start = (
        jnp.full((heads, slots), NEG_FILL, F32),
        jnp.zeros((heads, slots), F32),
        jnp.zeros((slots, heads, HEAD_DIM), F32),
    )
    pieces = (
        lax.all_gather(key, "seq").reshape(-1, slots, heads, HEAD_DIM),
        lax.all_gather(value, "seq").reshape(-1, slots, heads, HEAD_DIM),
        lax.all_gather(slot_clip, "seq"),
    )
    (best, total, accum), _ = lax.scan(absorb, start, pieces)
    attended = (accum / jnp.transpose(total)[:, :, None]).reshape(slots, width)
    attended = jnp.where(live[:, None], attended, 0.0).astype(BF16)
    half = slots // 2
    side = lax.axis_index("cfg")
    return [
        lax.dynamic_slice_in_dim(attended, which * half, half, 0) for which in (1 - side, side)
    ]


def chosen(mod, kind, clip, columns):
    picked = jnp.zeros((clip.shape[0], columns.stop - columns.start), F32)
    for index in range(CLIPS):
        picked = jnp.where(clip == index, mod[index, kind : kind + 1, columns], picked)
    return picked


def lowered_tiles(hidden, mixed, down, mod, clip):
    blk = lax.axis_index("blk")
    width = D // lax.axis_size("blk")
    for start in range(0, D, 2 * width):
        columns = slice(start, start + 2 * width)
        lowered = jnp.dot(hidden[...], down[:, columns], preferred_element_type=F32)
        lowered = chosen(mod, 3, clip, columns) * lowered
        for index in range(2):
            part = slice(start + index * width, start + (index + 1) * width)
            stream = jnp.where(blk == part.start // width, mixed[:, part], 0.0)
            yield part, lowered[:, index * width : (index + 1) * width] + stream


def project_kernel(*refs):
    att, w_out, out = refs[:3], refs[3], refs[4]
    rows_in = jnp.concatenate([piece[...] for piece in att], axis=1)
    depth = rows_in.shape[1]
    for start in range(0, D, 512):
        columns = slice(start, start + 512)
        out[:, columns] = jnp.dot(
            rows_in, w_out[:depth, columns], preferred_element_type=F32
        )


def project(att, w_out):
    return pl.pallas_call(
        project_kernel,
        out_shape=shape_of((att[0].shape[0], D), F32),
        in_specs=[VMEM] * 4,
        out_specs=VMEM,
        compiler_params=params(16),
        cost_estimate=cost(2**32, 2**22),
        name="project",
    )(*att, kept(w_out))


def feed_kernel(turn, count, *refs):
    att, (w_out, up, down, res, mod, clip_ref), refs = (
        refs[:count],
        refs[count : count + 6],
        refs[count + 6 :],
    )
    if turn == 0:
        out, mixed, hidden, normed = refs
    else:
        partial, hidden, mixed, normed = refs
    side = lax.axis_index("cfg")
    half = hidden.shape[0]
    which = 1 - side if turn == 0 else side
    rows = pl.ds(pl.multiple_of(which * half, half), half)
    rows_in = jnp.concatenate([piece[...] for piece in att], axis=1)
    depth = rows_in.shape[1]
    clip = clip_ref[rows, :][:, :1]
    tiles = [slice(start, start + 512) for start in range(0, D, 512)]
    for columns in tiles:
        projected = jnp.dot(rows_in, w_out[D - depth :, columns], preferred_element_type=F32)
        if turn == 1:
            projected = projected + partial[:, columns]
        mixed[:, columns] = (
            res[rows, columns].astype(F32) + chosen(mod, 0, clip, columns) * projected
        )
    held = mixed[...]
    centre = held - jnp.mean(held, axis=1, keepdims=True)
    spread = lax.rsqrt(jnp.mean(centre * centre, axis=1, keepdims=True) + 1e-06)
    for columns in tiles:
        stretch, shift = chosen(mod, 2, clip, columns), chosen(mod, 1, clip, columns)
        normed[:, columns] = (centre[:, columns] * spread * (1.0 + stretch) + shift).astype(BF16)
    for columns in tiles:
        raised = jnp.dot(normed[...], up[:, columns], preferred_element_type=F32)
        hidden[:, columns] = jax.nn.gelu(raised, approximate=True).astype(BF16)
    if turn == 0:
        for columns, terms in lowered_tiles(hidden, mixed, down, mod, clip):
            out[:, columns] = terms.astype(BF16)


def feed(turn, att, w_out, w_up, w_down, residual, mod, clip_wide):
    half = att[0].shape[0]
    inner = [pltpu.VMEM((half, D), BF16)]
    more = []
    if turn == 0:
        out_shape = shape_of((half, D))
        inner = [pltpu.VMEM((half, D), F32), pltpu.VMEM((half, D), BF16)] + inner
    else:
        out_shape = [shape_of((half, D)), shape_of((half, D), F32)]
        more = [project(att[:3], w_out)]
        att = att[3:]
    return pl.pallas_call(
        functools.partial(feed_kernel, turn, len(att)),
        out_shape=out_shape,
        in_specs=[VMEM] * (len(att) + 6 + len(more)),
        out_specs=VMEM if turn == 0 else [VMEM] * 2,
        scratch_shapes=inner,
        compiler_params=params(24),
        cost_estimate=cost(2**36, 2**24),
        name="feed",
    )(*att, kept(w_out), kept(w_up), kept(w_down), kept(residual), mod, clip_wide, *more)


def guide_kernel(hidden, mixed, down, other_ref, clip_ref, mod, scale_ref, *refs):
    outs, held = refs[:4], refs[4]
    side, blk = lax.axis_index("cfg"), lax.axis_index("blk")
    half, width = outs[0].shape
    clip = clip_ref[pl.ds(pl.multiple_of(side * half, half), half), :][:, :1]
    strength = jnp.zeros((half, 1), F32)
    for index in range(CLIPS):
        strength = jnp.where(clip == index, scale_ref[index], strength)
    lean = jnp.where(side == 0, strength, 1.0 - strength)
    for columns, mine in lowered_tiles(hidden, mixed, down, mod, clip):
        other = other_ref[:, columns].astype(F32)
        held[:, columns] = other + lean * (mine - other)
    for step, out in enumerate(outs):
        target = jnp.bitwise_xor(blk, step)
        columns = pl.ds(pl.multiple_of(target * width, width), width)
        out[...] = held[:, columns].astype(out.dtype)


def place_kernel(own, got1, got2, got3, placing, *outs):
    guided = own[...] + got1[...].astype(F32) + got2[...].astype(F32) + got3[...].astype(F32)
    placed = jnp.dot(placing[...], guided.astype(BF16), preferred_element_type=F32).astype(BF16)
    if len(outs) == 1:
        outs[0][...] = placed
    else:
        count = outs[0].shape[0]
        for index, out in enumerate(outs):
            out[...] = placed[index * count : (index + 1) * count, :]


def arrange_kernel(*refs):
    out = refs[4]
    place = lax.axis_index("seq")
    count = refs[0].shape[0]
    for step, source in zip(STEPS, refs):
        origin = jnp.bitwise_xor(place, step)
        out[pl.ds(pl.multiple_of(origin * count, count), count), :] = source[...]


def exchanged(value, axis, mask):
    pairs = [(index, index ^ mask) for index in range(lax.axis_size(axis))]
    return lax.ppermute(value, axis, pairs)


def shards(
    queries, keys, values, residual, w_out, w_up, w_down, modulation, guide_scale, slot_clip, owner
):
    slots, width = queries.shape[1:]
    half = slots // 2
    seq_count = lax.axis_size("seq")
    capacity = max(2, slots // seq_count)
    side, place = lax.axis_index("cfg"), lax.axis_index("seq")

    clip_wide = jnp.broadcast_to(slot_clip[:, None], (slots, 128))
    clip_half = lax.dynamic_slice_in_dim(slot_clip, side * half, half, 0)
    owner_half = lax.dynamic_slice_in_dim(owner[:, 0], side * half, half, 0)
    order = jnp.arange(half, dtype=jnp.int32)
    before = (owner_half[None, :] == owner_half[:, None]) & (order[None, :] < order[:, None])
    rank = jnp.sum(before.astype(jnp.int32), axis=1)
    if seq_count == 4:
        lane = jnp.bitwise_xor(owner_half, place)
    else:
        lane = owner_half
    target = jnp.where(clip_half < CLIPS, lane * capacity + rank, -1)
    placing = (
        jnp.arange(seq_count * capacity, dtype=jnp.int32)[:, None] == target[None, :]
    ).astype(BF16)

    near, w_half = fetch_near(w_out)
    if seq_count == 4:
        (up, down, stream), attended = attention_by_head(
            queries[0],
            keys[0],
            values[0],
            slot_clip,
            (clip_wide, placing, w_half),
            (w_up, w_down, residual[0]),
        )
    else:
        attended = attention_by_rows(queries[0], keys[0], values[0], slot_clip)
        up, down, stream = load((w_up, w_down, residual[0]), attended[0])

    whole = fetch_rest(w_out, near, w_half, attended[0])
    parts = []
    for turn in range(2):
        piece = attended[turn]
        gathered = [piece] + [exchanged(piece, "blk", mask) for mask in (1, 2, 3)]
        parts.append(feed(turn, gathered, whole, up, down, stream, modulation, clip_wide))
    other = exchanged(parts[0], "cfg", 1)
    own, *sent = pl.pallas_call(
        guide_kernel,
        out_shape=[shape_of((half, width), F32)] + [shape_of((half, width))] * 3,
        in_specs=[VMEM] * 6 + [pl.BlockSpec(memory_space=pltpu.SMEM)],
        out_specs=[VMEM] * 4,
        scratch_shapes=[pltpu.VMEM((half, D), F32)],
        compiler_params=params(16),
        name="guide",
    )(*parts[1], kept(down), other, clip_wide, modulation, guide_scale)
    got = [exchanged(piece, "blk", mask) for mask, piece in zip((1, 2, 3), sent)]
    by_step = seq_count == 4
    placed = pl.pallas_call(
        place_kernel,
        out_shape=[shape_of((capacity, width))] * 4
        if by_step
        else [shape_of((seq_count * capacity, width))],
        in_specs=[VMEM] * 5,
        out_specs=[VMEM] * (4 if by_step else 1),
        compiler_params=params(16),
        name="place",
    )(own, *got, placing)
    if not by_step:
        arrived = lax.all_to_all(
            placed[0].reshape(seq_count, capacity, width), "seq", split_axis=0, concat_axis=0,
            tiled=True,
        )
        return arrived.reshape(1, seq_count * capacity, width)
    home = [
        exchanged(placed[step], "seq", step) for step in STEPS[1:]
    ]
    arranged = pl.pallas_call(
        arrange_kernel,
        out_shape=shape_of((4 * capacity, width)),
        in_specs=[VMEM] * 4,
        out_specs=VMEM,
        compiler_params=params(16),
        name="arrange",
    )(placed[0], *home)
    return arranged[None]


def solution(mesh):
    placed = (
        P("cfg", "seq", "blk"),
        P("cfg", "seq", "blk"),
        P("cfg", "seq", "blk"),
        P("cfg", "seq", None),
        P("blk", None),
        P(None, "blk"),
        P("blk", None),
        P(),
        P(),
        P("seq"),
        P("seq", None),
    )
    return jax.shard_map(
        shards, mesh=mesh, in_specs=placed, out_specs=P("cfg", "seq", "blk"), check_vma=False
    )
```

```python
import functools
import math

import jax
import jax.numpy as jnp
from jax import lax
from jax.experimental import pallas as pl
from jax.experimental.pallas import tpu as pltpu
from jax.sharding import PartitionSpec as P

D = 1536
HEAD_DIM = 128
CLIPS = 3
NEG_FILL = -1e30
FAR = 2.0**100
VMEM = pl.BlockSpec(memory_space=pltpu.VMEM)
ANY = pl.BlockSpec(memory_space=pl.ANY)
F32 = jnp.float32
BF16 = jnp.bfloat16


def shape_of(extent, dtype=BF16):
    return jax.ShapeDtypeStruct(extent, dtype)


def params(mib):
    return pltpu.CompilerParams(vmem_limit_bytes=mib * 2**20)


def cost(flops, moved):
    return pl.CostEstimate(flops=flops, bytes_accessed=moved, transcendentals=0)


STEPS = (0, 2, 3, 1)


def head_at(side, place):
    return jnp.where(side == 0, place, 3 - place)


def works(side, place):
    return place < 3 if side == 0 else place >= 1


def hop(value, step, back=False):
    pairs = []
    for side in range(2):
        for place in range(4):
            target = place ^ step
            if works(side, target):
                pair = (side * 4 + place, side * 4 + target)
                pairs.append(pair[::-1] if back else pair)
    return lax.ppermute(value, ("cfg", "seq"), pairs)


def pack_kernel(q_ref, k_ref, v_ref, clip_ref, *refs):
    outs, clips, held, sems = refs[:4], refs[4], refs[5], refs[6]
    side, place = lax.axis_index("cfg"), lax.axis_index("seq")
    slots = q_ref.shape[0]
    copies = [pltpu.make_async_copy(clip_ref, clips, sems.at[3])]
    for part, source in enumerate((q_ref, k_ref, v_ref)):
        copies.append(pltpu.make_async_copy(source, held.at[part], sems.at[part]))
    for copy in copies:
        copy.start()
    copies[0].wait()
    numbers = clips[...].astype(F32)
    rest = jnp.zeros((16 - numbers.shape[0], 128), F32)
    rows = jnp.concatenate([numbers, rest], axis=0).astype(BF16)
    for out in outs:
        out[3 * slots :, :] = rows
    for part in range(3):
        copies[1 + part].wait()
        for step, out in zip(STEPS, outs):
            head = jnp.clip(head_at(side, jnp.bitwise_xor(place, step)), 0, 2)
            columns = pl.ds(pl.multiple_of(head * HEAD_DIM, HEAD_DIM), HEAD_DIM)
            out[part * slots : (part + 1) * slots, :] = held[part, :, columns]


def attend_kernel(*refs):
    blocks, outs, (q_aug, k_aug, v_aug, wide, found) = refs[:4], refs[-9:-5], refs[-5:]
    slots = outs[0].shape[0]
    count = slots // CLIPS
    group = 4 * count
    lane = lax.broadcasted_iota(jnp.int32, (count, 128), 1)
    row = lax.broadcasted_iota(jnp.int32, (count, 128), 0)
    q_tail = jnp.where(lane == 0, -FAR, 0.0).astype(BF16)
    v_tail = (lane == 0).astype(BF16)
    fills, bases = [], []
    for index, block in enumerate(blocks):
        numbers = block[3 * slots :, :].astype(F32)
        line = lax.broadcasted_iota(jnp.int32, numbers.shape, 0)
        spot = lax.broadcasted_iota(jnp.int32, numbers.shape, 1)
        live = (line < slots // 128) & (numbers < CLIPS - 0.5)
        filled = jnp.sum(live.astype(F32)).astype(jnp.int32)
        first = jnp.sum(jnp.where((line == 0) & (spot == 0), numbers, 0.0)).astype(jnp.int32)
        fills.append(filled)
        wide[index, : 3 * slots, :] = block[: 3 * slots, :].astype(F32)
        for turn in range(CLIPS):
            clip = lax.rem(first + turn, CLIPS)
            base = pl.multiple_of((clip * 4 + index) * count, count)
            bases.append(base)
            here = pl.ds(base, count)
            for part, target in enumerate((q_aug, k_aug, v_aug)):
                rows = pl.ds(part * slots + turn, count, stride=CLIPS)
                target[here, :128] = wide[index, rows, :].astype(BF16)
            padding = (lane == 0) & (CLIPS * row + turn >= filled)
            q_aug[here, 128:] = q_tail
            k_aug[here, 128:] = padding.astype(BF16)
            v_aug[here, 128:] = v_tail
    scale = math.log2(math.e) / math.sqrt(HEAD_DIM)

    def score(clip):
        here = slice(clip * group, (clip + 1) * group)
        return lax.dot_general(
            q_aug[here, :], k_aug[here, :], (((1,), (1,)), ((), ())), preferred_element_type=F32
        )

    ahead = score(0)
    for clip in range(CLIPS):
        scores = ahead
        if clip + 1 < CLIPS:
            ahead = score(clip + 1)
        here = slice(clip * group, (clip + 1) * group)
        peak = jnp.max(scores, axis=1, keepdims=True)
        probs = jnp.exp2((scores - peak) * scale).astype(BF16)
        summed = jnp.dot(probs, v_aug[here, :], preferred_element_type=F32)
        found[here, :] = summed[:, :128] / summed[:, 128:129]
    line = lax.broadcasted_iota(jnp.int32, (slots, 128), 0)
    for index, out in enumerate(outs):
        for turn in range(CLIPS):
            base = bases[index * CLIPS + turn]
            wide[index, pl.ds(turn, count, stride=CLIPS), :] = found[pl.ds(base, count), :]
        out[...] = jnp.where(line < fills[index], wide[index, :slots, :], 0.0).astype(BF16)


def regroup_kernel(own, back1, back2, back3, first, second):
    side, place = lax.axis_index("cfg"), lax.axis_index("seq")
    half = first.shape[0]
    for head in range(3):
        home = jnp.where(side == 0, head, 3 - head)
        step = jnp.bitwise_xor(home, place)
        columns = slice(head * HEAD_DIM, (head + 1) * HEAD_DIM)
        for index, source in zip(STEPS, (own, back1, back2, back3)):

            @pl.when(step == index)
            def _():
                for out, which in ((first, 1 - side), (second, side)):
                    rows = pl.ds(pl.multiple_of(which * half, half), half)
                    out[:, columns] = source[rows, :]


def kept(value):
    return pltpu.with_memory_space_constraint(value, pltpu.VMEM)


def afar(value):
    return pltpu.with_memory_space_constraint(value, pltpu.HBM)


def load_kernel(*refs):
    outs, sems = refs[4:7], refs[7]
    copies = [
        pltpu.make_async_copy(refs[index], out, sems.at[index]) for index, out in enumerate(outs)
    ]
    for copy in copies:
        copy.start()
    for copy in copies:
        copy.wait()


def load(arrays, after):
    return pl.pallas_call(
        load_kernel,
        out_shape=[pltpu.VMEM(array.shape, BF16) for array in arrays],
        in_specs=[ANY] * 4,
        out_specs=[VMEM] * 3,
        scratch_shapes=[pltpu.SemaphoreType.DMA((3,))],
        compiler_params=params(16),
        cost_estimate=cost(2**34, 2**24),
        name="load",
    )(*(afar(array) for array in arrays), after)


def across(value, masks):
    pairs = [
        (side * 4 + blk, side * 4 + (blk ^ masks[side])) for side in range(2) for blk in range(4)
    ]
    return lax.ppermute(value, ("cfg", "blk"), pairs)


def cut_kernel(got, out, sem):
    part = out.shape[0]
    offset = pl.multiple_of((1 - lax.axis_index("cfg")) * part, part)
    copy = pltpu.make_async_copy(got.at[pl.ds(offset, part), :], out, sem)
    copy.start()
    copy.wait()


def join_kernel(own, near, near_swap, far, far_swap, after, out, sems):
    side = lax.axis_index("cfg")
    width, part = own.shape[0], far.shape[0]
    plan = (
        (own, 0, width),
        (near, (1 + side) * width, width),
        (near_swap, (2 - side) * width, width),
        (far, 3 * width + (1 - side) * part, part),
        (far_swap, 3 * width + side * part, part),
    )
    copies = []
    for index, (source, offset, rows) in enumerate(plan):
        target = out.at[pl.ds(pl.multiple_of(offset, part), rows), :]
        copy = pltpu.make_async_copy(source, target, sems.at[index])
        copy.start()
        copies.append(copy)
    for copy in copies:
        copy.wait()


def gate_kernel(value, after, out):
    pass


def gate(value, after):
    return pl.pallas_call(
        gate_kernel,
        out_shape=shape_of(value.shape, value.dtype),
        in_specs=[ANY] * 2,
        out_specs=ANY,
        input_output_aliases={0: 0},
        compiler_params=params(1),
        name="gate",
    )(value, after)


def fetch_near(w_out):
    near = across(w_out, (1, 2))
    half = pl.pallas_call(
        cut_kernel,
        out_shape=shape_of((w_out.shape[0] // 2, D)),
        in_specs=[ANY],
        out_specs=ANY,
        scratch_shapes=[pltpu.SemaphoreType.DMA],
        compiler_params=params(16),
        name="cut",
    )(near)
    return near, half


def fetch_rest(w_out, near, half, after):
    far = across(half, (2, 1))
    far = gate(far, after)
    pieces = (afar(w_out), near, exchanged(near, "cfg", 1), far, exchanged(far, "cfg", 1))
    return pl.pallas_call(
        join_kernel,
        out_shape=pltpu.VMEM((D, D), BF16),
        in_specs=[ANY] * 6,
        out_specs=VMEM,
        scratch_shapes=[pltpu.SemaphoreType.DMA((5,))],
        compiler_params=params(16),
        name="join",
    )(*pieces, after)


def attention_by_head(query, key, value, slot_clip, early, weights):
    slots = query.shape[0]
    packed = pl.pallas_call(
        pack_kernel,
        out_shape=[shape_of((3 * slots + 16, 128))] * 4,
        in_specs=[ANY] * 4,
        out_specs=[VMEM] * 4,
        scratch_shapes=[
            pltpu.VMEM((slots // 128, 128), jnp.int32),
            pltpu.VMEM((3, slots, 3 * HEAD_DIM), BF16),
            pltpu.SemaphoreType.DMA((4,)),
        ],
        compiler_params=params(16),
        name="pack",
    )(afar(query), afar(key), afar(value), afar(slot_clip.reshape(slots // 128, 128)))
    blocks = [packed[0]] + [hop(packed[index], STEPS[index]) for index in (1, 2, 3)]
    early = (*early, *(kept(weight) for weight in load(weights, packed[0])))
    results = pl.pallas_call(
        attend_kernel,
        out_shape=[shape_of((slots, 128))] * 4,
        in_specs=[VMEM] * 4 + [ANY] * (len(early) - 3) + [VMEM] * 3,
        out_specs=[VMEM] * 4,
        scratch_shapes=[pltpu.VMEM((4 * slots, 256), BF16)] * 3
        + [pltpu.VMEM((4, 3 * slots + 8, 128), F32), pltpu.VMEM((4 * slots, 128), F32)],
        compiler_params=params(28),
        cost_estimate=cost(2**32, 2**21),
        name="attend",
    )(*blocks, *early)
    backs = [hop(results[index], STEPS[index], back=True) for index in (1, 2, 3)]
    half = slots // 2
    return early[-3:], pl.pallas_call(
        regroup_kernel,
        out_shape=[shape_of((half, 3 * HEAD_DIM))] * 2,
        in_specs=[VMEM] * 4,
        out_specs=[VMEM] * 2,
        compiler_params=params(16),
        name="regroup",
    )(results[0], *backs)


def attention_by_rows(query, key, value, slot_clip):
    slots, width = query.shape
    heads = width // HEAD_DIM
    live = slot_clip < CLIPS
    factor = 1.0 / math.sqrt(HEAD_DIM)
    query_heads = query.reshape(slots, heads, HEAD_DIM)

    def absorb(carry, piece):
        key_piece, value_piece, clip_piece = piece
        best, total, accum = carry
        kept = (clip_piece[None, :] == slot_clip[:, None]) & live[:, None]
        scores = jnp.einsum("qhd,khd->hqk", query_heads, key_piece, preferred_element_type=F32)
        scores = jnp.where(kept[None], scores * factor, NEG_FILL)
        new_best = jnp.maximum(best, jnp.max(scores, axis=-1))
        fade = jnp.exp(best - new_best)
        probs = jnp.exp(scores - new_best[..., None])
        total = total * fade + jnp.sum(probs, axis=-1)
        added = jnp.einsum(
            "hqk,khd->qhd", probs.astype(BF16), value_piece, preferred_element_type=F32
        )
        accum = accum * jnp.transpose(fade)[:, :, None] + added
        return (new_best, total, accum), None

    start = (
        jnp.full((heads, slots), NEG_FILL, F32),
        jnp.zeros((heads, slots), F32),
        jnp.zeros((slots, heads, HEAD_DIM), F32),
    )
    pieces = (
        lax.all_gather(key, "seq").reshape(-1, slots, heads, HEAD_DIM),
        lax.all_gather(value, "seq").reshape(-1, slots, heads, HEAD_DIM),
        lax.all_gather(slot_clip, "seq"),
    )
    (best, total, accum), _ = lax.scan(absorb, start, pieces)
    attended = (accum / jnp.transpose(total)[:, :, None]).reshape(slots, width)
    attended = jnp.where(live[:, None], attended, 0.0).astype(BF16)
    half = slots // 2
    side = lax.axis_index("cfg")
    return [
        lax.dynamic_slice_in_dim(attended, which * half, half, 0) for which in (1 - side, side)
    ]


def chosen(mod, kind, clip, columns):
    picked = jnp.zeros((clip.shape[0], columns.stop - columns.start), F32)
    for index in range(CLIPS):
        picked = jnp.where(clip == index, mod[index, kind : kind + 1, columns], picked)
    return picked


def lowered_tiles(hidden, mixed, down, mod, clip):
    blk = lax.axis_index("blk")
    width = D // lax.axis_size("blk")
    for start in range(0, D, 2 * width):
        columns = slice(start, start + 2 * width)
        lowered = jnp.dot(hidden[...], down[:, columns], preferred_element_type=F32)
        lowered = chosen(mod, 3, clip, columns) * lowered
        for index in range(2):
            part = slice(start + index * width, start + (index + 1) * width)
            stream = jnp.where(blk == part.start // width, mixed[:, part], 0.0)
            yield part, lowered[:, index * width : (index + 1) * width] + stream


def project_kernel(*refs):
    att, w_out, out = refs[:3], refs[3], refs[4]
    rows_in = jnp.concatenate([piece[...] for piece in att], axis=1)
    depth = rows_in.shape[1]
    for start in range(0, D, 512):
        columns = slice(start, start + 512)
        out[:, columns] = jnp.dot(
            rows_in, w_out[:depth, columns], preferred_element_type=F32
        )


def project(att, w_out):
    return pl.pallas_call(
        project_kernel,
        out_shape=shape_of((att[0].shape[0], D), F32),
        in_specs=[VMEM] * 4,
        out_specs=VMEM,
        compiler_params=params(16),
        cost_estimate=cost(2**32, 2**22),
        name="project",
    )(*att, kept(w_out))


def feed_kernel(turn, count, *refs):
    att, (w_out, up, down, res, mod, clip_ref), refs = (
        refs[:count],
        refs[count : count + 6],
        refs[count + 6 :],
    )
    if turn == 0:
        out, mixed, hidden, normed = refs
    else:
        partial, hidden, mixed, normed = refs
    side = lax.axis_index("cfg")
    half = hidden.shape[0]
    which = 1 - side if turn == 0 else side
    rows = pl.ds(pl.multiple_of(which * half, half), half)
    rows_in = jnp.concatenate([piece[...] for piece in att], axis=1)
    depth = rows_in.shape[1]
    clip = clip_ref[rows, :][:, :1]
    tiles = [slice(start, start + 512) for start in range(0, D, 512)]
    for columns in tiles:
        projected = jnp.dot(rows_in, w_out[D - depth :, columns], preferred_element_type=F32)
        if turn == 1:
            projected = projected + partial[:, columns]
        mixed[:, columns] = (
            res[rows, columns].astype(F32) + chosen(mod, 0, clip, columns) * projected
        )
    held = mixed[...]
    centre = held - jnp.mean(held, axis=1, keepdims=True)
    spread = lax.rsqrt(jnp.mean(centre * centre, axis=1, keepdims=True) + 1e-06)
    for columns in tiles:
        stretch, shift = chosen(mod, 2, clip, columns), chosen(mod, 1, clip, columns)
        normed[:, columns] = (centre[:, columns] * spread * (1.0 + stretch) + shift).astype(BF16)
    for columns in tiles:
        raised = jnp.dot(normed[...], up[:, columns], preferred_element_type=F32)
        hidden[:, columns] = jax.nn.gelu(raised, approximate=True).astype(BF16)
    if turn == 0:
        for columns, terms in lowered_tiles(hidden, mixed, down, mod, clip):
            out[:, columns] = terms.astype(BF16)


def feed(turn, att, w_out, w_up, w_down, residual, mod, clip_wide):
    half = att[0].shape[0]
    inner = [pltpu.VMEM((half, D), BF16)]
    more = []
    if turn == 0:
        out_shape = shape_of((half, D))
        inner = [pltpu.VMEM((half, D), F32), pltpu.VMEM((half, D), BF16)] + inner
    else:
        out_shape = [shape_of((half, D)), shape_of((half, D), F32)]
        more = [project(att[:3], w_out)]
        att = att[3:]
    return pl.pallas_call(
        functools.partial(feed_kernel, turn, len(att)),
        out_shape=out_shape,
        in_specs=[VMEM] * (len(att) + 6 + len(more)),
        out_specs=VMEM if turn == 0 else [VMEM] * 2,
        scratch_shapes=inner,
        compiler_params=params(24),
        cost_estimate=cost(2**36, 2**24),
        name="feed",
    )(*att, kept(w_out), kept(w_up), kept(w_down), kept(residual), mod, clip_wide, *more)


def guide_kernel(hidden, mixed, down, other_ref, clip_ref, mod, scale_ref, *refs):
    outs, held = refs[:4], refs[4]
    side, blk = lax.axis_index("cfg"), lax.axis_index("blk")
    half, width = outs[0].shape
    clip = clip_ref[pl.ds(pl.multiple_of(side * half, half), half), :][:, :1]
    strength = jnp.zeros((half, 1), F32)
    for index in range(CLIPS):
        strength = jnp.where(clip == index, scale_ref[index : index + 1, :1], strength)
    lean = jnp.where(side == 0, strength, 1.0 - strength)
    for columns, mine in lowered_tiles(hidden, mixed, down, mod, clip):
        other = other_ref[:, columns].astype(F32)
        held[:, columns] = other + lean * (mine - other)
    for step, out in enumerate(outs):
        target = jnp.bitwise_xor(blk, step)
        columns = pl.ds(pl.multiple_of(target * width, width), width)
        out[...] = held[:, columns].astype(out.dtype)


def place_kernel(own, got1, got2, got3, placing, *outs):
    guided = own[...] + got1[...].astype(F32) + got2[...].astype(F32) + got3[...].astype(F32)
    placed = jnp.dot(placing[...], guided.astype(BF16), preferred_element_type=F32).astype(BF16)
    if len(outs) == 1:
        outs[0][...] = placed
    else:
        count = outs[0].shape[0]
        for index, out in enumerate(outs):
            out[...] = placed[index * count : (index + 1) * count, :]


def arrange_kernel(*refs):
    out = refs[4]
    place = lax.axis_index("seq")
    count = refs[0].shape[0]
    for step, source in zip(STEPS, refs):
        origin = jnp.bitwise_xor(place, step)
        out[pl.ds(pl.multiple_of(origin * count, count), count), :] = source[...]


def exchanged(value, axis, mask):
    pairs = [(index, index ^ mask) for index in range(lax.axis_size(axis))]
    return lax.ppermute(value, axis, pairs)


def shards(
    queries, keys, values, residual, w_out, w_up, w_down, modulation, guide_scale, slot_clip, owner
):
    slots, width = queries.shape[1:]
    half = slots // 2
    seq_count = lax.axis_size("seq")
    capacity = max(2, slots // seq_count)
    side, place = lax.axis_index("cfg"), lax.axis_index("seq")

    clip_wide = jnp.broadcast_to(slot_clip[:, None], (slots, 128))
    scale_wide = jnp.broadcast_to(guide_scale[:, None], (CLIPS, 128))
    clip_half = lax.dynamic_slice_in_dim(slot_clip, side * half, half, 0)
    owner_half = lax.dynamic_slice_in_dim(owner[:, 0], side * half, half, 0)
    order = jnp.arange(half, dtype=jnp.int32)
    before = (owner_half[None, :] == owner_half[:, None]) & (order[None, :] < order[:, None])
    rank = jnp.sum(before.astype(jnp.int32), axis=1)
    if seq_count == 4:
        lane = jnp.bitwise_xor(owner_half, place)
    else:
        lane = owner_half
    target = jnp.where(clip_half < CLIPS, lane * capacity + rank, -1)
    placing = (
        jnp.arange(seq_count * capacity, dtype=jnp.int32)[:, None] == target[None, :]
    ).astype(BF16)

    near, w_half = fetch_near(w_out)
    if seq_count == 4:
        (up, down, stream), attended = attention_by_head(
            queries[0],
            keys[0],
            values[0],
            slot_clip,
            (clip_wide, placing, w_half, scale_wide),
            (w_up, w_down, residual[0]),
        )
    else:
        attended = attention_by_rows(queries[0], keys[0], values[0], slot_clip)
        up, down, stream = load((w_up, w_down, residual[0]), attended[0])

    whole = fetch_rest(w_out, near, w_half, attended[0])
    parts = []
    for turn in range(2):
        piece = attended[turn]
        gathered = [piece] + [exchanged(piece, "blk", mask) for mask in (1, 2, 3)]
        parts.append(feed(turn, gathered, whole, up, down, stream, modulation, clip_wide))
    other = exchanged(parts[0], "cfg", 1)
    own, *sent = pl.pallas_call(
        guide_kernel,
        out_shape=[shape_of((half, width), F32)] + [shape_of((half, width))] * 3,
        in_specs=[VMEM] * 7,
        out_specs=[VMEM] * 4,
        scratch_shapes=[pltpu.VMEM((half, D), F32)],
        compiler_params=params(16),
        name="guide",
    )(*parts[1], kept(down), other, clip_wide, modulation, scale_wide)
    got = [exchanged(piece, "blk", mask) for mask, piece in zip((1, 2, 3), sent)]
    by_step = seq_count == 4
    placed = pl.pallas_call(
        place_kernel,
        out_shape=[shape_of((capacity, width))] * 4
        if by_step
        else [shape_of((seq_count * capacity, width))],
        in_specs=[VMEM] * 5,
        out_specs=[VMEM] * (4 if by_step else 1),
        compiler_params=params(16),
        name="place",
    )(own, *got, placing)
    if not by_step:
        arrived = lax.all_to_all(
            placed[0].reshape(seq_count, capacity, width), "seq", split_axis=0, concat_axis=0,
            tiled=True,
        )
        return arrived.reshape(1, seq_count * capacity, width)
    home = [
        exchanged(placed[step], "seq", step) for step in STEPS[1:]
    ]
    arranged = pl.pallas_call(
        arrange_kernel,
        out_shape=shape_of((4 * capacity, width)),
        in_specs=[VMEM] * 4,
        out_specs=VMEM,
        compiler_params=params(16),
        name="arrange",
    )(placed[0], *home)
    return arranged[None]


def solution(mesh):
    placed = (
        P("cfg", "seq", "blk"),
        P("cfg", "seq", "blk"),
        P("cfg", "seq", "blk"),
        P("cfg", "seq", None),
        P("blk", None),
        P(None, "blk"),
        P("blk", None),
        P(),
        P(),
        P("seq"),
        P("seq", None),
    )
    return jax.shard_map(
        shards, mesh=mesh, in_specs=placed, out_specs=P("cfg", "seq", "blk"), check_vma=False
    )
```

```python
import functools
import math

import jax
import jax.numpy as jnp
from jax import lax
from jax.experimental import pallas as pl
from jax.experimental.pallas import tpu as pltpu
from jax.sharding import PartitionSpec as P

D = 1536
HEAD_DIM = 128
CLIPS = 3
NEG_FILL = -1e30
FAR = 2.0**100
VMEM = pl.BlockSpec(memory_space=pltpu.VMEM)
ANY = pl.BlockSpec(memory_space=pl.ANY)
F32 = jnp.float32
BF16 = jnp.bfloat16


def shape_of(extent, dtype=BF16):
    return jax.ShapeDtypeStruct(extent, dtype)


def params(mib):
    return pltpu.CompilerParams(vmem_limit_bytes=mib * 2**20)


def cost(flops, moved):
    return pl.CostEstimate(flops=flops, bytes_accessed=moved, transcendentals=0)


STEPS = (0, 2, 3, 1)


def head_at(side, place):
    return jnp.where(side == 0, place, 3 - place)


def works(side, place):
    return place < 3 if side == 0 else place >= 1


def hop(value, step, back=False):
    pairs = []
    for side in range(2):
        for place in range(4):
            target = place ^ step
            if works(side, target):
                pair = (side * 4 + place, side * 4 + target)
                pairs.append(pair[::-1] if back else pair)
    return lax.ppermute(value, ("cfg", "seq"), pairs)


def pack_kernel(q_ref, k_ref, v_ref, clip_ref, *refs):
    outs, clips, held, sems = refs[:4], refs[4], refs[5], refs[6]
    side, place = lax.axis_index("cfg"), lax.axis_index("seq")
    slots = q_ref.shape[0]
    copies = [pltpu.make_async_copy(clip_ref, clips, sems.at[3])]
    for part, source in enumerate((q_ref, k_ref, v_ref)):
        copies.append(pltpu.make_async_copy(source, held.at[part], sems.at[part]))
    for copy in copies:
        copy.start()
    copies[0].wait()
    numbers = clips[...].astype(F32)
    rest = jnp.zeros((16 - numbers.shape[0], 128), F32)
    rows = jnp.concatenate([numbers, rest], axis=0).astype(BF16)
    for out in outs:
        out[3 * slots :, :] = rows
    for part in range(3):
        copies[1 + part].wait()
        for step, out in zip(STEPS, outs):
            head = jnp.clip(head_at(side, jnp.bitwise_xor(place, step)), 0, 2)
            columns = pl.ds(pl.multiple_of(head * HEAD_DIM, HEAD_DIM), HEAD_DIM)
            out[part * slots : (part + 1) * slots, :] = held[part, :, columns]


def attend_kernel(*refs):
    blocks, outs, (q_aug, k_aug, v_aug, wide, found) = refs[:4], refs[-9:-5], refs[-5:]
    slots = outs[0].shape[0]
    count = slots // CLIPS
    group = 4 * count
    lane = lax.broadcasted_iota(jnp.int32, (count, 128), 1)
    row = lax.broadcasted_iota(jnp.int32, (count, 128), 0)
    q_tail = jnp.where(lane == 0, -FAR, 0.0).astype(BF16)
    v_tail = (lane == 0).astype(BF16)
    fills, bases = [], []
    for index, block in enumerate(blocks):
        numbers = block[3 * slots :, :].astype(F32)
        line = lax.broadcasted_iota(jnp.int32, numbers.shape, 0)
        spot = lax.broadcasted_iota(jnp.int32, numbers.shape, 1)
        live = (line < slots // 128) & (numbers < CLIPS - 0.5)
        filled = jnp.sum(live.astype(F32)).astype(jnp.int32)
        first = jnp.sum(jnp.where((line == 0) & (spot == 0), numbers, 0.0)).astype(jnp.int32)
        fills.append(filled)
        wide[index, : 3 * slots, :] = block[: 3 * slots, :].astype(F32)
        for turn in range(CLIPS):
            clip = lax.rem(first + turn, CLIPS)
            base = pl.multiple_of((clip * 4 + index) * count, count)
            bases.append(base)
            here = pl.ds(base, count)
            for part, target in enumerate((q_aug, k_aug, v_aug)):
                rows = pl.ds(part * slots + turn, count, stride=CLIPS)
                target[here, :128] = wide[index, rows, :].astype(BF16)
            padding = (lane == 0) & (CLIPS * row + turn >= filled)
            q_aug[here, 128:] = q_tail
            k_aug[here, 128:] = padding.astype(BF16)
            v_aug[here, 128:] = v_tail
    scale = math.log2(math.e) / math.sqrt(HEAD_DIM)

    def score(clip):
        here = slice(clip * group, (clip + 1) * group)
        return lax.dot_general(
            q_aug[here, :], k_aug[here, :], (((1,), (1,)), ((), ())), preferred_element_type=F32
        )

    ahead = score(0)
    for clip in range(CLIPS):
        scores = ahead
        if clip + 1 < CLIPS:
            ahead = score(clip + 1)
        here = slice(clip * group, (clip + 1) * group)
        peak = jnp.max(scores, axis=1, keepdims=True)
        probs = jnp.exp2((scores - peak) * scale).astype(BF16)
        summed = jnp.dot(probs, v_aug[here, :], preferred_element_type=F32)
        found[here, :] = summed[:, :128] / summed[:, 128:129]
    line = lax.broadcasted_iota(jnp.int32, (slots, 128), 0)
    for index, out in enumerate(outs):
        for turn in range(CLIPS):
            base = bases[index * CLIPS + turn]
            wide[index, pl.ds(turn, count, stride=CLIPS), :] = found[pl.ds(base, count), :]
        out[...] = jnp.where(line < fills[index], wide[index, :slots, :], 0.0).astype(BF16)


def regroup_kernel(own, back1, back2, back3, first, second):
    side, place = lax.axis_index("cfg"), lax.axis_index("seq")
    half = first.shape[0]
    for head in range(3):
        home = jnp.where(side == 0, head, 3 - head)
        step = jnp.bitwise_xor(home, place)
        columns = slice(head * HEAD_DIM, (head + 1) * HEAD_DIM)
        for index, source in zip(STEPS, (own, back1, back2, back3)):

            @pl.when(step == index)
            def _():
                for out, which in ((first, 1 - side), (second, side)):
                    rows = pl.ds(pl.multiple_of(which * half, half), half)
                    out[:, columns] = source[rows, :]


def kept(value):
    return pltpu.with_memory_space_constraint(value, pltpu.VMEM)


def afar(value):
    return pltpu.with_memory_space_constraint(value, pltpu.HBM)


def load_kernel(*refs):
    outs, sems = refs[4:7], refs[7]
    copies = [
        pltpu.make_async_copy(refs[index], out, sems.at[index]) for index, out in enumerate(outs)
    ]
    for copy in copies:
        copy.start()
    for copy in copies:
        copy.wait()


def load(arrays, after):
    return pl.pallas_call(
        load_kernel,
        out_shape=[pltpu.VMEM(array.shape, BF16) for array in arrays],
        in_specs=[ANY] * 4,
        out_specs=[VMEM] * 3,
        scratch_shapes=[pltpu.SemaphoreType.DMA((3,))],
        compiler_params=params(16),
        cost_estimate=cost(2**34, 2**24),
        name="load",
    )(*(afar(array) for array in arrays), after)


def across(value, masks):
    pairs = [
        (side * 4 + blk, side * 4 + (blk ^ masks[side])) for side in range(2) for blk in range(4)
    ]
    return lax.ppermute(value, ("cfg", "blk"), pairs)


def cut_kernel(got, out, sem):
    part = out.shape[0]
    offset = pl.multiple_of((1 - lax.axis_index("cfg")) * part, part)
    copy = pltpu.make_async_copy(got.at[pl.ds(offset, part), :], out, sem)
    copy.start()
    copy.wait()


def join_kernel(own, near, near_swap, far, far_swap, after, out, sems):
    side = lax.axis_index("cfg")
    width, part = own.shape[0], far.shape[0]
    plan = (
        (own, 0, width),
        (near, (1 + side) * width, width),
        (near_swap, (2 - side) * width, width),
        (far, 3 * width + (1 - side) * part, part),
        (far_swap, 3 * width + side * part, part),
    )
    copies = []
    for index, (source, offset, rows) in enumerate(plan):
        target = out.at[pl.ds(pl.multiple_of(offset, part), rows), :]
        copy = pltpu.make_async_copy(source, target, sems.at[index])
        copy.start()
        copies.append(copy)
    for copy in copies:
        copy.wait()


def gate_kernel(value, after, out):
    pass


def gate(value, after):
    return pl.pallas_call(
        gate_kernel,
        out_shape=shape_of(value.shape, value.dtype),
        in_specs=[ANY] * 2,
        out_specs=ANY,
        input_output_aliases={0: 0},
        compiler_params=params(1),
        name="gate",
    )(value, after)


def fetch_near(w_out):
    near = across(w_out, (1, 2))
    half = pl.pallas_call(
        cut_kernel,
        out_shape=shape_of((w_out.shape[0] // 2, D)),
        in_specs=[ANY],
        out_specs=ANY,
        scratch_shapes=[pltpu.SemaphoreType.DMA],
        compiler_params=params(16),
        name="cut",
    )(near)
    return near, half


def fetch_rest(w_out, near, half, after):
    far = across(half, (2, 1))
    far = gate(far, after)
    pieces = (afar(w_out), near, exchanged(near, "cfg", 1), far, exchanged(far, "cfg", 1))
    return pl.pallas_call(
        join_kernel,
        out_shape=pltpu.VMEM((D, D), BF16),
        in_specs=[ANY] * 6,
        out_specs=VMEM,
        scratch_shapes=[pltpu.SemaphoreType.DMA((5,))],
        compiler_params=params(16),
        name="join",
    )(*pieces, after)


def attention_by_head(query, key, value, slot_clip, early, weights):
    slots = query.shape[0]
    packed = pl.pallas_call(
        pack_kernel,
        out_shape=[shape_of((3 * slots + 16, 128))] * 4,
        in_specs=[ANY] * 4,
        out_specs=[VMEM] * 4,
        scratch_shapes=[
            pltpu.VMEM((slots // 128, 128), jnp.int32),
            pltpu.VMEM((3, slots, 3 * HEAD_DIM), BF16),
            pltpu.SemaphoreType.DMA((4,)),
        ],
        compiler_params=params(16),
        name="pack",
    )(afar(query), afar(key), afar(value), afar(slot_clip.reshape(slots // 128, 128)))
    blocks = [packed[0]] + [hop(packed[index], STEPS[index]) for index in (1, 2, 3)]
    early = (*early, *(kept(weight) for weight in load(weights, packed[0])))
    results = pl.pallas_call(
        attend_kernel,
        out_shape=[shape_of((slots, 128))] * 4,
        in_specs=[VMEM] * 4 + [ANY] * (len(early) - 3) + [VMEM] * 3,
        out_specs=[VMEM] * 4,
        scratch_shapes=[pltpu.VMEM((4 * slots, 256), BF16)] * 3
        + [pltpu.VMEM((4, 3 * slots + 8, 128), F32), pltpu.VMEM((4 * slots, 128), F32)],
        compiler_params=params(28),
        cost_estimate=cost(2**32, 2**21),
        name="attend",
    )(*blocks, *early)
    backs = [hop(results[index], STEPS[index], back=True) for index in (1, 2, 3)]
    half = slots // 2
    return early[-3:], pl.pallas_call(
        regroup_kernel,
        out_shape=[shape_of((half, 3 * HEAD_DIM))] * 2,
        in_specs=[VMEM] * 4,
        out_specs=[VMEM] * 2,
        compiler_params=params(16),
        name="regroup",
    )(results[0], *backs)


def attention_by_rows(query, key, value, slot_clip):
    slots, width = query.shape
    heads = width // HEAD_DIM
    live = slot_clip < CLIPS
    factor = 1.0 / math.sqrt(HEAD_DIM)
    query_heads = query.reshape(slots, heads, HEAD_DIM)

    def absorb(carry, piece):
        key_piece, value_piece, clip_piece = piece
        best, total, accum = carry
        kept = (clip_piece[None, :] == slot_clip[:, None]) & live[:, None]
        scores = jnp.einsum("qhd,khd->hqk", query_heads, key_piece, preferred_element_type=F32)
        scores = jnp.where(kept[None], scores * factor, NEG_FILL)
        new_best = jnp.maximum(best, jnp.max(scores, axis=-1))
        fade = jnp.exp(best - new_best)
        probs = jnp.exp(scores - new_best[..., None])
        total = total * fade + jnp.sum(probs, axis=-1)
        added = jnp.einsum(
            "hqk,khd->qhd", probs.astype(BF16), value_piece, preferred_element_type=F32
        )
        accum = accum * jnp.transpose(fade)[:, :, None] + added
        return (new_best, total, accum), None

    start = (
        jnp.full((heads, slots), NEG_FILL, F32),
        jnp.zeros((heads, slots), F32),
        jnp.zeros((slots, heads, HEAD_DIM), F32),
    )
    pieces = (
        lax.all_gather(key, "seq").reshape(-1, slots, heads, HEAD_DIM),
        lax.all_gather(value, "seq").reshape(-1, slots, heads, HEAD_DIM),
        lax.all_gather(slot_clip, "seq"),
    )
    (best, total, accum), _ = lax.scan(absorb, start, pieces)
    attended = (accum / jnp.transpose(total)[:, :, None]).reshape(slots, width)
    attended = jnp.where(live[:, None], attended, 0.0).astype(BF16)
    half = slots // 2
    side = lax.axis_index("cfg")
    return [
        lax.dynamic_slice_in_dim(attended, which * half, half, 0) for which in (1 - side, side)
    ]


def chosen(mod, kind, clip, columns):
    picked = jnp.zeros((clip.shape[0], columns.stop - columns.start), F32)
    for index in range(CLIPS):
        picked = jnp.where(clip == index, mod[index, kind : kind + 1, columns], picked)
    return picked


def lowered_tiles(hidden, mixed, down, mod, clip):
    blk = lax.axis_index("blk")
    width = D // lax.axis_size("blk")
    for start in range(0, D, 2 * width):
        columns = slice(start, start + 2 * width)
        lowered = jnp.dot(hidden[...], down[:, columns], preferred_element_type=F32)
        lowered = chosen(mod, 3, clip, columns) * lowered
        for index in range(2):
            part = slice(start + index * width, start + (index + 1) * width)
            stream = jnp.where(blk == part.start // width, mixed[:, part], 0.0)
            yield part, lowered[:, index * width : (index + 1) * width] + stream


def project_kernel(*refs):
    att, w_out, out = refs[:3], refs[3], refs[4]
    rows_in = jnp.concatenate([piece[...] for piece in att], axis=1)
    depth = rows_in.shape[1]
    for start in range(0, D, 512):
        columns = slice(start, start + 512)
        out[:, columns] = jnp.dot(
            rows_in, w_out[:depth, columns], preferred_element_type=F32
        )


def project(att, w_out):
    return pl.pallas_call(
        project_kernel,
        out_shape=shape_of((att[0].shape[0], D), F32),
        in_specs=[VMEM] * 4,
        out_specs=VMEM,
        compiler_params=params(16),
        cost_estimate=cost(2**32, 2**22),
        name="project",
    )(*att, kept(w_out))


def feed_kernel(turn, count, *refs):
    att, (w_out, up, down, res, mod, clip_ref), refs = (
        refs[:count],
        refs[count : count + 6],
        refs[count + 6 :],
    )
    if turn == 0:
        out, mixed, hidden, normed = refs
    else:
        partial, hidden, mixed, normed = refs
    side = lax.axis_index("cfg")
    half = hidden.shape[0]
    which = 1 - side if turn == 0 else side
    rows = pl.ds(pl.multiple_of(which * half, half), half)
    rows_in = jnp.concatenate([piece[...] for piece in att], axis=1)
    depth = rows_in.shape[1]
    clip = clip_ref[rows, :][:, :1]
    tiles = [slice(start, start + 512) for start in range(0, D, 512)]
    for columns in tiles:
        projected = jnp.dot(rows_in, w_out[D - depth :, columns], preferred_element_type=F32)
        if turn == 1:
            projected = projected + partial[:, columns]
        mixed[:, columns] = (
            res[rows, columns].astype(F32) + chosen(mod, 0, clip, columns) * projected
        )
    held = mixed[...]
    centre = held - jnp.mean(held, axis=1, keepdims=True)
    spread = lax.rsqrt(jnp.mean(centre * centre, axis=1, keepdims=True) + 1e-06)
    for columns in tiles:
        stretch, shift = chosen(mod, 2, clip, columns), chosen(mod, 1, clip, columns)
        normed[:, columns] = (centre[:, columns] * spread * (1.0 + stretch) + shift).astype(BF16)
    for columns in tiles:
        raised = jnp.dot(normed[...], up[:, columns], preferred_element_type=F32)
        hidden[:, columns] = jax.nn.gelu(raised, approximate=True).astype(BF16)
    if turn == 0:
        for columns, terms in lowered_tiles(hidden, mixed, down, mod, clip):
            out[:, columns] = terms.astype(BF16)


def feed(turn, att, w_out, w_up, w_down, residual, mod, clip_wide):
    half = att[0].shape[0]
    inner = [pltpu.VMEM((half, D), BF16)]
    more = []
    if turn == 0:
        out_shape = shape_of((half, D))
        inner = [pltpu.VMEM((half, D), F32), pltpu.VMEM((half, D), BF16)] + inner
    else:
        out_shape = [shape_of((half, D)), shape_of((half, D), F32)]
        more = [project(att[:3], w_out)]
        att = att[3:]
    return pl.pallas_call(
        functools.partial(feed_kernel, turn, len(att)),
        out_shape=out_shape,
        in_specs=[VMEM] * (len(att) + 6 + len(more)),
        out_specs=VMEM if turn == 0 else [VMEM] * 2,
        scratch_shapes=inner,
        compiler_params=params(24),
        cost_estimate=cost(2**36, 2**24),
        name="feed",
    )(*att, kept(w_out), kept(w_up), kept(w_down), kept(residual), mod, clip_wide, *more)


def guide_kernel(hidden, mixed, down, other_ref, clip_ref, mod, scale_ref, *refs):
    outs, held = refs[:4], refs[4]
    side, blk = lax.axis_index("cfg"), lax.axis_index("blk")
    half, width = outs[0].shape
    clip = clip_ref[pl.ds(pl.multiple_of(side * half, half), half), :][:, :1]
    strength = jnp.zeros((half, 1), F32)
    for index in range(CLIPS):
        strength = jnp.where(clip == index, scale_ref[index : index + 1, :1], strength)
    lean = jnp.where(side == 0, strength, 1.0 - strength)
    for columns, mine in lowered_tiles(hidden, mixed, down, mod, clip):
        other = other_ref[:, columns].astype(F32)
        held[:, columns] = other + lean * (mine - other)
    for step, out in enumerate(outs):
        target = jnp.bitwise_xor(blk, step)
        columns = pl.ds(pl.multiple_of(target * width, width), width)
        out[...] = held[:, columns].astype(out.dtype)


def place_kernel(own, got1, got2, got3, placing, *outs):
    guided = own[...] + got1[...].astype(F32) + got2[...].astype(F32) + got3[...].astype(F32)
    placed = jnp.dot(placing[...], guided.astype(BF16), preferred_element_type=F32).astype(BF16)
    if len(outs) == 1:
        outs[0][...] = placed
    else:
        count = outs[0].shape[0]
        for index, out in enumerate(outs):
            out[...] = placed[index * count : (index + 1) * count, :]


def arrange_kernel(*refs):
    out = refs[4]
    place = lax.axis_index("seq")
    count = refs[0].shape[0]
    for step, source in zip((0, 3, 2, 1), refs):
        origin = jnp.bitwise_xor(place, step)
        out[pl.ds(pl.multiple_of(origin * count, count), count), :] = source[...]


def exchanged(value, axis, mask):
    pairs = [(index, index ^ mask) for index in range(lax.axis_size(axis))]
    return lax.ppermute(value, axis, pairs)


def shards(
    queries, keys, values, residual, w_out, w_up, w_down, modulation, guide_scale, slot_clip, owner
):
    slots, width = queries.shape[1:]
    half = slots // 2
    seq_count = lax.axis_size("seq")
    capacity = max(2, slots // seq_count)
    side, place = lax.axis_index("cfg"), lax.axis_index("seq")

    clip_wide = jnp.broadcast_to(slot_clip[:, None], (slots, 128))
    scale_wide = jnp.broadcast_to(guide_scale[:, None], (CLIPS, 128))
    clip_half = lax.dynamic_slice_in_dim(slot_clip, side * half, half, 0)
    owner_half = lax.dynamic_slice_in_dim(owner[:, 0], side * half, half, 0)
    order = jnp.arange(half, dtype=jnp.int32)
    before = (owner_half[None, :] == owner_half[:, None]) & (order[None, :] < order[:, None])
    rank = jnp.sum(before.astype(jnp.int32), axis=1)
    if seq_count == 4:
        lane = jnp.bitwise_xor(owner_half, place)
    else:
        lane = owner_half
    target = jnp.where(clip_half < CLIPS, lane * capacity + rank, -1)
    placing = (
        jnp.arange(seq_count * capacity, dtype=jnp.int32)[:, None] == target[None, :]
    ).astype(BF16)

    near, w_half = fetch_near(w_out)
    if seq_count == 4:
        (up, down, stream), attended = attention_by_head(
            queries[0],
            keys[0],
            values[0],
            slot_clip,
            (clip_wide, placing, w_half, scale_wide),
            (w_up, w_down, residual[0]),
        )
    else:
        attended = attention_by_rows(queries[0], keys[0], values[0], slot_clip)
        up, down, stream = load((w_up, w_down, residual[0]), attended[0])

    whole = fetch_rest(w_out, near, w_half, attended[0])
    parts = []
    for turn in range(2):
        piece = attended[turn]
        gathered = [piece] + [exchanged(piece, "blk", mask) for mask in (1, 2, 3)]
        parts.append(feed(turn, gathered, whole, up, down, stream, modulation, clip_wide))
    other = exchanged(parts[0], "cfg", 1)
    own, *sent = pl.pallas_call(
        guide_kernel,
        out_shape=[shape_of((half, width), F32)] + [shape_of((half, width))] * 3,
        in_specs=[VMEM] * 7,
        out_specs=[VMEM] * 4,
        scratch_shapes=[pltpu.VMEM((half, D), F32)],
        compiler_params=params(16),
        name="guide",
    )(*parts[1], kept(down), other, clip_wide, modulation, scale_wide)
    got = [exchanged(piece, "blk", mask) for mask, piece in zip((1, 2, 3), sent)]
    by_step = seq_count == 4
    placed = pl.pallas_call(
        place_kernel,
        out_shape=[shape_of((capacity, width))] * 4
        if by_step
        else [shape_of((seq_count * capacity, width))],
        in_specs=[VMEM] * 5,
        out_specs=[VMEM] * (4 if by_step else 1),
        compiler_params=params(16),
        name="place",
    )(own, *got, placing)
    if not by_step:
        arrived = lax.all_to_all(
            placed[0].reshape(seq_count, capacity, width), "seq", split_axis=0, concat_axis=0,
            tiled=True,
        )
        return arrived.reshape(1, seq_count * capacity, width)
    home = [
        exchanged(placed[step], "seq", step) for step in (3, 2, 1)
    ]
    arranged = pl.pallas_call(
        arrange_kernel,
        out_shape=shape_of((4 * capacity, width)),
        in_specs=[VMEM] * 4,
        out_specs=VMEM,
        compiler_params=params(16),
        name="arrange",
    )(placed[0], *home)
    return arranged[None]


def solution(mesh):
    placed = (
        P("cfg", "seq", "blk"),
        P("cfg", "seq", "blk"),
        P("cfg", "seq", "blk"),
        P("cfg", "seq", None),
        P("blk", None),
        P(None, "blk"),
        P("blk", None),
        P(),
        P(),
        P("seq"),
        P("seq", None),
    )
    return jax.shard_map(
        shards, mesh=mesh, in_specs=placed, out_specs=P("cfg", "seq", "blk"), check_vma=False
    )
```

```python
import functools
import math

import jax
import jax.numpy as jnp
from jax import lax
from jax.experimental import pallas as pl
from jax.experimental.pallas import tpu as pltpu
from jax.sharding import PartitionSpec as P

D = 1536
HEAD_DIM = 128
CLIPS = 3
NEG_FILL = -1e30
FAR = 2.0**100
VMEM = pl.BlockSpec(memory_space=pltpu.VMEM)
ANY = pl.BlockSpec(memory_space=pl.ANY)
F32 = jnp.float32
BF16 = jnp.bfloat16


def shape_of(extent, dtype=BF16):
    return jax.ShapeDtypeStruct(extent, dtype)


def params(mib):
    return pltpu.CompilerParams(vmem_limit_bytes=mib * 2**20)


def cost(flops, moved):
    return pl.CostEstimate(flops=flops, bytes_accessed=moved, transcendentals=0)


STEPS = (0, 2, 3, 1)


def head_at(side, place):
    return jnp.where(side == 0, place, 3 - place)


def works(side, place):
    return place < 3 if side == 0 else place >= 1


def hop(value, step, back=False):
    pairs = []
    for side in range(2):
        for place in range(4):
            target = place ^ step
            if works(side, target):
                pair = (side * 4 + place, side * 4 + target)
                pairs.append(pair[::-1] if back else pair)
    return lax.ppermute(value, ("cfg", "seq"), pairs)


def pack_kernel(q_ref, k_ref, v_ref, clip_ref, *refs):
    outs, clips, held, sems = refs[:4], refs[4], refs[5], refs[6]
    side, place = lax.axis_index("cfg"), lax.axis_index("seq")
    slots = q_ref.shape[0]
    copies = [pltpu.make_async_copy(clip_ref, clips, sems.at[3])]
    for part, source in enumerate((q_ref, k_ref, v_ref)):
        copies.append(pltpu.make_async_copy(source, held.at[part], sems.at[part]))
    for copy in copies:
        copy.start()
    copies[0].wait()
    numbers = clips[...].astype(F32)
    rest = jnp.zeros((16 - numbers.shape[0], 128), F32)
    rows = jnp.concatenate([numbers, rest], axis=0).astype(BF16)
    for out in outs:
        out[3 * slots :, :] = rows
    for part in range(3):
        copies[1 + part].wait()
        for step, out in zip(STEPS, outs):
            head = jnp.clip(head_at(side, jnp.bitwise_xor(place, step)), 0, 2)
            columns = pl.ds(pl.multiple_of(head * HEAD_DIM, HEAD_DIM), HEAD_DIM)
            out[part * slots : (part + 1) * slots, :] = held[part, :, columns]


def attend_kernel(*refs):
    blocks, outs, (q_aug, k_aug, v_aug, wide, found) = refs[:4], refs[-9:-5], refs[-5:]
    slots = outs[0].shape[0]
    count = slots // CLIPS
    group = 4 * count
    lane = lax.broadcasted_iota(jnp.int32, (count, 128), 1)
    row = lax.broadcasted_iota(jnp.int32, (count, 128), 0)
    q_tail = jnp.where(lane == 0, -FAR, 0.0).astype(BF16)
    v_tail = (lane == 0).astype(BF16)
    fills, bases = [], []
    for index, block in enumerate(blocks):
        numbers = block[3 * slots :, :].astype(F32)
        line = lax.broadcasted_iota(jnp.int32, numbers.shape, 0)
        spot = lax.broadcasted_iota(jnp.int32, numbers.shape, 1)
        live = (line < slots // 128) & (numbers < CLIPS - 0.5)
        filled = jnp.sum(live.astype(F32)).astype(jnp.int32)
        first = jnp.sum(jnp.where((line == 0) & (spot == 0), numbers, 0.0)).astype(jnp.int32)
        fills.append(filled)
        wide[index, : 3 * slots, :] = block[: 3 * slots, :].astype(F32)
        for turn in range(CLIPS):
            clip = lax.rem(first + turn, CLIPS)
            base = pl.multiple_of((clip * 4 + index) * count, count)
            bases.append(base)
            here = pl.ds(base, count)
            for part, target in enumerate((q_aug, k_aug, v_aug)):
                rows = pl.ds(part * slots + turn, count, stride=CLIPS)
                target[here, :128] = wide[index, rows, :].astype(BF16)
            padding = (lane == 0) & (CLIPS * row + turn >= filled)
            q_aug[here, 128:] = q_tail
            k_aug[here, 128:] = padding.astype(BF16)
            v_aug[here, 128:] = v_tail
    scale = math.log2(math.e) / math.sqrt(HEAD_DIM)

    def score(clip):
        here = slice(clip * group, (clip + 1) * group)
        return lax.dot_general(
            q_aug[here, :], k_aug[here, :], (((1,), (1,)), ((), ())), preferred_element_type=F32
        )

    ahead = score(0)
    for clip in range(CLIPS):
        scores = ahead
        if clip + 1 < CLIPS:
            ahead = score(clip + 1)
        here = slice(clip * group, (clip + 1) * group)
        peak = jnp.max(scores, axis=1, keepdims=True)
        probs = jnp.exp2((scores - peak) * scale).astype(BF16)
        summed = jnp.dot(probs, v_aug[here, :], preferred_element_type=F32)
        found[here, :] = summed[:, :128] / summed[:, 128:129]
    line = lax.broadcasted_iota(jnp.int32, (slots, 128), 0)
    for index, out in enumerate(outs):
        for turn in range(CLIPS):
            base = bases[index * CLIPS + turn]
            wide[index, pl.ds(turn, count, stride=CLIPS), :] = found[pl.ds(base, count), :]
        out[...] = jnp.where(line < fills[index], wide[index, :slots, :], 0.0).astype(BF16)


def regroup_kernel(own, back1, back2, back3, first, second):
    side, place = lax.axis_index("cfg"), lax.axis_index("seq")
    half = first.shape[0]
    for head in range(3):
        home = jnp.where(side == 0, head, 3 - head)
        step = jnp.bitwise_xor(home, place)
        columns = slice(head * HEAD_DIM, (head + 1) * HEAD_DIM)
        for index, source in zip(STEPS, (own, back1, back2, back3)):

            @pl.when(step == index)
            def _():
                for out, which in ((first, 1 - side), (second, side)):
                    rows = pl.ds(pl.multiple_of(which * half, half), half)
                    out[:, columns] = source[rows, :]


def kept(value):
    return pltpu.with_memory_space_constraint(value, pltpu.VMEM)


def afar(value):
    return pltpu.with_memory_space_constraint(value, pltpu.HBM)


def load_kernel(*refs):
    outs, sems = refs[4:7], refs[7]
    copies = [
        pltpu.make_async_copy(refs[index], out, sems.at[index]) for index, out in enumerate(outs)
    ]
    for copy in copies:
        copy.start()
    for copy in copies:
        copy.wait()


def load(arrays, after):
    return pl.pallas_call(
        load_kernel,
        out_shape=[pltpu.VMEM(array.shape, BF16) for array in arrays],
        in_specs=[ANY] * 4,
        out_specs=[VMEM] * 3,
        scratch_shapes=[pltpu.SemaphoreType.DMA((3,))],
        compiler_params=params(16),
        cost_estimate=cost(2**34, 2**24),
        name="load",
    )(*(afar(array) for array in arrays), after)


def across(value, masks):
    pairs = [
        (side * 4 + blk, side * 4 + (blk ^ masks[side])) for side in range(2) for blk in range(4)
    ]
    return lax.ppermute(value, ("cfg", "blk"), pairs)


def cut_kernel(got, out, sem):
    part = out.shape[0]
    offset = pl.multiple_of((1 - lax.axis_index("cfg")) * part, part)
    copy = pltpu.make_async_copy(got.at[pl.ds(offset, part), :], out, sem)
    copy.start()
    copy.wait()


def join_kernel(own, near, near_swap, far, far_swap, after, out, sems):
    side = lax.axis_index("cfg")
    width, part = own.shape[0], far.shape[0]
    plan = (
        (own, 0, width),
        (near, (1 + side) * width, width),
        (near_swap, (2 - side) * width, width),
        (far, 3 * width + (1 - side) * part, part),
        (far_swap, 3 * width + side * part, part),
    )
    copies = []
    for index, (source, offset, rows) in enumerate(plan):
        target = out.at[pl.ds(pl.multiple_of(offset, part), rows), :]
        copy = pltpu.make_async_copy(source, target, sems.at[index])
        copy.start()
        copies.append(copy)
    for copy in copies:
        copy.wait()


def gate_kernel(value, after, out):
    pass


def gate(value, after):
    return pl.pallas_call(
        gate_kernel,
        out_shape=shape_of(value.shape, value.dtype),
        in_specs=[ANY] * 2,
        out_specs=ANY,
        input_output_aliases={0: 0},
        compiler_params=params(1),
        name="gate",
    )(value, after)


def fetch_near(w_out):
    near = across(w_out, (1, 2))
    half = pl.pallas_call(
        cut_kernel,
        out_shape=shape_of((w_out.shape[0] // 2, D)),
        in_specs=[ANY],
        out_specs=ANY,
        scratch_shapes=[pltpu.SemaphoreType.DMA],
        compiler_params=params(16),
        name="cut",
    )(near)
    return near, half


def fetch_rest(w_out, near, half, after):
    far = across(half, (2, 1))
    far = gate(far, after)
    pieces = (afar(w_out), near, exchanged(near, "cfg", 1), far, exchanged(far, "cfg", 1))
    return pl.pallas_call(
        join_kernel,
        out_shape=pltpu.VMEM((D, D), BF16),
        in_specs=[ANY] * 6,
        out_specs=VMEM,
        scratch_shapes=[pltpu.SemaphoreType.DMA((5,))],
        compiler_params=params(16),
        name="join",
    )(*pieces, after)


def attention_by_head(query, key, value, slot_clip, early, weights):
    slots = query.shape[0]
    packed = pl.pallas_call(
        pack_kernel,
        out_shape=[shape_of((3 * slots + 16, 128))] * 4,
        in_specs=[ANY] * 4,
        out_specs=[VMEM] * 4,
        scratch_shapes=[
            pltpu.VMEM((slots // 128, 128), jnp.int32),
            pltpu.VMEM((3, slots, 3 * HEAD_DIM), BF16),
            pltpu.SemaphoreType.DMA((4,)),
        ],
        compiler_params=params(16),
        name="pack",
    )(afar(query), afar(key), afar(value), afar(slot_clip.reshape(slots // 128, 128)))
    blocks = [packed[0]] + [hop(packed[index], STEPS[index]) for index in (1, 2, 3)]
    early = (*early, *(kept(weight) for weight in load(weights, packed[0])))
    results = pl.pallas_call(
        attend_kernel,
        out_shape=[shape_of((slots, 128))] * 4,
        in_specs=[VMEM] * 4 + [ANY] * (len(early) - 3) + [VMEM] * 3,
        out_specs=[VMEM] * 4,
        scratch_shapes=[pltpu.VMEM((4 * slots, 256), BF16)] * 3
        + [pltpu.VMEM((4, 3 * slots + 8, 128), F32), pltpu.VMEM((4 * slots, 128), F32)],
        compiler_params=params(28),
        cost_estimate=cost(2**32, 2**21),
        name="attend",
    )(*blocks, *early)
    backs = [hop(results[index], STEPS[index], back=True) for index in (1, 2, 3)]
    half = slots // 2
    return early[-3:], pl.pallas_call(
        regroup_kernel,
        out_shape=[shape_of((half, 3 * HEAD_DIM))] * 2,
        in_specs=[VMEM] * 4,
        out_specs=[VMEM] * 2,
        compiler_params=params(16),
        name="regroup",
    )(results[0], *backs)


def attention_by_rows(query, key, value, slot_clip):
    slots, width = query.shape
    heads = width // HEAD_DIM
    live = slot_clip < CLIPS
    factor = 1.0 / math.sqrt(HEAD_DIM)
    query_heads = query.reshape(slots, heads, HEAD_DIM)

    def absorb(carry, piece):
        key_piece, value_piece, clip_piece = piece
        best, total, accum = carry
        kept = (clip_piece[None, :] == slot_clip[:, None]) & live[:, None]
        scores = jnp.einsum("qhd,khd->hqk", query_heads, key_piece, preferred_element_type=F32)
        scores = jnp.where(kept[None], scores * factor, NEG_FILL)
        new_best = jnp.maximum(best, jnp.max(scores, axis=-1))
        fade = jnp.exp(best - new_best)
        probs = jnp.exp(scores - new_best[..., None])
        total = total * fade + jnp.sum(probs, axis=-1)
        added = jnp.einsum(
            "hqk,khd->qhd", probs.astype(BF16), value_piece, preferred_element_type=F32
        )
        accum = accum * jnp.transpose(fade)[:, :, None] + added
        return (new_best, total, accum), None

    start = (
        jnp.full((heads, slots), NEG_FILL, F32),
        jnp.zeros((heads, slots), F32),
        jnp.zeros((slots, heads, HEAD_DIM), F32),
    )
    pieces = (
        lax.all_gather(key, "seq").reshape(-1, slots, heads, HEAD_DIM),
        lax.all_gather(value, "seq").reshape(-1, slots, heads, HEAD_DIM),
        lax.all_gather(slot_clip, "seq"),
    )
    (best, total, accum), _ = lax.scan(absorb, start, pieces)
    attended = (accum / jnp.transpose(total)[:, :, None]).reshape(slots, width)
    attended = jnp.where(live[:, None], attended, 0.0).astype(BF16)
    half = slots // 2
    side = lax.axis_index("cfg")
    return [
        lax.dynamic_slice_in_dim(attended, which * half, half, 0) for which in (1 - side, side)
    ]


def chosen(mod, kind, clip, columns):
    picked = jnp.zeros((clip.shape[0], columns.stop - columns.start), F32)
    for index in range(CLIPS):
        picked = jnp.where(clip == index, mod[index, kind : kind + 1, columns], picked)
    return picked


def lowered_tiles(hidden, mixed, down, mod, clip):
    blk = lax.axis_index("blk")
    width = D // lax.axis_size("blk")
    for start in range(0, D, 2 * width):
        columns = slice(start, start + 2 * width)
        lowered = jnp.dot(hidden[...], down[:, columns], preferred_element_type=F32)
        lowered = chosen(mod, 3, clip, columns) * lowered
        for index in range(2):
            part = slice(start + index * width, start + (index + 1) * width)
            stream = jnp.where(blk == part.start // width, mixed[:, part], 0.0)
            yield part, lowered[:, index * width : (index + 1) * width] + stream


def project_kernel(*refs):
    att, w_out, out = (refs[0], refs[2], refs[1]), refs[3], refs[4]
    rows_in = jnp.concatenate([piece[...] for piece in att], axis=1)
    depth = rows_in.shape[1]
    for start in range(0, D, 512):
        columns = slice(start, start + 512)
        out[:, columns] = jnp.dot(
            rows_in, w_out[:depth, columns], preferred_element_type=F32
        )


def project(att, w_out):
    return pl.pallas_call(
        project_kernel,
        out_shape=shape_of((att[0].shape[0], D), F32),
        in_specs=[VMEM] * 4,
        out_specs=VMEM,
        compiler_params=params(16),
        cost_estimate=cost(2**32, 2**22),
        name="project",
    )(att[0], att[2], att[1], kept(w_out))


def feed_kernel(turn, count, *refs):
    att, (w_out, up, down, res, mod, clip_ref), refs = (
        refs[:count],
        refs[count : count + 6],
        refs[count + 6 :],
    )
    if turn == 0:
        out, mixed, hidden, normed = refs
    else:
        partial, hidden, mixed, normed = refs
    side = lax.axis_index("cfg")
    half = hidden.shape[0]
    which = 1 - side if turn == 0 else side
    rows = pl.ds(pl.multiple_of(which * half, half), half)
    rows_in = jnp.concatenate([piece[...] for piece in att], axis=1)
    depth = rows_in.shape[1]
    clip = clip_ref[rows, :][:, :1]
    tiles = [slice(start, start + 512) for start in range(0, D, 512)]
    for columns in tiles:
        projected = jnp.dot(rows_in, w_out[D - depth :, columns], preferred_element_type=F32)
        if turn == 1:
            projected = projected + partial[:, columns]
        mixed[:, columns] = (
            res[rows, columns].astype(F32) + chosen(mod, 0, clip, columns) * projected
        )
    held = mixed[...]
    centre = held - jnp.mean(held, axis=1, keepdims=True)
    spread = lax.rsqrt(jnp.mean(centre * centre, axis=1, keepdims=True) + 1e-06)
    for columns in tiles:
        stretch, shift = chosen(mod, 2, clip, columns), chosen(mod, 1, clip, columns)
        normed[:, columns] = (centre[:, columns] * spread * (1.0 + stretch) + shift).astype(BF16)
    for columns in tiles:
        raised = jnp.dot(normed[...], up[:, columns], preferred_element_type=F32)
        hidden[:, columns] = jax.nn.gelu(raised, approximate=True).astype(BF16)
    if turn == 0:
        for columns, terms in lowered_tiles(hidden, mixed, down, mod, clip):
            out[:, columns] = terms.astype(BF16)


def feed(turn, att, w_out, w_up, w_down, residual, mod, clip_wide):
    half = att[0].shape[0]
    inner = [pltpu.VMEM((half, D), BF16)]
    more = []
    if turn == 0:
        out_shape = shape_of((half, D))
        inner = [pltpu.VMEM((half, D), F32), pltpu.VMEM((half, D), BF16)] + inner
    else:
        out_shape = [shape_of((half, D)), shape_of((half, D), F32)]
        more = [project(att[:3], w_out)]
        att = att[3:]
    return pl.pallas_call(
        functools.partial(feed_kernel, turn, len(att)),
        out_shape=out_shape,
        in_specs=[VMEM] * (len(att) + 6 + len(more)),
        out_specs=VMEM if turn == 0 else [VMEM] * 2,
        scratch_shapes=inner,
        compiler_params=params(24),
        cost_estimate=cost(2**36, 2**24),
        name="feed",
    )(*att, kept(w_out), kept(w_up), kept(w_down), kept(residual), mod, clip_wide, *more)


def guide_kernel(hidden, mixed, down, other_ref, clip_ref, mod, scale_ref, *refs):
    outs, held = refs[:4], refs[4]
    side, blk = lax.axis_index("cfg"), lax.axis_index("blk")
    half, width = outs[0].shape
    clip = clip_ref[pl.ds(pl.multiple_of(side * half, half), half), :][:, :1]
    strength = jnp.zeros((half, 1), F32)
    for index in range(CLIPS):
        strength = jnp.where(clip == index, scale_ref[index : index + 1, :1], strength)
    lean = jnp.where(side == 0, strength, 1.0 - strength)
    for columns, mine in lowered_tiles(hidden, mixed, down, mod, clip):
        other = other_ref[:, columns].astype(F32)
        held[:, columns] = other + lean * (mine - other)
    for step, out in enumerate(outs):
        target = jnp.bitwise_xor(blk, step)
        columns = pl.ds(pl.multiple_of(target * width, width), width)
        out[...] = held[:, columns].astype(out.dtype)


def place_kernel(own, got1, got2, got3, placing, *outs):
    guided = own[...] + got1[...].astype(F32) + got2[...].astype(F32) + got3[...].astype(F32)
    placed = jnp.dot(placing[...], guided.astype(BF16), preferred_element_type=F32).astype(BF16)
    if len(outs) == 1:
        outs[0][...] = placed
    else:
        count = outs[0].shape[0]
        for index, out in enumerate(outs):
            out[...] = placed[index * count : (index + 1) * count, :]


def arrange_kernel(*refs):
    out = refs[4]
    place = lax.axis_index("seq")
    count = refs[0].shape[0]
    for step, source in zip((0, 3, 2, 1), refs):
        origin = jnp.bitwise_xor(place, step)
        out[pl.ds(pl.multiple_of(origin * count, count), count), :] = source[...]


def exchanged(value, axis, mask):
    pairs = [(index, index ^ mask) for index in range(lax.axis_size(axis))]
    return lax.ppermute(value, axis, pairs)


def shards(
    queries, keys, values, residual, w_out, w_up, w_down, modulation, guide_scale, slot_clip, owner
):
    slots, width = queries.shape[1:]
    half = slots // 2
    seq_count = lax.axis_size("seq")
    capacity = max(2, slots // seq_count)
    side, place = lax.axis_index("cfg"), lax.axis_index("seq")

    clip_wide = jnp.broadcast_to(slot_clip[:, None], (slots, 128))
    scale_wide = jnp.broadcast_to(guide_scale[:, None], (CLIPS, 128))
    clip_half = lax.dynamic_slice_in_dim(slot_clip, side * half, half, 0)
    owner_half = lax.dynamic_slice_in_dim(owner[:, 0], side * half, half, 0)
    order = jnp.arange(half, dtype=jnp.int32)
    before = (owner_half[None, :] == owner_half[:, None]) & (order[None, :] < order[:, None])
    rank = jnp.sum(before.astype(jnp.int32), axis=1)
    if seq_count == 4:
        lane = jnp.bitwise_xor(owner_half, place)
    else:
        lane = owner_half
    target = jnp.where(clip_half < CLIPS, lane * capacity + rank, -1)
    placing = (
        jnp.arange(seq_count * capacity, dtype=jnp.int32)[:, None] == target[None, :]
    ).astype(BF16)

    near, w_half = fetch_near(w_out)
    if seq_count == 4:
        (up, down, stream), attended = attention_by_head(
            queries[0],
            keys[0],
            values[0],
            slot_clip,
            (clip_wide, placing, w_half, scale_wide),
            (w_up, w_down, residual[0]),
        )
    else:
        attended = attention_by_rows(queries[0], keys[0], values[0], slot_clip)
        up, down, stream = load((w_up, w_down, residual[0]), attended[0])

    whole = fetch_rest(w_out, near, w_half, attended[0])
    parts = []
    for turn in range(2):
        piece = attended[turn]
        gathered = [piece] + [exchanged(piece, "blk", mask) for mask in (1, 2, 3)]
        parts.append(feed(turn, gathered, whole, up, down, stream, modulation, clip_wide))
    other = exchanged(parts[0], "cfg", 1)
    own, *sent = pl.pallas_call(
        guide_kernel,
        out_shape=[shape_of((half, width), F32)] + [shape_of((half, width))] * 3,
        in_specs=[VMEM] * 7,
        out_specs=[VMEM] * 4,
        scratch_shapes=[pltpu.VMEM((half, D), F32)],
        compiler_params=params(16),
        name="guide",
    )(*parts[1], kept(down), other, clip_wide, modulation, scale_wide)
    got = [exchanged(piece, "blk", mask) for mask, piece in zip((1, 2, 3), sent)]
    by_step = seq_count == 4
    placed = pl.pallas_call(
        place_kernel,
        out_shape=[shape_of((capacity, width))] * 4
        if by_step
        else [shape_of((seq_count * capacity, width))],
        in_specs=[VMEM] * 5,
        out_specs=[VMEM] * (4 if by_step else 1),
        compiler_params=params(16),
        name="place",
    )(own, *got, placing)
    if not by_step:
        arrived = lax.all_to_all(
            placed[0].reshape(seq_count, capacity, width), "seq", split_axis=0, concat_axis=0,
            tiled=True,
        )
        return arrived.reshape(1, seq_count * capacity, width)
    home = [
        exchanged(placed[step], "seq", step) for step in (3, 2, 1)
    ]
    arranged = pl.pallas_call(
        arrange_kernel,
        out_shape=shape_of((4 * capacity, width)),
        in_specs=[VMEM] * 4,
        out_specs=VMEM,
        compiler_params=params(16),
        name="arrange",
    )(placed[0], *home)
    return arranged[None]


def solution(mesh):
    placed = (
        P("cfg", "seq", "blk"),
        P("cfg", "seq", "blk"),
        P("cfg", "seq", "blk"),
        P("cfg", "seq", None),
        P("blk", None),
        P(None, "blk"),
        P("blk", None),
        P(),
        P(),
        P("seq"),
        P("seq", None),
    )
    return jax.shard_map(
        shards, mesh=mesh, in_specs=placed, out_specs=P("cfg", "seq", "blk"), check_vma=False
    )
```
